32 devices in a mesh: chain: 8 (over y, x, core), space: 4 (over z).
Axes of the slice: x: 2, y: 2, z: 4, core: 2. Of those that a mesh axis runs over, the one named last changes fastest.
Arguments:
- positions: float32 [3, 262144], P(None, ('chain', 'space')), may hold values from -6 to 6
- noise: float32 [2, 3, 262144], P(None, None, ('chain', 'space')), may hold values from -6 to 6
- cell_owner: int32 [262144, 1], P(('chain', 'space')), may hold values from 0 to 31; in each aligned block of 8192 rows (0 to 8191, 8192 to 16383, ...) at most 512 rows name the same one
- tile_rows: int32 [16384], P(('chain', 'space')), may hold values from 0 to 127
- tile_cols: int32 [16384], P(('chain', 'space')), may hold values from 0 to 383
- loop_left: int32 [512], P(('chain', 'space')), may hold values from 0 to 258047, as said below
- loop_span: int32 [512], P(('chain', 'space')), may hold values from 1 to 4096
Outputs:
- final_positions: float32 [3, 262144], P(None, ('chain', 'space'))
The draws below stay inside these ranges and needn't reach their ends.
Inputs may be any that keep to these rules, and one draw needn't show every extreme that they name: `cell_owner`: among the monomers of one device at most 512 name the same owner, a bound that some block reaches of them. Extruders e * 16 to e * 16 + 15 have their left anchor among the monomers of device e, and loop_left + loop_span < 262144.
All inputs are finite; a program needn't handle non-finite values.
Results may differ from the reference program's by a relative error of at most 0.0003.
Values sent between devices are 32-bit elements; how exact they have to be, the bound alone decides.
No kernel may reach another device: no remote copies, remote signals or barrier semaphores. Data moves between devices by JAX's collectives and lax.ppermute only.
A program may use at most 128 MiB of HBM per device.

```python
import math
import jax
import jax.numpy as jnp
import numpy as np
from jax import lax

MDEV = 8192
EXT_DEV = 16
TILES = 512
STEPS = 2
NMON = 262144
EXTRUDERS = 512
SPAN = 4096
CAP = 512
SLOTS = 16384
NB = 128
N_SPACE = 4
DEVICES = 32


def anchor_pair(key):
    base_key = jax.random.fold_in(key, 17)
    key_left, key_span = jax.random.split(base_key)
    device_of = jnp.arange(EXTRUDERS, dtype=jnp.int32) // EXT_DEV
    last_block = device_of == NMON // MDEV - 1
    span_drawn = jax.random.randint(key_span, (EXTRUDERS,), 1, SPAN + 1, dtype=jnp.int32)
    span_drawn = jnp.where(jnp.arange(EXTRUDERS, dtype=jnp.int32) % EXT_DEV == 0, SPAN, span_drawn).astype(jnp.int32)
    upper_bound = jnp.where(last_block, MDEV - SPAN, MDEV).astype(jnp.int32)
    offset = jax.random.randint(key_left, (EXTRUDERS,), 0, upper_bound, dtype=jnp.int32)
    return ((device_of * MDEV + offset).astype(jnp.int32), span_drawn)


def draw_loop_left(key, part):
    return anchor_pair(key)[0]


def draw_loop_span(key, part):
    return anchor_pair(key)[1]


def touch_ends(drawn, own_key, least, high):
    dims = drawn.shape
    index_at = [jax.random.randint(jax.random.fold_in(own_key, axis), (), 0, dims[axis]) for axis in range(len(dims))]
    drawn = drawn.at[tuple(index_at)].set(least)
    longest = dims.index(max(dims))
    index_at[longest] = (index_at[longest] + 1) % dims[longest]
    return drawn.at[tuple(index_at)].set(high)


def shard_levels(stream_key, dims, pieces, least, largest):
    def one(position, parts):
        draws = jax.random.uniform(jax.random.fold_in(jax.random.fold_in(stream_key, 6), position), (parts,), jnp.float32, least / len(pieces), largest / len(pieces))
        return jnp.repeat(jnp.exp(draws), dims[position] // parts).reshape((-1,) + (1,) * (len(dims) - position - 1))

    factor_of = one(*pieces[0])
    for cut in pieces[1:]:
        factor_of = factor_of * one(*cut)
    return factor_of


def assign_block(key, own, number, rows, count, top, limit, slope):
    order = jax.random.permutation(key, count)
    packed, ordinary = load_shares(count, rows * top, limit, slope, True), load_shares(count, rows * top, limit, slope, False)
    places = jnp.arange(count)

    def named(lengths, rotation):
        used = int((lengths > 0).sum())
        fixed = max(1, used // 4)
        shifted = fixed + (places - fixed + rotation * (used - fixed)) % max(1, count - fixed)
        return jnp.zeros((count,), jnp.int32).at[order[jnp.where(places < fixed, places, shifted)]].set(jnp.asarray(lengths, jnp.int32))

    lengths = jnp.where(number % 4 == 0, named(packed, number // 4), named(ordinary, number - number // 4 - 1))
    mixed = jax.random.permutation(jax.random.fold_in(own, 3), count)
    donor, sink = mixed[0:count // 2 * 2:2], mixed[1:count // 2 * 2:2]
    slack = jnp.minimum(lengths[donor] - 1, limit - lengths[sink]) // 2
    slack = jnp.where((donor == order[0]) | (sink == order[0]) | (lengths[sink] == 0), 0, jnp.maximum(slack, 0))
    shifted = jax.random.randint(jax.random.fold_in(own, 4), (count // 2,), 0, 1 << 20) % (slack + 1)
    lengths = lengths.at[donor].add(-shifted).at[sink].add(shifted)
    members = jnp.searchsorted(jnp.cumsum(lengths), jnp.arange(rows * top), side="right").astype(jnp.int32)
    listing = members.reshape(top, rows).T
    listing = listing[jax.random.permutation(jax.random.fold_in(own, 1), rows)]
    rotation = jax.random.randint(jax.random.fold_in(own, 2), (rows, 1), 0, top)
    return jnp.take_along_axis(listing, (jnp.arange(top)[None, :] + rotation) % top, axis=1)


def load_shares(count, total, reach, lean, full):
    loads = [(1 << 20) // math.isqrt(standing ** lean) + 1 for standing in range(1, count + 1)]
    largest = reach if full else min(reach, max(-(-total // count), total * loads[0] // sum(loads)))
    least = 1 if total - largest >= count - 1 else 0
    holding, spare = [largest] + [least] * (count - 1), total - largest - least * (count - 1)
    while spare > 0:
        candidates = [i for i in range(1, count) if holding[i] < largest] or [i for i in range(1, count) if holding[i] < reach]
        whole, budget = sum([loads[i] for i in candidates]), spare
        for i in candidates:
            more = min(reach - holding[i], max(1, budget * loads[i] // whole), spare)
            holding[i] = holding[i] + more
            spare = spare - more
    return np.array(holding)


def gaussian(own_key, shape, spread, most, cuts=(), kind=jnp.bfloat16):
    result = spread * jax.random.normal(own_key, shape, jnp.float32)
    if cuts:
        result = result * shard_levels(own_key, shape, cuts, -0.22, 0.18)
    return jnp.clip(result, -most, most).astype(kind)


def setup_inputs(seed: int = 0) -> dict:
    arg_keys = jax.random.split(jax.random.key(seed), 8)
    positions = gaussian(arg_keys[0], (3, NMON), 1.0, 6.0, ((1, 32),), jnp.float32)
    noise = gaussian(arg_keys[1], (STEPS, 3, NMON), 1.0, 6.0, ((2, 32),), jnp.float32)
    cell_owner_keys = jax.random.split(jax.random.fold_in(arg_keys[2], 1), NMON // MDEV)
    cell_owner_turns = jax.random.permutation(jax.random.fold_in(arg_keys[2], 3), NMON // MDEV)
    cell_owner = jax.vmap(lambda own, number: assign_block(jax.random.fold_in(arg_keys[2], 2), own, number, MDEV, DEVICES, 1, CAP, 2))(cell_owner_keys, cell_owner_turns).reshape((NMON, 1))
    tile_rows = touch_ends(jax.random.randint(arg_keys[3], (DEVICES * TILES,), 0, NB), jax.random.fold_in(arg_keys[3], 1), 0, NB - 1).astype(jnp.int32)
    tile_cols = touch_ends(jax.random.randint(arg_keys[4], (DEVICES * TILES,), 0, 3 * NB), jax.random.fold_in(arg_keys[4], 1), 0, (3 * NB) - 1).astype(jnp.int32)
    loop_left = draw_loop_left(jax.random.fold_in(arg_keys[7], 71), 0)
    loop_span = draw_loop_span(jax.random.fold_in(arg_keys[7], 71), 0)
    return dict(positions=positions, noise=noise, cell_owner=cell_owner, tile_rows=tile_rows, tile_cols=tile_cols, loop_left=loop_left, loop_span=loop_span)


time_step = 0.05
bond_stiff = 1.0
loop_stiff = 2.0
cutoff_sq = 2.25
contact_coef = 0.4 / 2.25
noise_gain = math.sqrt(0.1)

def slot_ranks(owners, devices):
    count_rows = owners.shape[0]
    ordering = jnp.argsort(owners, stable=True).astype(jnp.int32)
    sorted_owner = owners[ordering]
    group_first = jnp.searchsorted(sorted_owner, jnp.arange(devices, dtype=jnp.int32)).astype(jnp.int32)
    placed = jnp.arange(count_rows, dtype=jnp.int32) - group_first[sorted_owner]
    return jnp.zeros((count_rows,), jnp.int32).at[ordering].set(placed)

def tile_force(near_block, far_block, same_block):
    difference = near_block[:3, :, None] - far_block[:3, None, :]
    dist_sq = lax.optimization_barrier(jnp.sum(difference * difference, axis=0))
    weight = contact_coef * jnp.maximum(1.0 - dist_sq / cutoff_sq, 0.0) * near_block[3][:, None] * far_block[3][None, :]
    diagonal = jnp.arange(128)[:, None] == jnp.arange(128)[None, :]
    weight = jnp.where(jnp.logical_and(same_block, diagonal), 0.0, weight)
    return lax.optimization_barrier(jnp.sum(weight[None] * difference, axis=2))

def contact_forces(cells, extended, row_ids, col_ids):
    blocks = cells.shape[1] // 128
    own_blocks = cells.reshape(4, blocks, 128).transpose(1, 0, 2)
    wide_blocks = extended.reshape(4, 3 * blocks, 128).transpose(1, 0, 2)
    group_size = min(row_ids.shape[0], 32)
    row_groups = row_ids.reshape(-1, group_size)
    col_groups = col_ids.reshape(-1, group_size)

    def accumulate(running, entry):
        rows_now, cols_now = entry
        tile_terms = jax.vmap(tile_force)(own_blocks[rows_now], wide_blocks[cols_now], cols_now == rows_now + blocks)
        return (running.at[rows_now].add(tile_terms), None)
    start_total = jnp.zeros((blocks, 3, 128), jnp.float32)
    running, unused = lax.scan(accumulate, start_total, (row_groups, col_groups))
    return running.transpose(1, 0, 2).reshape(3, blocks * 128)

def reference(positions, noise, cell_owner, tile_rows, tile_cols, loop_left, loop_span):
    owners = cell_owner[:, 0]
    sources = jnp.arange(NMON, dtype=jnp.int32) // MDEV
    ranks = jax.vmap(lambda owner_block: slot_ranks(owner_block, DEVICES))(owners.reshape(DEVICES, MDEV)).reshape(NMON)
    slots = sources * CAP + ranks
    right_end = loop_left + loop_span

    def all_forces(current):
        live = jnp.concatenate([current, jnp.ones((1, NMON), current.dtype)], axis=0)
        cells = jnp.zeros((DEVICES, 4, SLOTS), current.dtype).at[owners, :, slots].set(live.T)
        zero_cells = jnp.zeros((4, SLOTS), current.dtype)

        def per_device(device_id):
            space_pos = device_id % N_SPACE
            below_cells = jnp.where(space_pos > 0, cells[jnp.maximum(device_id - 1, 0)], zero_cells)
            above_cells = jnp.where(space_pos < N_SPACE - 1, cells[jnp.minimum(device_id + 1, DEVICES - 1)], zero_cells)
            extended = jnp.concatenate([below_cells, cells[device_id], above_cells], axis=1)
            row_part = lax.dynamic_slice_in_dim(tile_rows, (device_id * TILES).astype(jnp.int32), TILES)
            col_part = lax.dynamic_slice_in_dim(tile_cols, (device_id * TILES).astype(jnp.int32), TILES)
            return contact_forces(cells[device_id], extended, row_part, col_part)
        contact = lax.map(per_device, jnp.arange(DEVICES, dtype=jnp.int32))
        excluded = contact[owners, :, slots].T
        step_diff = current[:, 1:] - current[:, :-1]
        bond = bond_stiff * (jnp.pad(step_diff, ((0, 0), (0, 1))) - jnp.pad(step_diff, ((0, 0), (1, 0))))
        tension = loop_stiff * (current[:, right_end] - current[:, loop_left])
        linked = jnp.zeros_like(current).at[:, loop_left].add(tension).at[:, right_end].add(-tension)
        return excluded + bond + linked
    current = positions
    for step_index in range(STEPS):
        current = current + time_step * all_forces(current) + noise_gain * noise[step_index]
    return current
```

```python
import functools
import math

import jax
import jax.numpy as jnp
from jax import lax
from jax.experimental import pallas as pl
from jax.experimental.pallas import tpu as pltpu
from jax.sharding import PartitionSpec as P

time_step = 0.05
bond_stiff = 1.0
loop_stiff = 2.0
cutoff_sq = 2.25
contact_coef = 0.4 / 2.25
noise_gain = math.sqrt(0.1)
longest_loop = 4096
lanes = 128
far_away = 1e15

vmem = pl.BlockSpec(memory_space=pltpu.VMEM)
smem = pl.BlockSpec(memory_space=pltpu.SMEM)
f32 = jnp.float32
bf16 = jnp.bfloat16


def call(body, outs, in_specs, args, scratch=(), flops=0, moved=2_000_000):
    many = isinstance(outs, list)
    return pl.pallas_call(
        body,
        out_shape=outs,
        in_specs=in_specs,
        out_specs=[vmem] * len(outs) if many else vmem,
        scratch_shapes=list(scratch),
        compiler_params=pltpu.CompilerParams(vmem_limit_bytes=32 * 1024 * 1024),
        cost_estimate=pl.CostEstimate(flops=flops, bytes_accessed=moved, transcendentals=0),
    )(*args)


def iota(shape, dim):
    return lax.broadcasted_iota(jnp.int32, shape, dim)


def pick(row, where_to):
    return jnp.take_along_axis(
        jnp.broadcast_to(row, where_to.shape), where_to, axis=1, mode="promise_in_bounds"
    )


def fill_slots(index_ref, source_ref, out_ref, per_owner):
    rows = source_ref.shape[1] // lanes
    fields = source_ref.shape[0]

    def one(group, carry):
        code = index_ref[pl.ds(pl.multiple_of(group * 8, 8), 8), :]
        row_of = (code >> 7) - 1
        lane_of = code & 127
        held = [jnp.full((8, lanes), far_away, f32) for _ in range(fields)]
        for j in range(rows):
            here = row_of == j
            for c in range(fields):
                row = source_ref[c : c + 1, j * lanes : (j + 1) * lanes]
                held[c] = jnp.where(here, pick(row, lane_of), held[c])
        owners_here = 8 // per_owner
        for i in range(owners_here):
            for c in range(fields):
                out_ref[group * owners_here + i, c * per_owner : (c + 1) * per_owner, :] = held[c][
                    i * per_owner : (i + 1) * per_owner, :
                ]
        return carry

    lax.fori_loop(0, index_ref.shape[0] // 8, one, 0)


def take_slots(slot_ref, source_ref, group, per_owner):
    slot = slot_ref[pl.ds(pl.multiple_of(group * 8, 8), 8), :]
    row_of = slot >> 7
    lane_of = slot & 127
    fields = source_ref.shape[1] // per_owner
    held = [jnp.zeros((8, lanes), f32) for _ in range(fields)]
    for s in range(source_ref.shape[0] * per_owner):
        here = row_of == s
        for c in range(fields):
            at = c * per_owner + s % per_owner
            row = source_ref[s // per_owner, at : at + 1, :]
            held[c] = jnp.where(here, pick(row, lane_of), held[c])
    return held


def index_kernel(capacity, owner_ref, x_ref, out_ref, index_ref, slot_ref, total_ref):
    rows = owner_ref.shape[0]
    devices = out_ref.shape[0]
    own = owner_ref[...]
    lane = iota((rows, lanes), 1)
    tri = jnp.where(
        iota((lanes, 2 * lanes), 1) >= lanes,
        1.0,
        jnp.where(iota((lanes, 2 * lanes), 0) < iota((lanes, 2 * lanes), 1), 1.0, 0.0),
    ).astype(bf16)

    def count(chunk, carry):
        prefix, total = carry
        masks = jnp.concatenate(
            [jnp.where(own == chunk * 8 + i, 1.0, 0.0) for i in range(8)], axis=0
        ).astype(bf16)
        both = jnp.dot(masks, tri, preferred_element_type=f32)
        for i in range(8):
            o = chunk * 8 + i
            part = both[i * rows : (i + 1) * rows]
            prefix = jnp.where(own == o, part[:, :lanes], prefix)
            total = jnp.where(lane == o, part[:, lanes:], total)
        return prefix, total

    zero = jnp.zeros((rows, lanes), f32)
    prefix, total = lax.fori_loop(0, devices // 8, count, (zero, zero))
    lower = jnp.where(iota((rows, rows), 1) < iota((rows, rows), 0), 1.0, 0.0).astype(bf16)
    above = jnp.dot(lower, total.astype(bf16), preferred_element_type=f32)
    offset = jnp.take_along_axis(above, own, axis=1, mode="promise_in_bounds")
    slot_ref[...] = own * capacity + (prefix + offset).astype(jnp.int32)

    down = iota((lanes, lanes), 0)
    lane_code = iota((lanes, lanes), 1).astype(f32)
    total_ref[...] = jnp.zeros_like(total_ref)

    def spread(j, carry):
        slot = slot_ref[pl.ds(j, 1), :]
        high = (slot >> 7) == down
        low = jnp.where((slot & 127) == down, 1.0, 0.0).astype(bf16)
        row_code = ((j + 1) * lanes).astype(f32)
        left = jnp.concatenate(
            [jnp.where(high, lane_code, 0.0), jnp.where(high, row_code, 0.0)], axis=1
        ).astype(bf16)
        right = jnp.concatenate([low, low], axis=1)
        total_ref[...] += lax.dot_general(
            left, right, (((1,), (1,)), ((), ())), preferred_element_type=f32
        )
        return carry

    lax.fori_loop(0, rows, spread, 0)
    index_ref[...] = total_ref[...].astype(jnp.int32)
    fill_slots(index_ref, x_ref, out_ref, out_ref.shape[1] // 3)


def chain_forces(ends_ref, x_ref, after_ref, before_ref, wide_ref, force_ref):
    mono_dev = x_ref.shape[1]
    blocks = mono_dev // lanes
    wide_ref[...] = jnp.zeros_like(wide_ref)
    wide_ref[0:3, 0:lanes] = before_ref[:, mono_dev - lanes :]
    wide_ref[0:3, lanes : lanes + mono_dev] = x_ref[...]
    wide_ref[0:3, lanes + mono_dev :] = after_ref[...]
    lane = iota((8, lanes), 1)
    has_before = ends_ref[0, 0].astype(f32)
    has_after = ends_ref[0, 1].astype(f32)
    for j in range(blocks):
        here = wide_ref[:, (j + 1) * lanes : (j + 2) * lanes]
        left = wide_ref[:, j * lanes : (j + 1) * lanes]
        right = wide_ref[:, (j + 2) * lanes : (j + 3) * lanes]
        down = pltpu.roll(jnp.where(lane == lanes - 1, left, here), 1, 1) - here
        up = pltpu.roll(jnp.where(lane == 0, right, here), lanes - 1, 1) - here
        if j == 0:
            down = jnp.where(lane == 0, down * has_before, down)
        if j == blocks - 1:
            up = jnp.where(lane == lanes - 1, up * has_after, up)
        force_ref[:, j * lanes : (j + 1) * lanes] = bond_stiff * down + bond_stiff * up

    def window(ref, at):
        return ref.at[:, pl.ds(pl.multiple_of((at >> 7) * lanes, lanes), lanes)]

    def value(block, at):
        return jnp.sum(jnp.where(lane[: block.shape[0]] == (at & 127), block, 0.0), axis=1, keepdims=True)

    todo = []
    for e in range(ends_ref.shape[1]):
        a, b = ends_ref[1, e], ends_ref[2, e]
        pull = loop_stiff * (value(window(wide_ref, b + lanes)[...], b) - value(window(wide_ref, a + lanes)[...], a))
        todo.append((a, pull))
        todo.append((jnp.minimum(b, mono_dev - 1), jnp.where(b < mono_dev, -pull, 0.0)))
    for e in range(ends_ref.shape[1]):
        a, b = ends_ref[3, e], ends_ref[4, e] - mono_dev
        b_in = jnp.maximum(b, 0)
        far_end = value(window(before_ref, a)[...], a)
        pull = loop_stiff * (value(window(wide_ref, b_in + lanes)[...], b_in)[0:3] - far_end)
        wanted = jnp.logical_and(b >= 0, ends_ref[0, 0] > 0)
        pull = jnp.where(wanted, -pull, 0.0)
        todo.append((b_in, jnp.concatenate([pull, jnp.zeros((5, 1), f32)], axis=0)))
    for at, pull in todo:
        spot = window(force_ref, at)
        spot[...] = spot[...] + jnp.where(lane == (at & 127), pull, 0.0)


def chain_step(step, ends_ref, x_ref, after_ref, before_ref, noise_ref, out_ref, wide_ref, force_ref):
    chain_forces(ends_ref, x_ref, after_ref, before_ref, wide_ref, force_ref)
    for c in range(3):
        out_ref[c : c + 1, :] = (
            x_ref[c : c + 1, :]
            + time_step * force_ref[c : c + 1, :]
            + noise_gain * noise_ref[c, step : step + 1, :]
        )


def first_kernel(ends_ref, x_ref, after_ref, before_ref, noise_ref, index_ref, y_ref, out_ref, wide_ref, force_ref):
    chain_step(0, ends_ref, x_ref, after_ref, before_ref, noise_ref, y_ref, wide_ref, force_ref)
    fill_slots(index_ref, y_ref, out_ref, out_ref.shape[1] // 3)


def contact_kernel(ends_ref, rows_ref, cols_ref, own_ref, below_ref, above_ref, out_ref, table, near, far, pulled, total):
    devices = own_ref.shape[0]
    per_owner = own_ref.shape[1] // 3
    blocks = devices * per_owner
    scale = 1.0 / math.sqrt(cutoff_sq)
    has_below = jnp.full((1, lanes), ends_ref[0], jnp.int32) > 0
    has_above = jnp.full((1, lanes), ends_ref[1], jnp.int32) > 0

    def build(o, carry):
        for k in range(per_owner):
            block = o * per_owner + k
            for c in range(3):
                at = c * per_owner + k
                table[block, c : c + 1, :] = jnp.where(has_below, below_ref[o, at : at + 1, :] * scale, far_away)
                table[blocks + block, c : c + 1, :] = own_ref[o, at : at + 1, :] * scale
                table[2 * blocks + block, c : c + 1, :] = jnp.where(
                    has_above, above_ref[o, at : at + 1, :] * scale, far_away
                )
        return carry

    lax.fori_loop(0, devices, build, 0)
    total[...] = jnp.zeros_like(total)
    down = iota((8, lanes), 0)

    def group(g, carry):
        same = jnp.zeros((8, lanes), jnp.int32)
        for i in range(8):
            r, q = rows_ref[g * 8 + i], cols_ref[g * 8 + i]
            near[4 * i : 4 * i + 4, :] = table[blocks + r]
            far[4 * i : 4 * i + 4, :] = table[q]
            same = jnp.where(down == i, (q == r + blocks).astype(jnp.int32), same)
        px, py, pz = [near[pl.ds(c, 8, stride=4), :] for c in range(3)]
        fx, fy, fz = [far[pl.ds(c, 8, stride=4), :] for c in range(3)]
        ax = ay = az = jnp.zeros((8, lanes), f32)
        for s in range(lanes):
            if s == 0:
                dx, dy, dz = px - fx, py - fy, pz - fz
            else:
                dx = px - pltpu.roll(fx, s, 1)
                dy = py - pltpu.roll(fy, s, 1)
                dz = pz - pltpu.roll(fz, s, 1)
            w = jnp.maximum(1.0 - (dx * dx + dy * dy + dz * dz), 0.0)
            if s == 0:
                w = jnp.where(same > 0, 0.0, w)
            ax = ax + w * dx
            ay = ay + w * dy
            az = az + w * dz
        pulled[pl.ds(0, 8, stride=4), :] = ax
        pulled[pl.ds(1, 8, stride=4), :] = ay
        pulled[pl.ds(2, 8, stride=4), :] = az
        for i in range(8):
            r = rows_ref[g * 8 + i]
            total[r] = total[r] + pulled[4 * i : 4 * i + 4, :]
        return carry

    lax.fori_loop(0, rows_ref.shape[0] // 8, group, 0)
    back = contact_coef * math.sqrt(cutoff_sq)

    def finish(o, carry):
        for k in range(per_owner):
            for c in range(3):
                at = c * per_owner + k
                out_ref[o, at : at + 1, :] = total[o * per_owner + k, c : c + 1, :] * back
        return carry

    lax.fori_loop(0, devices, finish, 0)


def gather_kernel(slot_ref, source_ref, base_ref, out_ref):
    per_owner = source_ref.shape[1] // 3

    def one(group, carry):
        held = take_slots(slot_ref, source_ref, group, per_owner)
        for i in range(8):
            at = pl.ds(pl.multiple_of((group * 8 + i) * lanes, lanes), lanes)
            for c in range(3):
                out_ref[c : c + 1, at] = base_ref[c : c + 1, at] + time_step * held[c][i : i + 1, :]
        return carry

    lax.fori_loop(0, slot_ref.shape[0] // 8, one, 0)


def shifted(value, axis, steps):
    count = lax.axis_size(axis)
    first, last = (max(0, -steps), min(count, count - steps))
    return lax.ppermute(value, axis, [(source, source + steps) for source in range(first, last)])


def local(positions, noise, cell_owner, tile_rows, tile_cols, loop_left, loop_span):
    both = ("chain", "space")
    devices = lax.axis_size(both)
    mono_dev = positions.shape[1]
    capacity = 2 * mono_dev // devices
    per_owner = capacity // lanes
    rows = mono_dev // lanes
    blocks = devices * per_owner
    extruders = loop_left.shape[0]
    device_id = lax.axis_index(both)
    space_id = lax.axis_index("space")

    left = loop_left - device_id * mono_dev
    anchors = jnp.stack([left, left + loop_span])
    anchors_before = shifted(anchors, both, 1)
    edge = jnp.zeros((1, extruders), jnp.int32)
    edge = edge.at[0, 0].set((device_id > 0).astype(jnp.int32))
    edge = edge.at[0, 1].set((device_id < devices - 1).astype(jnp.int32))
    ends = jnp.concatenate([edge, anchors, anchors_before], axis=0)
    slabs = jnp.stack([space_id > 0, space_id < lax.axis_size("space") - 1]).astype(jnp.int32)
    noise_t = noise.transpose(1, 0, 2)

    sent = jax.ShapeDtypeStruct((devices, 3 * per_owner, lanes), f32)
    chain = jax.ShapeDtypeStruct((3, mono_dev), f32)
    chain_scratch = [
        pltpu.VMEM((8, lanes + mono_dev + longest_loop), f32),
        pltpu.VMEM((8, mono_dev), f32),
    ]

    before = shifted(positions, both, 1)
    after = shifted(positions[:, :longest_loop], both, -1)
    x_out, index, slot = call(
        functools.partial(index_kernel, capacity),
        [
            sent,
            jax.ShapeDtypeStruct((blocks, lanes), jnp.int32),
            jax.ShapeDtypeStruct((rows, lanes), jnp.int32),
        ],
        [vmem, vmem],
        (cell_owner.reshape(rows, lanes), positions),
        [pltpu.VMEM((blocks, lanes), f32)],
    )

    def exchange(value):
        return lax.all_to_all(value, both, split_axis=0, concat_axis=0, tiled=True)

    def contact(cells):
        below = shifted(cells, "space", 1)
        above = shifted(cells, "space", -1)
        return call(
            contact_kernel,
            sent,
            [smem, smem, smem, vmem, vmem, vmem],
            (slabs, tile_rows, tile_cols, cells, below, above),
            [
                pltpu.VMEM((3 * blocks, 4, lanes), f32),
                pltpu.VMEM((32, lanes), f32),
                pltpu.VMEM((32, lanes), f32),
                pltpu.VMEM((32, lanes), f32),
                pltpu.VMEM((blocks, 4, lanes), f32),
            ],
            flops=16 * tile_rows.shape[0] * lanes * lanes,
        )

    x_cells = exchange(x_out)
    y_chain, y_out = call(
        first_kernel,
        [chain, sent],
        [smem] + [vmem] * 5,
        (ends, positions, after, before, noise_t, index),
        chain_scratch,
    )
    y_cells = exchange(y_out)
    contact0 = contact(x_cells)
    back0 = exchange(contact0)
    x1_cells = y_cells + time_step * contact0
    contact1 = contact(x1_cells)
    back1 = exchange(contact1)

    x1 = call(gather_kernel, chain, [vmem] * 3, (slot, back0, y_chain))
    before1 = shifted(x1, both, 1)
    after1 = shifted(x1[:, :longest_loop], both, -1)
    z = call(
        functools.partial(chain_step, 1),
        chain,
        [smem] + [vmem] * 4,
        (ends, x1, after1, before1, noise_t),
        chain_scratch,
    )
    return call(gather_kernel, chain, [vmem] * 3, (slot, back1, z))


def solution(mesh):
    in_specs = (
        P(None, ("chain", "space")),
        P(None, None, ("chain", "space")),
        P(("chain", "space"), None),
        P(("chain", "space")),
        P(("chain", "space")),
        P(("chain", "space")),
        P(("chain", "space")),
    )
    out_specs = P(None, ("chain", "space"))
    return jax.shard_map(local, mesh=mesh, in_specs=in_specs, out_specs=out_specs, check_vma=False)
```

```python
import functools
import math

import jax
import jax.numpy as jnp
from jax import lax
from jax.experimental import pallas as pl
from jax.experimental.pallas import tpu as pltpu
from jax.sharding import PartitionSpec as P

time_step = 0.05
bond_stiff = 1.0
loop_stiff = 2.0
cutoff_sq = 2.25
contact_coef = 0.4 / 2.25
noise_gain = math.sqrt(0.1)
longest_loop = 4096
lanes = 128
far_away = 1e15
pairs_at_once = 32

vmem = pl.BlockSpec(memory_space=pltpu.VMEM)
smem = pl.BlockSpec(memory_space=pltpu.SMEM)
both = ("chain", "space")
f32 = jnp.float32
bf16 = jnp.bfloat16


def call(body, outs, in_specs, args, scratch=(), flops=0, moved=2_000_000):
    many = isinstance(outs, list)
    return pl.pallas_call(
        body,
        out_shape=outs,
        in_specs=in_specs,
        out_specs=[vmem] * len(outs) if many else vmem,
        scratch_shapes=list(scratch),
        compiler_params=pltpu.CompilerParams(vmem_limit_bytes=32 * 1024 * 1024),
        cost_estimate=pl.CostEstimate(flops=flops, bytes_accessed=moved, transcendentals=0),
    )(*args)


def iota(shape, dim):
    return lax.broadcasted_iota(jnp.int32, shape, dim)


def pick(row, where_to):
    return jnp.take_along_axis(
        jnp.broadcast_to(row, where_to.shape), where_to, axis=1, mode="promise_in_bounds"
    )


def fill_slots(index_ref, source_ref, per_owner, store):
    rows = source_ref.shape[1] // lanes
    fields = source_ref.shape[0]
    owners_here = 8 // per_owner

    def one(group, carry):
        code = index_ref[pl.ds(pl.multiple_of(group * 8, 8), 8), :]
        row_of = (code >> 7) - 1
        lane_of = code & 127
        held = [jnp.full((8, lanes), far_away, f32) for _ in range(fields)]
        for j in range(rows):
            here = row_of == j
            for c in range(fields):
                row = source_ref[c : c + 1, j * lanes : (j + 1) * lanes]
                held[c] = jnp.where(here, pick(row, lane_of), held[c])
        for i in range(owners_here):
            for c in range(fields):
                store(group * owners_here + i, c, held[c][i * per_owner : (i + 1) * per_owner, :])
        return carry

    lax.fori_loop(0, index_ref.shape[0] // 8, one, 0)


def index_kernel(slabs, owner_ref, x_ref, out_ref, index_ref, slot_ref, turned_ref, total_ref):
    rows = owner_ref.shape[0]
    devices = out_ref.shape[0]
    per_owner = out_ref.shape[1] // 9
    own = owner_ref[...]
    lane = iota((rows, lanes), 1)
    tri = jnp.where(
        iota((lanes, 2 * lanes), 1) >= lanes,
        1.0,
        jnp.where(iota((lanes, 2 * lanes), 0) < iota((lanes, 2 * lanes), 1), 1.0, 0.0),
    ).astype(bf16)

    def count(chunk, carry):
        prefix, total = carry
        masks = jnp.concatenate(
            [jnp.where(own == chunk * 8 + i, 1.0, 0.0) for i in range(8)], axis=0
        ).astype(bf16)
        sums = jnp.dot(masks, tri, preferred_element_type=f32)
        for i in range(8):
            o = chunk * 8 + i
            part = sums[i * rows : (i + 1) * rows]
            prefix = jnp.where(own == o, part[:, :lanes], prefix)
            total = jnp.where(lane == o, part[:, lanes:], total)
        return prefix, total

    zero = jnp.zeros((rows, lanes), f32)
    prefix, total = lax.fori_loop(0, devices // 8, count, (zero, zero))
    lower = jnp.where(iota((rows, rows), 1) < iota((rows, rows), 0), 1.0, 0.0).astype(bf16)
    above = jnp.dot(lower, total.astype(bf16), preferred_element_type=f32)
    offset = jnp.take_along_axis(above, own, axis=1, mode="promise_in_bounds")
    slot = own * (per_owner * lanes) + (prefix + offset).astype(jnp.int32)
    slot_ref[...] = slot

    turned_ref[...] = jnp.concatenate([slot & 127] * (lanes // rows), axis=0).T
    down = iota((lanes, lanes), 0)
    across = iota((lanes, lanes), 1)
    lane_code = across.astype(f32)
    total_ref[...] = jnp.zeros_like(total_ref)
    at_once = 8

    def spread(chunk, carry):
        left, right = [], []
        low = turned_ref[...]
        low = jnp.where(chunk > 0, pltpu.roll(low, lanes - chunk * at_once, 1), low)
        for i in range(at_once):
            j = chunk * at_once + i
            high = (slot_ref[pl.ds(j, 1), :] >> 7) == down
            row_code = (j + 1).astype(f32)
            left.append(
                jnp.concatenate(
                    [jnp.where(high, lane_code, 0.0), jnp.where(high, row_code, 0.0)], axis=0
                ).astype(bf16)
            )
            right.append(jnp.where(low[:, i : i + 1] == across, 1.0, 0.0).astype(bf16))
        total_ref[...] += jnp.dot(
            jnp.concatenate(left, axis=1),
            jnp.concatenate(right, axis=0),
            preferred_element_type=f32,
        )
        return carry

    lax.fori_loop(0, rows // at_once, spread, 0)
    blocks = index_ref.shape[0]
    index_ref[...] = (total_ref[0:blocks, :] + lanes * total_ref[blocks:, :]).astype(jnp.int32)

    def store(owner, c, values):
        place = lax.rem(owner, slabs)
        width = 3 * per_owner
        at = c * per_owner
        up = lax.rem(owner + 1, devices)
        below = lax.rem(owner + devices - 1, devices)
        out_ref[owner, width + at : width + at + per_owner, :] = values
        out_ref[up, at : at + per_owner, :] = jnp.where(place < slabs - 1, values, far_away)
        out_ref[below, 2 * width + at : 2 * width + at + per_owner, :] = jnp.where(
            place > 0, values, far_away
        )

    fill_slots(index_ref, x_ref, per_owner, store)


def chain_forces(left_ref, span_ref, x_ref, after_ref, before_ref, anchors_ref, wide_ref, force_ref):
    mono_dev = x_ref.shape[1]
    blocks = mono_dev // lanes
    extruders = left_ref.shape[0]
    count = lax.axis_size("chain") * lax.axis_size("space")
    me = lax.axis_index("chain") * lax.axis_size("space") + lax.axis_index("space")
    wide_ref[...] = jnp.zeros_like(wide_ref)
    wide_ref[0:3, 0:lanes] = before_ref[0:3, mono_dev - lanes :]
    wide_ref[0:3, lanes : lanes + mono_dev] = x_ref[...]
    wide_ref[0:3, lanes + mono_dev :] = after_ref[...]
    lane = iota((8, lanes), 1)
    has_before = (me > 0).astype(f32)
    has_after = (me < count - 1).astype(f32)
    for j in range(blocks):
        here = wide_ref[:, (j + 1) * lanes : (j + 2) * lanes]
        left = wide_ref[:, j * lanes : (j + 1) * lanes]
        right = wide_ref[:, (j + 2) * lanes : (j + 3) * lanes]
        down = pltpu.roll(jnp.where(lane == lanes - 1, left, here), 1, 1) - here
        up = pltpu.roll(jnp.where(lane == 0, right, here), lanes - 1, 1) - here
        if j == 0:
            down = jnp.where(lane == 0, down * has_before, down)
        if j == blocks - 1:
            up = jnp.where(lane == lanes - 1, up * has_after, up)
        force_ref[:, j * lanes : (j + 1) * lanes] = bond_stiff * down + bond_stiff * up

    def window(ref, at):
        return ref.at[:, pl.ds(pl.multiple_of((at >> 7) * lanes, lanes), lanes)]

    def value(block, at):
        there = iota(block.shape, 1) == (at & 127)
        return jnp.sum(jnp.where(there, block, 0.0), axis=1, keepdims=True)

    todo = []
    for e in range(extruders):
        a = left_ref[e] - me * mono_dev
        b = a + span_ref[e]
        pull = loop_stiff * (
            value(window(wide_ref, b + lanes)[...], b) - value(window(wide_ref, a + lanes)[...], a)
        )
        todo.append((a, pull))
        todo.append((jnp.minimum(b, mono_dev - 1), jnp.where(b < mono_dev, -pull, 0.0)))
    for e in range(extruders):
        a = anchors_ref[0, e] - (me - 1) * mono_dev
        b = a + anchors_ref[1, e] - mono_dev
        wanted = jnp.logical_and(b >= 0, me > 0)
        a = jnp.where(wanted, a, 0)
        b = jnp.where(wanted, b, 0)
        far_end = value(window(before_ref, a)[0:3, :], a)
        pull = loop_stiff * (value(window(wide_ref, b + lanes)[...], b)[0:3] - far_end)
        pull = jnp.where(wanted, -pull, 0.0)
        todo.append((b, jnp.concatenate([pull, jnp.zeros((5, 1), f32)], axis=0)))
    for at, pull in todo:
        spot = window(force_ref, at)
        spot[...] = spot[...] + jnp.where(lane == (at & 127), pull, 0.0)


def chain_kernel(
    step, left_ref, span_ref, anchors_ref, x_ref, after_ref, before_ref, noise_ref, base_ref, out_ref, wide_ref, force_ref
):
    chain_forces(left_ref, span_ref, x_ref, after_ref, before_ref, anchors_ref, wide_ref, force_ref)
    for c in range(3):
        out_ref[c : c + 1, :] = (
            base_ref[c : c + 1, :]
            + time_step * force_ref[c : c + 1, :]
            + noise_gain * noise_ref[c, step : step + 1, :]
        )


def first_kernel(
    left_ref, span_ref, anchors_ref, x_ref, after_ref, before_ref, noise_ref, index_ref, out_ref, y_ref, wide_ref, force_ref
):
    chain_kernel(
        0, left_ref, span_ref, anchors_ref, x_ref, after_ref, before_ref, noise_ref, x_ref, y_ref, wide_ref, force_ref
    )
    per_owner = out_ref.shape[1] // 3

    def store(owner, c, values):
        out_ref[owner, c * per_owner : (c + 1) * per_owner, :] = values

    fill_slots(index_ref, y_ref, per_owner, store)


def pieces(x):
    high = x.astype(bf16).astype(f32)
    middle = (x - high).astype(bf16).astype(f32)
    return high, middle, x - high - middle


def contact_kernel(merged, rows_ref, cols_ref, *refs):
    if merged:
        cells_ref, refs = refs[0], refs[1:]
        width = cells_ref.shape[1] // 3
        sides = [(cells_ref, 0), (cells_ref, width), (cells_ref, 2 * width)]
    else:
        sides = [(refs[0], 0), (refs[1], 0), (refs[2], 0)]
        width = refs[0].shape[1]
        refs = refs[3:]
    out_ref, refs = refs[0], refs[1:]
    far_t, far_x, near_t, stage, cap, total = refs
    devices = out_ref.shape[0]
    per_owner = width // 3
    blocks = devices * per_owner
    owners = 8 // per_owner
    scale = 1.0 / math.sqrt(cutoff_sq)
    place = lax.axis_index("space")
    has_below = place > 0
    has_above = place < lax.axis_size("space") - 1
    cap[0:lanes, :] = jnp.full((lanes, lanes), 1e30, f32)
    cap[lanes:, :] = jnp.where(iota((lanes, lanes), 0) == iota((lanes, lanes), 1), 0.0, 1e30)
    stage[...] = jnp.zeros_like(stage)
    total[...] = jnp.zeros_like(total)

    def eight(ref, first, group, c):
        at = first + c * per_owner
        return jnp.concatenate(
            [ref[group * owners + i, at : at + per_owner, :] for i in range(owners)], axis=0
        )

    def build(group, carry):
        for side, valid in enumerate((has_below, None, has_above)):
            ref, first = sides[side]
            xs = [eight(ref, first, group, c) for c in range(3)]
            live = xs[0] < 0.5 * far_away
            if valid is not None:
                live = jnp.logical_and(live, jnp.full((8, lanes), valid.astype(jnp.int32)) > 0)
            xs = [jnp.where(live, x, 0.0) * scale for x in xs]
            square = xs[0] * xs[0] + xs[1] * xs[1] + xs[2] * xs[2]
            high, middle, low = [list(part) for part in zip(*[pieces(x) for x in xs])]
            one = [jnp.ones((8, lanes), f32)] * 3
            spot = stage.at[side]
            far = high + middle + high + list(pieces(jnp.where(live, -square, -1e9))) + one
            for f, v in enumerate(far):
                spot[pl.ds(f, 8, stride=16), :] = v
            at = pl.ds(pl.multiple_of((side * blocks + group * 8) * 16, lanes), lanes)
            far_t[at, :] = spot[...].astype(bf16).T
            for f in range(3):
                spot[pl.ds(6 + f, 8, stride=16), :] = low[f]
            far_x[at, :] = spot[...].astype(bf16)
            if side == 1:
                spot = stage.at[3]
                near = [2.0 * v for v in high + high + middle] + one
                near += list(pieces(jnp.where(live, 1.0 - square, -1e9)))
                for f, v in enumerate(near):
                    spot[pl.ds(f, 8, stride=16), :] = v
                near_t[pl.ds(pl.multiple_of(group * lanes, lanes), lanes), :] = spot[...].astype(bf16)
        return carry

    lax.fori_loop(0, blocks // 8, build, 0)
    zero = jnp.zeros((lanes, lanes), bf16)

    def sixteen(ref, block):
        return ref[pl.ds(pl.multiple_of(block * 16, 16), 16), :]

    pairs = min(pairs_at_once, rows_ref.shape[0] // 2)

    def tiles(step, carry):
        results = []
        for pair in range(pairs):
            first = (step * pairs + pair) * 2
            ids = [(rows_ref[first + i], cols_ref[first + i]) for i in range(2)]
            left, right = [], []
            for r, q in ids:
                near = sixteen(near_t, r)
                right.append(
                    jnp.concatenate(
                        [jnp.where((q & 7) == k, near, jnp.zeros_like(near)) for k in range(8)], axis=0
                    )
                )
                left.append(far_t[pl.ds(pl.multiple_of((q >> 3) * lanes, lanes), lanes), :])
            right = jnp.concatenate(
                [jnp.concatenate([right[0], zero], axis=1), jnp.concatenate([zero, right[1]], axis=1)],
                axis=0,
            )
            reach = jnp.dot(jnp.concatenate(left, axis=1), right, preferred_element_type=f32)
            for i, (r, q) in enumerate(ids):
                same = (q == r + blocks).astype(jnp.int32)
                most = cap[pl.ds(pl.multiple_of(same * lanes, lanes), lanes), :]
                w = jnp.maximum(jnp.minimum(reach[:, i * lanes : (i + 1) * lanes], most), 0.0).astype(bf16)
                results.append((r, jnp.dot(sixteen(far_x, q), w, preferred_element_type=f32)))
        for r, v in results:
            spot = total.at[pl.ds(pl.multiple_of(r * 16, 16), 16), :]
            spot[...] = spot[...] + v
        return carry

    lax.fori_loop(0, rows_ref.shape[0] // (2 * pairs), tiles, 0)
    back = contact_coef * math.sqrt(cutoff_sq)

    def finish(group, carry):
        sums = [total[pl.ds(group * lanes + f, 8, stride=16), :] for f in range(13)]
        for c in range(3):
            place = eight(sides[1][0], sides[1][1], group, c)
            here = jnp.where(place < 0.5 * far_away, place, 0.0) * scale
            force = (here * sums[12] - (sums[c] + sums[3 + c] + sums[6 + c])) * back
            for i in range(owners):
                out_ref[group * owners + i, c * per_owner : (c + 1) * per_owner, :] = force[
                    i * per_owner : (i + 1) * per_owner
                ]
        return carry

    lax.fori_loop(0, blocks // 8, finish, 0)


def gather_kernel(slot_ref, source_ref, *refs):
    base_ref, out_ref = refs if len(refs) == 2 else (None, refs[0])
    per_owner = source_ref.shape[1] // 3

    def one(group, carry):
        slot = slot_ref[pl.ds(pl.multiple_of(group * 8, 8), 8), :]
        row_of = slot >> 7
        lane_of = slot & 127
        held = [jnp.zeros((8, lanes), f32) for _ in range(3)]
        for s in range(source_ref.shape[0] * per_owner):
            here = row_of == s
            for c in range(3):
                at = c * per_owner + s % per_owner
                row = source_ref[s // per_owner, at : at + 1, :]
                held[c] = jnp.where(here, pick(row, lane_of), held[c])
        for i in range(8):
            at = pl.ds(pl.multiple_of((group * 8 + i) * lanes, lanes), lanes)
            for c in range(3):
                value = held[c][i : i + 1, :]
                if base_ref is not None:
                    value = base_ref[c : c + 1, at] + time_step * value
                out_ref[c : c + 1, at] = value
        return carry

    lax.fori_loop(0, slot_ref.shape[0] // 8, one, 0)


def shifted(value, axis, steps):
    count = lax.axis_size(axis)
    first, last = (max(0, -steps), min(count, count - steps))
    return lax.ppermute(value, axis, [(source, source + steps) for source in range(first, last)])


def local(positions, noise, cell_owner, tile_rows, tile_cols, loop_left, loop_span):
    devices = lax.axis_size(both)
    mono_dev = positions.shape[1]
    per_owner = 2 * mono_dev // devices // lanes
    rows = mono_dev // lanes
    blocks = devices * per_owner
    noise_t = noise.transpose(1, 0, 2)

    sent = jax.ShapeDtypeStruct((devices, 3 * per_owner, lanes), f32)
    chain = jax.ShapeDtypeStruct((3, mono_dev), f32)
    chain_scratch = [
        pltpu.VMEM((8, lanes + mono_dev + longest_loop), f32),
        pltpu.VMEM((8, mono_dev), f32),
    ]

    def exchange(value):
        return lax.all_to_all(value, both, split_axis=0, concat_axis=0, tiled=True)

    def contact(merged, cells):
        return call(
            functools.partial(contact_kernel, merged),
            sent,
            [smem, smem] + [vmem] * len(cells),
            (tile_rows, tile_cols, *cells),
            [
                pltpu.VMEM((3 * blocks * 16, lanes), bf16),
                pltpu.VMEM((3 * blocks * 16, lanes), bf16),
                pltpu.VMEM((blocks * 16, lanes), bf16),
                pltpu.VMEM((4, lanes, lanes), f32),
                pltpu.VMEM((2 * lanes, lanes), f32),
                pltpu.VMEM((blocks * 16, lanes), f32),
            ],
            flops=16 * tile_rows.shape[0] * lanes * lanes,
        )

    anchors_before = shifted(jnp.stack([loop_left, loop_span]), both, 1)
    before = shifted(positions, both, 1)
    after = shifted(positions[:, :longest_loop], both, -1)
    x_out, index, slot = call(
        functools.partial(index_kernel, lax.axis_size("space")),
        [
            jax.ShapeDtypeStruct((devices, 9 * per_owner, lanes), f32),
            jax.ShapeDtypeStruct((blocks, lanes), jnp.int32),
            jax.ShapeDtypeStruct((rows, lanes), jnp.int32),
        ],
        [vmem, vmem],
        (cell_owner.reshape(rows, lanes), positions),
        [pltpu.VMEM((lanes, lanes), jnp.int32), pltpu.VMEM((2 * blocks, lanes), f32)],
    )
    x_cells = exchange(x_out)
    y_out = call(
        first_kernel,
        sent,
        [smem] * 3 + [vmem] * 5,
        (loop_left, loop_span, anchors_before, positions, after, before, noise_t, index),
        [pltpu.VMEM((3, mono_dev), f32)] + chain_scratch,
    )
    y_cells = exchange(y_out)
    contact0 = contact(True, (x_cells,))
    x1_cells = y_cells + time_step * contact0
    below = shifted(x1_cells, "space", 1)
    above = shifted(x1_cells, "space", -1)
    x1_back = exchange(x1_cells)
    contact1 = contact(False, (below, x1_cells, above))
    back1 = exchange(contact1)

    x1 = call(gather_kernel, chain, [vmem] * 2, (slot, x1_back))
    before1 = shifted(x1, both, 1)
    after1 = shifted(x1[:, :longest_loop], both, -1)
    pushed = call(gather_kernel, chain, [vmem] * 3, (slot, back1, x1))
    return call(
        functools.partial(chain_kernel, 1),
        chain,
        [smem] * 3 + [vmem] * 5,
        (loop_left, loop_span, anchors_before, x1, after1, before1, noise_t, pushed),
        chain_scratch,
    )


def solution(mesh):
    in_specs = (
        P(None, ("chain", "space")),
        P(None, None, ("chain", "space")),
        P(("chain", "space"), None),
        P(("chain", "space")),
        P(("chain", "space")),
        P(("chain", "space")),
        P(("chain", "space")),
    )
    out_specs = P(None, ("chain", "space"))
    return jax.shard_map(local, mesh=mesh, in_specs=in_specs, out_specs=out_specs, check_vma=False)
```

```python
import functools
import math

import jax
import jax.numpy as jnp
from jax import lax
from jax.experimental import pallas as pl
from jax.experimental.pallas import tpu as pltpu
from jax.sharding import PartitionSpec as P

time_step = 0.05
bond_stiff = 1.0
loop_stiff = 2.0
cutoff_sq = 2.25
contact_coef = 0.4 / 2.25
noise_gain = math.sqrt(0.1)
longest_loop = 4096
lanes = 128
far_away = 1e15
pairs_at_once = 64

vmem = pl.BlockSpec(memory_space=pltpu.VMEM)
smem = pl.BlockSpec(memory_space=pltpu.SMEM)
both = ("chain", "space")
f32 = jnp.float32
bf16 = jnp.bfloat16


def call(body, outs, in_specs, args, scratch=(), flops=0, moved=2_000_000):
    many = isinstance(outs, list)
    return pl.pallas_call(
        body,
        out_shape=outs,
        in_specs=in_specs,
        out_specs=[vmem] * len(outs) if many else vmem,
        scratch_shapes=list(scratch),
        compiler_params=pltpu.CompilerParams(vmem_limit_bytes=32 * 1024 * 1024),
        cost_estimate=pl.CostEstimate(flops=flops, bytes_accessed=moved, transcendentals=0),
    )(*args)


def iota(shape, dim):
    return lax.broadcasted_iota(jnp.int32, shape, dim)


def pick(row, where_to):
    return jnp.take_along_axis(
        jnp.broadcast_to(row, where_to.shape), where_to, axis=1, mode="promise_in_bounds"
    )


def fill_slots(index_ref, source_ref, per_owner, store):
    rows = source_ref.shape[1] // lanes
    fields = source_ref.shape[0]
    owners_here = 8 // per_owner

    def one(group, carry):
        code = index_ref[pl.ds(pl.multiple_of(group * 8, 8), 8), :]
        row_of = (code >> 7) - 1
        lane_of = code & 127
        held = [jnp.full((8, lanes), far_away, f32) for _ in range(fields)]
        for j in range(rows):
            here = row_of == j
            for c in range(fields):
                row = source_ref[c : c + 1, j * lanes : (j + 1) * lanes]
                held[c] = jnp.where(here, pick(row, lane_of), held[c])
        for i in range(owners_here):
            for c in range(fields):
                store(group * owners_here + i, c, held[c][i * per_owner : (i + 1) * per_owner, :])
        return carry

    lax.fori_loop(0, index_ref.shape[0] // 8, one, 0)


def index_kernel(devices, owner_ref, index_ref, slot_ref, turned_ref, total_ref):
    rows = owner_ref.shape[0]
    per_owner = index_ref.shape[0] // devices
    own = owner_ref[...]
    lane = iota((rows, lanes), 1)
    tri = jnp.where(
        iota((lanes, 2 * lanes), 1) >= lanes,
        1.0,
        jnp.where(iota((lanes, 2 * lanes), 0) < iota((lanes, 2 * lanes), 1), 1.0, 0.0),
    ).astype(bf16)

    def count(chunk, carry):
        prefix, total = carry
        masks = jnp.concatenate(
            [jnp.where(own == chunk * 8 + i, 1.0, 0.0) for i in range(8)], axis=0
        ).astype(bf16)
        sums = jnp.dot(masks, tri, preferred_element_type=f32)
        for i in range(8):
            o = chunk * 8 + i
            part = sums[i * rows : (i + 1) * rows]
            prefix = jnp.where(own == o, part[:, :lanes], prefix)
            total = jnp.where(lane == o, part[:, lanes:], total)
        return prefix, total

    zero = jnp.zeros((rows, lanes), f32)
    prefix, total = lax.fori_loop(0, devices // 8, count, (zero, zero))
    lower = jnp.where(iota((rows, rows), 1) < iota((rows, rows), 0), 1.0, 0.0).astype(bf16)
    above = jnp.dot(lower, total.astype(bf16), preferred_element_type=f32)
    offset = jnp.take_along_axis(above, own, axis=1, mode="promise_in_bounds")
    slot = own * (per_owner * lanes) + (prefix + offset).astype(jnp.int32)
    slot_ref[...] = slot

    turned_ref[...] = jnp.concatenate([slot & 127] * (lanes // rows), axis=0).T
    down = iota((lanes, lanes), 0)
    across = iota((lanes, lanes), 1)
    lane_code = across.astype(f32)
    total_ref[...] = jnp.zeros_like(total_ref)
    at_once = 8

    def spread(chunk, carry):
        left, right = [], []
        low = turned_ref[...]
        low = jnp.where(chunk > 0, pltpu.roll(low, lanes - chunk * at_once, 1), low)
        for i in range(at_once):
            j = chunk * at_once + i
            high = (slot_ref[pl.ds(j, 1), :] >> 7) == down
            row_code = (j + 1).astype(f32)
            left.append(
                jnp.concatenate(
                    [jnp.where(high, lane_code, 0.0), jnp.where(high, row_code, 0.0)], axis=0
                ).astype(bf16)
            )
            right.append(jnp.where(low[:, i : i + 1] == across, 1.0, 0.0).astype(bf16))
        total_ref[...] += jnp.dot(
            jnp.concatenate(left, axis=1),
            jnp.concatenate(right, axis=0),
            preferred_element_type=f32,
        )
        return carry

    lax.fori_loop(0, rows // at_once, spread, 0)
    blocks = index_ref.shape[0]
    index_ref[...] = (total_ref[0:blocks, :] + lanes * total_ref[blocks:, :]).astype(jnp.int32)


def send_kernel(slabs, index_ref, x_ref, after_ref, before_ref, out_ref):
    devices = out_ref.shape[0]
    per_owner = out_ref.shape[1] // 9

    def store(owner, c, values):
        place = lax.rem(owner, slabs)
        width = 3 * per_owner
        at = c * per_owner
        up = lax.rem(owner + 1, devices)
        below = lax.rem(owner + devices - 1, devices)
        out_ref[owner, width + at : width + at + per_owner, :] = values
        out_ref[up, at : at + per_owner, :] = jnp.where(place < slabs - 1, values, far_away)
        out_ref[below, 2 * width + at : 2 * width + at + per_owner, :] = jnp.where(
            place > 0, values, far_away
        )

    fill_slots(index_ref, x_ref, per_owner, store)


def chain_forces(left_ref, span_ref, x_ref, after_ref, before_ref, anchors_ref, wide_ref, force_ref):
    mono_dev = x_ref.shape[1]
    blocks = mono_dev // lanes
    extruders = left_ref.shape[0]
    count = lax.axis_size("chain") * lax.axis_size("space")
    me = lax.axis_index("chain") * lax.axis_size("space") + lax.axis_index("space")
    wide_ref[...] = jnp.zeros_like(wide_ref)
    wide_ref[0:3, 0:lanes] = before_ref[0:3, mono_dev - lanes :]
    wide_ref[0:3, lanes : lanes + mono_dev] = x_ref[...]
    wide_ref[0:3, lanes + mono_dev :] = after_ref[...]
    lane = iota((8, lanes), 1)
    has_before = (me > 0).astype(f32)
    has_after = (me < count - 1).astype(f32)
    for j in range(blocks):
        here = wide_ref[:, (j + 1) * lanes : (j + 2) * lanes]
        left = wide_ref[:, j * lanes : (j + 1) * lanes]
        right = wide_ref[:, (j + 2) * lanes : (j + 3) * lanes]
        down = pltpu.roll(jnp.where(lane == lanes - 1, left, here), 1, 1) - here
        up = pltpu.roll(jnp.where(lane == 0, right, here), lanes - 1, 1) - here
        if j == 0:
            down = jnp.where(lane == 0, down * has_before, down)
        if j == blocks - 1:
            up = jnp.where(lane == lanes - 1, up * has_after, up)
        force_ref[:, j * lanes : (j + 1) * lanes] = bond_stiff * down + bond_stiff * up

    def window(ref, at):
        return ref.at[:, pl.ds(pl.multiple_of((at >> 7) * lanes, lanes), lanes)]

    def value(block, at):
        there = iota(block.shape, 1) == (at & 127)
        return jnp.sum(jnp.where(there, block, 0.0), axis=1, keepdims=True)

    todo = []
    for e in range(extruders):
        a = left_ref[e] - me * mono_dev
        b = a + span_ref[e]
        pull = loop_stiff * (
            value(window(wide_ref, b + lanes)[...], b) - value(window(wide_ref, a + lanes)[...], a)
        )
        todo.append((a, pull))
        todo.append((jnp.minimum(b, mono_dev - 1), jnp.where(b < mono_dev, -pull, 0.0)))
    for e in range(extruders):
        a = anchors_ref[0, e] - (me - 1) * mono_dev
        b = a + anchors_ref[1, e] - mono_dev
        wanted = jnp.logical_and(b >= 0, me > 0)
        a = jnp.where(wanted, a, 0)
        b = jnp.where(wanted, b, 0)
        far_end = value(window(before_ref, a)[0:3, :], a)
        pull = loop_stiff * (value(window(wide_ref, b + lanes)[...], b)[0:3] - far_end)
        pull = jnp.where(wanted, -pull, 0.0)
        todo.append((b, jnp.concatenate([pull, jnp.zeros((5, 1), f32)], axis=0)))
    for at, pull in todo:
        spot = window(force_ref, at)
        spot[...] = spot[...] + jnp.where(lane == (at & 127), pull, 0.0)


def chain_kernel(
    step, left_ref, span_ref, anchors_ref, x_ref, after_ref, before_ref, noise_ref, base_ref, out_ref, wide_ref, force_ref
):
    chain_forces(left_ref, span_ref, x_ref, after_ref, before_ref, anchors_ref, wide_ref, force_ref)
    for c in range(3):
        out_ref[c : c + 1, :] = (
            base_ref[c : c + 1, :]
            + time_step * force_ref[c : c + 1, :]
            + noise_gain * noise_ref[c, step : step + 1, :]
        )


def first_kernel(
    left_ref, span_ref, anchors_ref, x_ref, after_ref, before_ref, noise_ref, index_ref, out_ref, y_ref, wide_ref, force_ref
):
    chain_kernel(
        0, left_ref, span_ref, anchors_ref, x_ref, after_ref, before_ref, noise_ref, x_ref, y_ref, wide_ref, force_ref
    )
    per_owner = out_ref.shape[1] // 3

    def store(owner, c, values):
        out_ref[owner, c * per_owner : (c + 1) * per_owner, :] = values

    fill_slots(index_ref, y_ref, per_owner, store)


def pieces(x):
    high = x.astype(bf16).astype(f32)
    middle = (x - high).astype(bf16).astype(f32)
    return high, middle, x - high - middle


def contact_kernel(merged, rows_ref, cols_ref, *refs):
    if merged:
        cells_ref, refs = refs[0], refs[1:]
        width = cells_ref.shape[1] // 3
        sides = [(cells_ref, 0), (cells_ref, width), (cells_ref, 2 * width)]
    else:
        sides = [(refs[0], 0), (refs[1], 0), (refs[2], 0)]
        width = refs[0].shape[1]
        refs = refs[3:]
    out_ref, refs = refs[0], refs[1:]
    far_t, far_x, near_t, stage, cap, total = refs
    devices = out_ref.shape[0]
    per_owner = width // 3
    blocks = devices * per_owner
    owners = 8 // per_owner
    scale = 1.0 / math.sqrt(cutoff_sq)
    place = lax.axis_index("space")
    has_below = place > 0
    has_above = place < lax.axis_size("space") - 1
    cap[0:lanes, :] = jnp.full((lanes, lanes), 1e30, f32)
    cap[lanes:, :] = jnp.where(iota((lanes, lanes), 0) == iota((lanes, lanes), 1), 0.0, 1e30)
    stage[...] = jnp.zeros_like(stage)
    total[...] = jnp.zeros_like(total)

    def eight(ref, first, group, c):
        at = first + c * per_owner
        return jnp.concatenate(
            [ref[group * owners + i, at : at + per_owner, :] for i in range(owners)], axis=0
        )

    def build(group, carry):
        for side, valid in enumerate((has_below, None, has_above)):
            ref, first = sides[side]
            xs = [eight(ref, first, group, c) for c in range(3)]
            live = xs[0] < 0.5 * far_away
            if valid is not None:
                live = jnp.logical_and(live, jnp.full((8, lanes), valid.astype(jnp.int32)) > 0)
            xs = [jnp.where(live, x, 0.0) * scale for x in xs]
            square = xs[0] * xs[0] + xs[1] * xs[1] + xs[2] * xs[2]
            high, middle, low = [list(part) for part in zip(*[pieces(x) for x in xs])]
            one = [jnp.ones((8, lanes), f32)] * 3
            spot = stage.at[side]
            far = high + middle + high + list(pieces(jnp.where(live, -square, -1e9))) + one
            for f, v in enumerate(far):
                spot[pl.ds(f, 8, stride=16), :] = v
            at = pl.ds(pl.multiple_of((side * blocks + group * 8) * 16, lanes), lanes)
            far_t[at, :] = spot[...].astype(bf16).T
            for f in range(3):
                spot[pl.ds(6 + f, 8, stride=16), :] = low[f]
            far_x[at, :] = spot[...].astype(bf16)
            if side == 1:
                spot = stage.at[3]
                near = [2.0 * v for v in high + high + middle] + one
                near += list(pieces(jnp.where(live, 1.0 - square, -1e9)))
                for f, v in enumerate(near):
                    spot[pl.ds(f, 8, stride=16), :] = v
                near_t[pl.ds(pl.multiple_of(group * lanes, lanes), lanes), :] = spot[...].astype(bf16)
        return carry

    lax.fori_loop(0, blocks // 8, build, 0)
    zero = jnp.zeros((lanes, lanes), bf16)

    def sixteen(ref, block):
        return ref[pl.ds(pl.multiple_of(block * 16, 16), 16), :]

    pairs = min(pairs_at_once, rows_ref.shape[0] // 2)

    def tiles(step, carry):
        results = []
        for pair in range(pairs):
            first = (step * pairs + pair) * 2
            ids = [(rows_ref[first + i], cols_ref[first + i]) for i in range(2)]
            left, right = [], []
            for r, q in ids:
                near = sixteen(near_t, r)
                right.append(
                    jnp.concatenate(
                        [jnp.where((q & 7) == k, near, jnp.zeros_like(near)) for k in range(8)], axis=0
                    )
                )
                left.append(far_t[pl.ds(pl.multiple_of((q >> 3) * lanes, lanes), lanes), :])
            right = jnp.concatenate(
                [jnp.concatenate([right[0], zero], axis=1), jnp.concatenate([zero, right[1]], axis=1)],
                axis=0,
            )
            reach = jnp.dot(jnp.concatenate(left, axis=1), right, preferred_element_type=f32)
            for i, (r, q) in enumerate(ids):
                same = (q == r + blocks).astype(jnp.int32)
                most = cap[pl.ds(pl.multiple_of(same * lanes, lanes), lanes), :]
                w = jnp.maximum(jnp.minimum(reach[:, i * lanes : (i + 1) * lanes], most), 0.0).astype(bf16)
                results.append((r, jnp.dot(sixteen(far_x, q), w, preferred_element_type=f32)))
        for r, v in results:
            spot = total.at[pl.ds(pl.multiple_of(r * 16, 16), 16), :]
            spot[...] = spot[...] + v
        return carry

    lax.fori_loop(0, rows_ref.shape[0] // (2 * pairs), tiles, 0)
    back = contact_coef * math.sqrt(cutoff_sq)

    def finish(group, carry):
        sums = [total[pl.ds(group * lanes + f, 8, stride=16), :] for f in range(13)]
        for c in range(3):
            place = eight(sides[1][0], sides[1][1], group, c)
            here = jnp.where(place < 0.5 * far_away, place, 0.0) * scale
            force = (here * sums[12] - (sums[c] + sums[3 + c] + sums[6 + c])) * back
            for i in range(owners):
                out_ref[group * owners + i, c * per_owner : (c + 1) * per_owner, :] = force[
                    i * per_owner : (i + 1) * per_owner
                ]
        return carry

    lax.fori_loop(0, blocks // 8, finish, 0)


def gather_kernel(slot_ref, source_ref, *refs):
    base_ref, out_ref = refs if len(refs) == 2 else (None, refs[0])
    per_owner = source_ref.shape[1] // 3

    def one(group, carry):
        slot = slot_ref[pl.ds(pl.multiple_of(group * 8, 8), 8), :]
        row_of = slot >> 7
        lane_of = slot & 127
        held = [jnp.zeros((8, lanes), f32) for _ in range(3)]
        for s in range(source_ref.shape[0] * per_owner):
            here = row_of == s
            for c in range(3):
                at = c * per_owner + s % per_owner
                row = source_ref[s // per_owner, at : at + 1, :]
                held[c] = jnp.where(here, pick(row, lane_of), held[c])
        for i in range(8):
            at = pl.ds(pl.multiple_of((group * 8 + i) * lanes, lanes), lanes)
            for c in range(3):
                value = held[c][i : i + 1, :]
                if base_ref is not None:
                    value = base_ref[c : c + 1, at] + time_step * value
                out_ref[c : c + 1, at] = value
        return carry

    lax.fori_loop(0, slot_ref.shape[0] // 8, one, 0)


def shifted(value, axis, steps):
    count = lax.axis_size(axis)
    first, last = (max(0, -steps), min(count, count - steps))
    return lax.ppermute(value, axis, [(source, source + steps) for source in range(first, last)])


def local(positions, noise, cell_owner, tile_rows, tile_cols, loop_left, loop_span):
    devices = lax.axis_size(both)
    mono_dev = positions.shape[1]
    per_owner = 2 * mono_dev // devices // lanes
    rows = mono_dev // lanes
    blocks = devices * per_owner
    noise_t = noise.transpose(1, 0, 2)

    sent = jax.ShapeDtypeStruct((devices, 3 * per_owner, lanes), f32)
    chain = jax.ShapeDtypeStruct((3, mono_dev), f32)
    chain_scratch = [
        pltpu.VMEM((8, lanes + mono_dev + longest_loop), f32),
        pltpu.VMEM((8, mono_dev), f32),
    ]

    def exchange(value):
        return lax.all_to_all(value, both, split_axis=0, concat_axis=0, tiled=True)

    def contact(merged, cells):
        return call(
            functools.partial(contact_kernel, merged),
            sent,
            [smem, smem] + [vmem] * len(cells),
            (tile_rows, tile_cols, *cells),
            [
                pltpu.VMEM((3 * blocks * 16, lanes), bf16),
                pltpu.VMEM((3 * blocks * 16, lanes), bf16),
                pltpu.VMEM((blocks * 16, lanes), bf16),
                pltpu.VMEM((4, lanes, lanes), f32),
                pltpu.VMEM((2 * lanes, lanes), f32),
                pltpu.VMEM((blocks * 16, lanes), f32),
            ],
            flops=1600 * tile_rows.shape[0] * lanes * lanes,
        )

    extruders = loop_left.shape[0]
    anchors = jnp.concatenate([loop_left, loop_span]).astype(f32)
    anchors = jnp.pad(anchors, (0, mono_dev - 2 * extruders))
    before = shifted(jnp.concatenate([positions, anchors[None]], axis=0), both, 1)
    after = shifted(positions[:, :longest_loop], both, -1)
    index, slot = call(
        functools.partial(index_kernel, devices),
        [
            jax.ShapeDtypeStruct((blocks, lanes), jnp.int32),
            jax.ShapeDtypeStruct((rows, lanes), jnp.int32),
        ],
        [vmem],
        (cell_owner.reshape(rows, lanes),),
        [pltpu.VMEM((lanes, lanes), jnp.int32), pltpu.VMEM((2 * blocks, lanes), f32)],
    )
    x_out = call(
        functools.partial(send_kernel, lax.axis_size("space")),
        jax.ShapeDtypeStruct((devices, 9 * per_owner, lanes), f32),
        [vmem] * 4,
        (index, positions, after, before),
    )
    anchors_before = before[3, : 2 * extruders].astype(jnp.int32).reshape(2, extruders)
    x_cells = exchange(x_out)
    y_out = call(
        first_kernel,
        sent,
        [smem] * 3 + [vmem] * 5,
        (loop_left, loop_span, anchors_before, positions, after, before, noise_t, index),
        [pltpu.VMEM((3, mono_dev), f32)] + chain_scratch,
    )
    y_cells = exchange(y_out)
    contact0 = contact(True, (x_cells,))
    x1_cells = y_cells + time_step * contact0
    below = shifted(x1_cells, "space", 1)
    above = shifted(x1_cells, "space", -1)
    x1_back = exchange(x1_cells)
    contact1 = contact(False, (below, x1_cells, above))
    back1 = exchange(contact1)

    x1 = call(gather_kernel, chain, [vmem] * 2, (slot, x1_back))
    before1 = shifted(x1, both, 1)
    after1 = shifted(x1[:, :longest_loop], both, -1)
    pushed = call(gather_kernel, chain, [vmem] * 3, (slot, back1, x1))
    return call(
        functools.partial(chain_kernel, 1),
        chain,
        [smem] * 3 + [vmem] * 5,
        (loop_left, loop_span, anchors_before, x1, after1, before1, noise_t, pushed),
        chain_scratch,
    )


def solution(mesh):
    in_specs = (
        P(None, ("chain", "space")),
        P(None, None, ("chain", "space")),
        P(("chain", "space"), None),
        P(("chain", "space")),
        P(("chain", "space")),
        P(("chain", "space")),
        P(("chain", "space")),
    )
    out_specs = P(None, ("chain", "space"))
    return jax.shard_map(local, mesh=mesh, in_specs=in_specs, out_specs=out_specs, check_vma=False)
```

```python
import functools
import math

import jax
import jax.numpy as jnp
from jax import lax
from jax.experimental import pallas as pl
from jax.experimental.pallas import tpu as pltpu
from jax.sharding import PartitionSpec as P

time_step = 0.05
bond_stiff = 1.0
loop_stiff = 2.0
cutoff_sq = 2.25
contact_coef = 0.4 / 2.25
noise_gain = math.sqrt(0.1)
longest_loop = 4096
lanes = 128
far_away = 1e15
pairs_at_once = 64

vmem = pl.BlockSpec(memory_space=pltpu.VMEM)
smem = pl.BlockSpec(memory_space=pltpu.SMEM)
both = ("chain", "space")
f32 = jnp.float32
bf16 = jnp.bfloat16


def call(body, outs, in_specs, args, scratch=(), micros=1):
    many = isinstance(outs, list)
    return pl.pallas_call(
        body,
        out_shape=outs,
        in_specs=in_specs,
        out_specs=[vmem] * len(outs) if many else vmem,
        scratch_shapes=list(scratch),
        compiler_params=pltpu.CompilerParams(vmem_limit_bytes=32 * 1024 * 1024),
        cost_estimate=pl.CostEstimate(
            flops=int(micros * 1e9), bytes_accessed=1_000_000, transcendentals=0
        ),
    )(*args)


def iota(shape, dim):
    return lax.broadcasted_iota(jnp.int32, shape, dim)


def pick(row, where_to):
    return jnp.take_along_axis(
        jnp.broadcast_to(row, where_to.shape), where_to, axis=1, mode="promise_in_bounds"
    )


def fill_slots(index_ref, source_ref, per_owner, store):
    rows = source_ref.shape[1] // lanes
    fields = source_ref.shape[0]
    owners_here = 8 // per_owner

    def one(group, carry):
        code = index_ref[pl.ds(pl.multiple_of(group * 8, 8), 8), :]
        row_of = (code >> 7) - 1
        lane_of = code & 127
        held = [jnp.full((8, lanes), far_away, f32) for _ in range(fields)]
        for j in range(rows):
            here = row_of == j
            for c in range(fields):
                row = source_ref[c : c + 1, j * lanes : (j + 1) * lanes]
                held[c] = jnp.where(here, pick(row, lane_of), held[c])
        for i in range(owners_here):
            for c in range(fields):
                store(group * owners_here + i, c, held[c][i * per_owner : (i + 1) * per_owner, :])
        return carry

    lax.fori_loop(0, index_ref.shape[0] // 8, one, 0)


def index_kernel(devices, owner_ref, index_ref, slot_ref, turned_ref, total_ref):
    rows = owner_ref.shape[0]
    per_owner = index_ref.shape[0] // devices
    own = owner_ref[...]
    lane = iota((rows, lanes), 1)
    tri = jnp.where(
        iota((lanes, 2 * lanes), 1) >= lanes,
        1.0,
        jnp.where(iota((lanes, 2 * lanes), 0) < iota((lanes, 2 * lanes), 1), 1.0, 0.0),
    ).astype(bf16)

    def count(chunk, carry):
        prefix, total = carry
        masks = jnp.concatenate(
            [jnp.where(own == chunk * 8 + i, 1.0, 0.0) for i in range(8)], axis=0
        ).astype(bf16)
        sums = jnp.dot(masks, tri, preferred_element_type=f32)
        for i in range(8):
            o = chunk * 8 + i
            part = sums[i * rows : (i + 1) * rows]
            prefix = jnp.where(own == o, part[:, :lanes], prefix)
            total = jnp.where(lane == o, part[:, lanes:], total)
        return prefix, total

    zero = jnp.zeros((rows, lanes), f32)
    prefix, total = lax.fori_loop(0, devices // 8, count, (zero, zero))
    lower = jnp.where(iota((rows, rows), 1) < iota((rows, rows), 0), 1.0, 0.0).astype(bf16)
    above = jnp.dot(lower, total.astype(bf16), preferred_element_type=f32)
    offset = jnp.take_along_axis(above, own, axis=1, mode="promise_in_bounds")
    slot = own * (per_owner * lanes) + (prefix + offset).astype(jnp.int32)
    slot_ref[...] = slot

    turned_ref[...] = jnp.concatenate([slot & 127] * (lanes // rows), axis=0).T
    down = iota((lanes, lanes), 0)
    across = iota((lanes, lanes), 1)
    lane_code = across.astype(f32)
    total_ref[...] = jnp.zeros_like(total_ref)
    at_once = 8

    def spread(chunk, carry):
        left, right = [], []
        low = turned_ref[...]
        low = jnp.where(chunk > 0, pltpu.roll(low, lanes - chunk * at_once, 1), low)
        for i in range(at_once):
            j = chunk * at_once + i
            high = (slot_ref[pl.ds(j, 1), :] >> 7) == down
            row_code = (j + 1).astype(f32)
            left.append(
                jnp.concatenate(
                    [jnp.where(high, lane_code, 0.0), jnp.where(high, row_code, 0.0)], axis=0
                ).astype(bf16)
            )
            right.append(jnp.where(low[:, i : i + 1] == across, 1.0, 0.0).astype(bf16))
        total_ref[...] += jnp.dot(
            jnp.concatenate(left, axis=1),
            jnp.concatenate(right, axis=0),
            preferred_element_type=f32,
        )
        return carry

    lax.fori_loop(0, rows // at_once, spread, 0)
    blocks = index_ref.shape[0]
    index_ref[...] = (total_ref[0:blocks, :] + lanes * total_ref[blocks:, :]).astype(jnp.int32)


def send_kernel(index_ref, x_ref, after_ref, before_ref, out_ref):
    per_owner = out_ref.shape[1] // 3

    def store(owner, c, values):
        out_ref[owner, c * per_owner : (c + 1) * per_owner, :] = values

    fill_slots(index_ref, x_ref, per_owner, store)


def chain_forces(left_ref, span_ref, x_ref, after_ref, before_ref, anchors_ref, wide_ref, force_ref):
    mono_dev = x_ref.shape[1]
    blocks = mono_dev // lanes
    extruders = left_ref.shape[0]
    count = lax.axis_size("chain") * lax.axis_size("space")
    me = lax.axis_index("chain") * lax.axis_size("space") + lax.axis_index("space")
    wide_ref[...] = jnp.zeros_like(wide_ref)
    wide_ref[0:3, 0:lanes] = before_ref[0:3, mono_dev - lanes :]
    wide_ref[0:3, lanes : lanes + mono_dev] = x_ref[...]
    wide_ref[0:3, lanes + mono_dev :] = after_ref[...]
    lane = iota((8, lanes), 1)
    has_before = (me > 0).astype(f32)
    has_after = (me < count - 1).astype(f32)
    for j in range(blocks):
        here = wide_ref[:, (j + 1) * lanes : (j + 2) * lanes]
        left = wide_ref[:, j * lanes : (j + 1) * lanes]
        right = wide_ref[:, (j + 2) * lanes : (j + 3) * lanes]
        down = pltpu.roll(jnp.where(lane == lanes - 1, left, here), 1, 1) - here
        up = pltpu.roll(jnp.where(lane == 0, right, here), lanes - 1, 1) - here
        if j == 0:
            down = jnp.where(lane == 0, down * has_before, down)
        if j == blocks - 1:
            up = jnp.where(lane == lanes - 1, up * has_after, up)
        force_ref[:, j * lanes : (j + 1) * lanes] = bond_stiff * down + bond_stiff * up

    def window(ref, at):
        return ref.at[:, pl.ds(pl.multiple_of((at >> 7) * lanes, lanes), lanes)]

    def value(block, at):
        there = iota(block.shape, 1) == (at & 127)
        return jnp.sum(jnp.where(there, block, 0.0), axis=1, keepdims=True)

    todo = []
    for e in range(extruders):
        a = left_ref[e] - me * mono_dev
        b = a + span_ref[e]
        pull = loop_stiff * (
            value(window(wide_ref, b + lanes)[...], b) - value(window(wide_ref, a + lanes)[...], a)
        )
        todo.append((a, pull))
        todo.append((jnp.minimum(b, mono_dev - 1), jnp.where(b < mono_dev, -pull, 0.0)))
    for e in range(extruders):
        a = anchors_ref[0, e] - (me - 1) * mono_dev
        b = a + anchors_ref[1, e] - mono_dev
        wanted = jnp.logical_and(b >= 0, me > 0)
        a = jnp.where(wanted, a, 0)
        b = jnp.where(wanted, b, 0)
        far_end = value(window(before_ref, a)[0:3, :], a)
        pull = loop_stiff * (value(window(wide_ref, b + lanes)[...], b)[0:3] - far_end)
        pull = jnp.where(wanted, -pull, 0.0)
        todo.append((b, jnp.concatenate([pull, jnp.zeros((5, 1), f32)], axis=0)))
    for at, pull in todo:
        spot = window(force_ref, at)
        spot[...] = spot[...] + jnp.where(lane == (at & 127), pull, 0.0)


def chain_kernel(
    step, left_ref, span_ref, anchors_ref, x_ref, after_ref, before_ref, noise_ref, base_ref, out_ref, wide_ref, force_ref
):
    chain_forces(left_ref, span_ref, x_ref, after_ref, before_ref, anchors_ref, wide_ref, force_ref)
    for c in range(3):
        out_ref[c : c + 1, :] = (
            base_ref[c : c + 1, :]
            + time_step * force_ref[c : c + 1, :]
            + noise_gain * noise_ref[c, step : step + 1, :]
        )


def first_kernel(
    left_ref, span_ref, anchors_ref, x_ref, after_ref, before_ref, noise_ref, index_ref, out_ref, y_ref, wide_ref, force_ref
):
    chain_kernel(
        0, left_ref, span_ref, anchors_ref, x_ref, after_ref, before_ref, noise_ref, x_ref, y_ref, wide_ref, force_ref
    )
    per_owner = out_ref.shape[1] // 3

    def store(owner, c, values):
        out_ref[owner, c * per_owner : (c + 1) * per_owner, :] = values

    fill_slots(index_ref, y_ref, per_owner, store)


def pieces(x):
    high = x.astype(bf16).astype(f32)
    middle = (x - high).astype(bf16).astype(f32)
    return high, middle, x - high - middle


def contact_kernel(
    rows_ref, cols_ref, below_ref, own_ref, above_ref, out_ref, far_t, far_x, near_t, stage, cap, total
):
    devices = out_ref.shape[0]
    per_owner = out_ref.shape[1] // 3
    blocks = devices * per_owner
    owners = 8 // per_owner
    scale = 1.0 / math.sqrt(cutoff_sq)
    place = lax.axis_index("space")
    has_below = place > 0
    has_above = place < lax.axis_size("space") - 1
    cap[0:lanes, :] = jnp.full((lanes, lanes), 1e30, f32)
    cap[lanes:, :] = jnp.where(iota((lanes, lanes), 0) == iota((lanes, lanes), 1), 0.0, 1e30)
    stage[...] = jnp.zeros_like(stage)
    total[...] = jnp.zeros_like(total)

    def eight(ref, group, c):
        return ref[c, pl.ds(pl.multiple_of(group * 8, 8), 8), :]

    def build(group, carry):
        sides = ((below_ref, has_below), (own_ref, None), (above_ref, has_above))
        for side, (ref, valid) in enumerate(sides):
            xs = [eight(ref, group, c) for c in range(3)]
            live = xs[0] < 0.5 * far_away
            if valid is not None:
                live = jnp.logical_and(live, jnp.full((8, lanes), valid.astype(jnp.int32)) > 0)
            xs = [jnp.where(live, x, 0.0) * scale for x in xs]
            square = xs[0] * xs[0] + xs[1] * xs[1] + xs[2] * xs[2]
            high, middle, low = [list(part) for part in zip(*[pieces(x) for x in xs])]
            one = [jnp.ones((8, lanes), f32)] * 3
            spot = stage.at[side]
            far = high + middle + high + list(pieces(jnp.where(live, -square, -1e9))) + one
            for f, v in enumerate(far):
                spot[pl.ds(f, 8, stride=16), :] = v
            at = pl.ds(pl.multiple_of((side * blocks + group * 8) * 16, lanes), lanes)
            far_t[at, :] = spot[...].astype(bf16).T
            for f in range(3):
                spot[pl.ds(6 + f, 8, stride=16), :] = low[f]
            far_x[at, :] = spot[...].astype(bf16)
            if side == 1:
                spot = stage.at[3]
                near = [2.0 * v for v in high + high + middle] + one
                near += list(pieces(jnp.where(live, 1.0 - square, -1e9)))
                for f, v in enumerate(near):
                    spot[pl.ds(f, 8, stride=16), :] = v
                near_t[pl.ds(pl.multiple_of(group * lanes, lanes), lanes), :] = spot[...].astype(bf16)
        return carry

    lax.fori_loop(0, blocks // 8, build, 0)
    zero = jnp.zeros((lanes, lanes), bf16)

    def sixteen(ref, block):
        return ref[pl.ds(pl.multiple_of(block * 16, 16), 16), :]

    pairs = min(pairs_at_once, rows_ref.shape[0] // 2)

    def tiles(step, carry):
        results = []
        for pair in range(pairs):
            first = (step * pairs + pair) * 2
            ids = [(rows_ref[first + i], cols_ref[first + i]) for i in range(2)]
            left, right = [], []
            for r, q in ids:
                near = sixteen(near_t, r)
                right.append(
                    jnp.concatenate(
                        [jnp.where((q & 7) == k, near, jnp.zeros_like(near)) for k in range(8)], axis=0
                    )
                )
                left.append(far_t[pl.ds(pl.multiple_of((q >> 3) * lanes, lanes), lanes), :])
            right = jnp.concatenate(
                [jnp.concatenate([right[0], zero], axis=1), jnp.concatenate([zero, right[1]], axis=1)],
                axis=0,
            )
            reach = jnp.dot(jnp.concatenate(left, axis=1), right, preferred_element_type=f32)
            for i, (r, q) in enumerate(ids):
                same = (q == r + blocks).astype(jnp.int32)
                most = cap[pl.ds(pl.multiple_of(same * lanes, lanes), lanes), :]
                w = jnp.maximum(jnp.minimum(reach[:, i * lanes : (i + 1) * lanes], most), 0.0).astype(bf16)
                results.append((r, jnp.dot(sixteen(far_x, q), w, preferred_element_type=f32)))
        for r, v in results:
            spot = total.at[pl.ds(pl.multiple_of(r * 16, 16), 16), :]
            spot[...] = spot[...] + v
        return carry

    lax.fori_loop(0, rows_ref.shape[0] // (2 * pairs), tiles, 0)
    back = contact_coef * math.sqrt(cutoff_sq)

    def finish(group, carry):
        sums = [total[pl.ds(group * lanes + f, 8, stride=16), :] for f in range(13)]
        for c in range(3):
            place = eight(own_ref, group, c)
            here = jnp.where(place < 0.5 * far_away, place, 0.0) * scale
            force = (here * sums[12] - (sums[c] + sums[3 + c] + sums[6 + c])) * back
            for i in range(owners):
                out_ref[group * owners + i, c * per_owner : (c + 1) * per_owner, :] = force[
                    i * per_owner : (i + 1) * per_owner
                ]
        return carry

    lax.fori_loop(0, blocks // 8, finish, 0)


def gather_kernel(slot_ref, source_ref, *refs):
    base_ref, out_ref = refs if len(refs) == 2 else (None, refs[0])
    per_owner = source_ref.shape[1] // 3

    def one(group, carry):
        slot = slot_ref[pl.ds(pl.multiple_of(group * 8, 8), 8), :]
        row_of = slot >> 7
        lane_of = slot & 127
        held = [jnp.zeros((8, lanes), f32) for _ in range(3)]
        for s in range(source_ref.shape[0] * per_owner):
            here = row_of == s
            for c in range(3):
                at = c * per_owner + s % per_owner
                row = source_ref[s // per_owner, at : at + 1, :]
                held[c] = jnp.where(here, pick(row, lane_of), held[c])
        for i in range(8):
            at = pl.ds(pl.multiple_of((group * 8 + i) * lanes, lanes), lanes)
            for c in range(3):
                value = held[c][i : i + 1, :]
                if base_ref is not None:
                    value = base_ref[c : c + 1, at] + time_step * value
                out_ref[c : c + 1, at] = value
        return carry

    lax.fori_loop(0, slot_ref.shape[0] // 8, one, 0)


def turn_kernel(cells_ref, later_ref, out_ref):
    per_owner = cells_ref.shape[1] // 3
    for o in range(cells_ref.shape[0]):
        for c in range(3):
            out_ref[c, o * per_owner : (o + 1) * per_owner, :] = cells_ref[
                o, c * per_owner : (c + 1) * per_owner, :
            ]


def advance_kernel(y_ref, force_ref, plain_ref, turned_ref):
    per_owner = y_ref.shape[1] // 3
    for o in range(y_ref.shape[0]):
        for c in range(3):
            at = slice(c * per_owner, (c + 1) * per_owner)
            value = y_ref[o, at, :] + time_step * force_ref[o, at, :]
            plain_ref[o, at, :] = value
            turned_ref[c, o * per_owner : (o + 1) * per_owner, :] = value


def shifted(value, axis, steps):
    count = lax.axis_size(axis)
    first, last = (max(0, -steps), min(count, count - steps))
    return lax.ppermute(value, axis, [(source, source + steps) for source in range(first, last)])


def local(positions, noise, cell_owner, tile_rows, tile_cols, loop_left, loop_span):
    devices = lax.axis_size(both)
    mono_dev = positions.shape[1]
    per_owner = 2 * mono_dev // devices // lanes
    rows = mono_dev // lanes
    blocks = devices * per_owner
    noise_t = noise.transpose(1, 0, 2)

    sent = jax.ShapeDtypeStruct((devices, 3 * per_owner, lanes), f32)
    chain = jax.ShapeDtypeStruct((3, mono_dev), f32)
    chain_scratch = [
        pltpu.VMEM((8, lanes + mono_dev + longest_loop), f32),
        pltpu.VMEM((8, mono_dev), f32),
    ]

    def exchange(value):
        return lax.all_to_all(value, both, split_axis=0, concat_axis=0, tiled=True)

    def contact(cells):
        below = shifted(cells, "space", 1)
        above = shifted(cells, "space", -1)
        return call(
            contact_kernel,
            sent,
            [smem, smem] + [vmem] * 3,
            (tile_rows, tile_cols, below, cells, above),
            [
                pltpu.VMEM((3 * blocks * 16, lanes), bf16),
                pltpu.VMEM((3 * blocks * 16, lanes), bf16),
                pltpu.VMEM((blocks * 16, lanes), bf16),
                pltpu.VMEM((4, lanes, lanes), f32),
                pltpu.VMEM((2 * lanes, lanes), f32),
                pltpu.VMEM((blocks * 16, lanes), f32),
            ],
            micros=14,
        )

    extruders = loop_left.shape[0]
    anchors = jnp.concatenate([loop_left, loop_span]).astype(f32)
    anchors = jnp.pad(anchors, (0, mono_dev - 2 * extruders))
    before = shifted(jnp.concatenate([positions, anchors[None]], axis=0), both, 1)
    after = shifted(positions[:, :longest_loop], both, -1)
    index, slot = call(
        functools.partial(index_kernel, devices),
        [
            jax.ShapeDtypeStruct((blocks, lanes), jnp.int32),
            jax.ShapeDtypeStruct((rows, lanes), jnp.int32),
        ],
        [vmem],
        (cell_owner.reshape(rows, lanes),),
        [pltpu.VMEM((lanes, lanes), jnp.int32), pltpu.VMEM((2 * blocks, lanes), f32)],
        micros=6,
    )
    x_out = call(
        send_kernel,
        sent,
        [vmem] * 4,
        (index, positions, after, before),
        micros=4,
    )
    anchors_before = before[3, : 2 * extruders].astype(jnp.int32).reshape(2, extruders)
    x_cells = exchange(x_out)
    y_out = call(
        first_kernel,
        sent,
        [smem] * 3 + [vmem] * 5,
        (loop_left, loop_span, anchors_before, positions, after, before, noise_t, index),
        [pltpu.VMEM((3, mono_dev), f32)] + chain_scratch,
        micros=6,
    )
    y_cells = exchange(y_out)
    turned = jax.ShapeDtypeStruct((3, blocks, lanes), f32)
    hbm = pl.BlockSpec(memory_space=pl.ANY)
    contact0 = contact(call(turn_kernel, turned, [vmem, hbm], (x_cells, y_out)))
    x1_cells, x1_turned = call(advance_kernel, [sent, turned], [vmem] * 2, (y_cells, contact0))
    x1_back = exchange(x1_cells)
    contact1 = contact(x1_turned)
    back1 = exchange(contact1)

    x1 = call(gather_kernel, chain, [vmem] * 2, (slot, x1_back), micros=4)
    before1 = shifted(x1, both, 1)
    after1 = shifted(x1[:, :longest_loop], both, -1)
    pushed = call(gather_kernel, chain, [vmem] * 3, (slot, back1, x1), micros=4)
    return call(
        functools.partial(chain_kernel, 1),
        chain,
        [smem] * 3 + [vmem] * 5,
        (loop_left, loop_span, anchors_before, x1, after1, before1, noise_t, pushed),
        chain_scratch,
    )


def solution(mesh):
    in_specs = (
        P(None, ("chain", "space")),
        P(None, None, ("chain", "space")),
        P(("chain", "space"), None),
        P(("chain", "space")),
        P(("chain", "space")),
        P(("chain", "space")),
        P(("chain", "space")),
    )
    out_specs = P(None, ("chain", "space"))
    return jax.shard_map(local, mesh=mesh, in_specs=in_specs, out_specs=out_specs, check_vma=False)
```

```python
import functools
import math

import jax
import jax.numpy as jnp
from jax import lax
from jax.experimental import pallas as pl
from jax.experimental.pallas import tpu as pltpu
from jax.sharding import PartitionSpec as P

time_step = 0.05
bond_stiff = 1.0
loop_stiff = 2.0
cutoff_sq = 2.25
contact_coef = 0.4 / 2.25
noise_gain = math.sqrt(0.1)
longest_loop = 4096
lanes = 128
far_away = 1e15
pairs_at_once = 64

vmem = pl.BlockSpec(memory_space=pltpu.VMEM)
smem = pl.BlockSpec(memory_space=pltpu.SMEM)
both = ("chain", "space")
f32 = jnp.float32
bf16 = jnp.bfloat16


def call(body, outs, in_specs, args, scratch=(), micros=1):
    many = isinstance(outs, list)
    return pl.pallas_call(
        body,
        out_shape=outs,
        in_specs=in_specs,
        out_specs=[vmem] * len(outs) if many else vmem,
        scratch_shapes=list(scratch),
        compiler_params=pltpu.CompilerParams(vmem_limit_bytes=32 * 1024 * 1024),
        cost_estimate=pl.CostEstimate(
            flops=int(micros * 1e9), bytes_accessed=1_000_000, transcendentals=0
        ),
    )(*args)


def iota(shape, dim):
    return lax.broadcasted_iota(jnp.int32, shape, dim)


def pick(row, where_to):
    return jnp.take_along_axis(
        jnp.broadcast_to(row, where_to.shape), where_to, axis=1, mode="promise_in_bounds"
    )


def fill_slots(index_ref, source_ref, per_owner, store):
    rows = source_ref.shape[1] // lanes
    fields = source_ref.shape[0]
    owners_here = 8 // per_owner

    def one(group, carry):
        code = index_ref[pl.ds(pl.multiple_of(group * 8, 8), 8), :]
        row_of = (code >> 7) - 1
        lane_of = code & 127
        held = [jnp.full((8, lanes), far_away, f32) for _ in range(fields)]
        for j in range(rows):
            here = row_of == j
            for c in range(fields):
                row = source_ref[c : c + 1, j * lanes : (j + 1) * lanes]
                held[c] = jnp.where(here, pick(row, lane_of), held[c])
        for i in range(owners_here):
            for c in range(fields):
                store(group * owners_here + i, c, held[c][i * per_owner : (i + 1) * per_owner, :])
        return carry

    lax.fori_loop(0, index_ref.shape[0] // 8, one, 0)


def index_kernel(devices, owner_ref, index_ref, slot_ref, turned_ref, total_ref):
    rows = owner_ref.shape[0]
    per_owner = index_ref.shape[0] // devices
    own = owner_ref[...]
    lane = iota((rows, lanes), 1)
    tri = jnp.where(
        iota((lanes, 2 * lanes), 1) >= lanes,
        1.0,
        jnp.where(iota((lanes, 2 * lanes), 0) < iota((lanes, 2 * lanes), 1), 1.0, 0.0),
    ).astype(bf16)

    def count(chunk, carry):
        prefix, total = carry
        masks = jnp.concatenate(
            [jnp.where(own == chunk * 8 + i, 1.0, 0.0) for i in range(8)], axis=0
        ).astype(bf16)
        sums = jnp.dot(masks, tri, preferred_element_type=f32)
        for i in range(8):
            o = chunk * 8 + i
            part = sums[i * rows : (i + 1) * rows]
            prefix = jnp.where(own == o, part[:, :lanes], prefix)
            total = jnp.where(lane == o, part[:, lanes:], total)
        return prefix, total

    zero = jnp.zeros((rows, lanes), f32)
    prefix, total = lax.fori_loop(0, devices // 8, count, (zero, zero))
    lower = jnp.where(iota((rows, rows), 1) < iota((rows, rows), 0), 1.0, 0.0).astype(bf16)
    above = jnp.dot(lower, total.astype(bf16), preferred_element_type=f32)
    offset = jnp.take_along_axis(above, own, axis=1, mode="promise_in_bounds")
    slot = own * (per_owner * lanes) + (prefix + offset).astype(jnp.int32)
    slot_ref[...] = slot

    turned_ref[...] = jnp.concatenate([slot & 127] * (lanes // rows), axis=0).T
    down = iota((lanes, lanes), 0)
    across = iota((lanes, lanes), 1)
    lane_code = across.astype(f32)
    total_ref[...] = jnp.zeros_like(total_ref)
    at_once = 8

    def spread(chunk, carry):
        left, right = [], []
        low = turned_ref[...]
        low = jnp.where(chunk > 0, pltpu.roll(low, lanes - chunk * at_once, 1), low)
        for i in range(at_once):
            j = chunk * at_once + i
            high = (slot_ref[pl.ds(j, 1), :] >> 7) == down
            row_code = (j + 1).astype(f32)
            left.append(
                jnp.concatenate(
                    [jnp.where(high, lane_code, 0.0), jnp.where(high, row_code, 0.0)], axis=0
                ).astype(bf16)
            )
            right.append(jnp.where(low[:, i : i + 1] == across, 1.0, 0.0).astype(bf16))
        total_ref[...] += jnp.dot(
            jnp.concatenate(left, axis=1),
            jnp.concatenate(right, axis=0),
            preferred_element_type=f32,
        )
        return carry

    lax.fori_loop(0, rows // at_once, spread, 0)
    blocks = index_ref.shape[0]
    index_ref[...] = (total_ref[0:blocks, :] + lanes * total_ref[blocks:, :]).astype(jnp.int32)


def send_kernel(index_ref, x_ref, after_ref, before_ref, out_ref):
    per_owner = out_ref.shape[1] // 3

    def store(owner, c, values):
        out_ref[owner, c * per_owner : (c + 1) * per_owner, :] = values

    fill_slots(index_ref, x_ref, per_owner, store)


def column(block, at):
    there = iota(block.shape, 1) == at
    return jnp.sum(jnp.where(there, block, 0.0), axis=1, keepdims=True)


def window(ref, at):
    return ref.at[:, pl.ds(pl.multiple_of((at >> 7) * lanes, lanes), lanes)]


def value(ref, at):
    return column(window(ref, at)[...], at & 127)


def my_place():
    return lax.axis_index("chain") * lax.axis_size("space") + lax.axis_index("space")


def loops_before(anchors_ref, mono_dev):
    me = my_place()
    found = []
    for e in range(anchors_ref.shape[1]):
        a = anchors_ref[0, e] - (me - 1) * mono_dev
        b = a + anchors_ref[1, e] - mono_dev
        wanted = jnp.logical_and(b >= 0, me > 0)
        found.append((jnp.where(wanted, a, 0), jnp.where(wanted, b, 0), wanted))
    return found


def chain_forces(left_ref, span_ref, anchors_ref, x_ref, ghost, wide_ref, force_ref):
    mono_dev = x_ref.shape[1]
    blocks = mono_dev // lanes
    extruders = left_ref.shape[0]
    count = lax.axis_size("chain") * lax.axis_size("space")
    me = my_place()
    wide_ref[...] = jnp.zeros_like(wide_ref)
    wide_ref[0:3, :] = x_ref[...]
    ghost = jnp.concatenate([ghost, jnp.zeros((5, lanes), f32)], axis=0)

    def ghost_at(k):
        return jnp.broadcast_to(ghost[:, k : k + 1], (8, lanes))

    lane = iota((8, lanes), 1)
    has_before = (me > 0).astype(f32)
    has_after = (me < count - 1).astype(f32)
    for j in range(blocks):
        here = wide_ref[:, j * lanes : (j + 1) * lanes]
        left = wide_ref[:, (j - 1) * lanes : j * lanes] if j > 0 else ghost_at(2 * extruders)
        right = wide_ref[:, (j + 1) * lanes : (j + 2) * lanes] if j < blocks - 1 else ghost_at(2 * extruders + 1)
        down = pltpu.roll(jnp.where(lane == lanes - 1, left, here), 1, 1) - here
        up = pltpu.roll(jnp.where(lane == 0, right, here), lanes - 1, 1) - here
        if j == 0:
            down = jnp.where(lane == 0, down * has_before, down)
        if j == blocks - 1:
            up = jnp.where(lane == lanes - 1, up * has_after, up)
        force_ref[:, j * lanes : (j + 1) * lanes] = bond_stiff * down + bond_stiff * up

    todo = []
    for e in range(extruders):
        a = left_ref[e] - me * mono_dev
        b = a + span_ref[e]
        b_here = jnp.minimum(b, mono_dev - 1)
        right = jnp.where(b < mono_dev, value(wide_ref, b_here), ghost[:, extruders + e : extruders + e + 1])
        pull = loop_stiff * (right - value(wide_ref, a))
        todo.append((a, pull))
        todo.append((b_here, jnp.where(b < mono_dev, -pull, 0.0)))
    for e, (a, b, wanted) in enumerate(loops_before(anchors_ref, mono_dev)):
        pull = loop_stiff * (value(wide_ref, b) - ghost[:, e : e + 1])
        todo.append((b, jnp.where(wanted, -pull, 0.0)))
    for at, pull in todo:
        spot = window(force_ref, at)
        spot[...] = spot[...] + jnp.where(lane == (at & 127), pull, 0.0)


def chain_step(step, x_ref, noise_ref, out_ref, force_ref):
    for c in range(3):
        out_ref[c : c + 1, :] = (
            x_ref[c : c + 1, :]
            + time_step * force_ref[c : c + 1, :]
            + noise_gain * noise_ref[c, step : step + 1, :]
        )


def first_kernel(
    left_ref,
    span_ref,
    anchors_ref,
    x_ref,
    after_ref,
    before_ref,
    noise_ref,
    index_ref,
    slot_ref,
    out_ref,
    y_ref,
    wide_ref,
    force_ref,
):
    mono_dev = x_ref.shape[1]
    extruders = left_ref.shape[0]
    per_owner = out_ref.shape[1] // 3
    me = my_place()
    lane = iota((3, lanes), 1)
    found = loops_before(anchors_ref, mono_dev)
    ghost = jnp.zeros((3, lanes), f32)
    for e in range(extruders):
        a, b, wanted = found[e]
        ghost = jnp.where(lane == e, column(window(before_ref, a)[0:3, :], a & 127), ghost)
        far_end = left_ref[e] - me * mono_dev + span_ref[e] - mono_dev
        ghost = jnp.where(lane == extruders + e, value(after_ref, jnp.maximum(far_end, 0)), ghost)
    ghost = jnp.where(lane == 2 * extruders, before_ref[0:3, mono_dev - 1 : mono_dev], ghost)
    ghost = jnp.where(lane == 2 * extruders + 1, after_ref[:, 0:1], ghost)
    chain_forces(left_ref, span_ref, anchors_ref, x_ref, ghost, wide_ref, force_ref)
    chain_step(0, x_ref, noise_ref, y_ref, force_ref)

    def store(owner, c, values):
        out_ref[owner, c * per_owner : (c + 1) * per_owner, :] = values

    fill_slots(index_ref, y_ref, per_owner, store)

    asked = [(left_ref[e] - me * mono_dev, True) for e in range(extruders)]
    asked += [(b, wanted) for _, b, wanted in found]
    asked += [(mono_dev - 1, True), (0, True)]
    lane = iota((1, lanes), 1)
    slots = jnp.full((1, lanes), -1.0, f32)
    for k, (at, wanted) in enumerate(asked):
        slot = column(slot_ref[pl.ds(at >> 7, 1), :].astype(f32), at & 127)
        slots = jnp.where(jnp.logical_and(lane == k, wanted), slot, slots)
    slots = slots.astype(jnp.int32)
    width = per_owner * lanes
    for o in range(out_ref.shape[0]):
        local_slot = slots - o * width
        here = jnp.logical_and(local_slot >= 0, local_slot < width)
        out_ref[o, 3 * per_owner : 3 * per_owner + 1, :] = jnp.where(here, local_slot + 1, 0).astype(f32)


def pieces(x):
    high = x.astype(bf16).astype(f32)
    middle = (x - high).astype(bf16).astype(f32)
    return high, middle, x - high - middle


def contact_kernel(
    rows_ref, cols_ref, below_ref, own_ref, above_ref, out_ref, far_t, far_x, near_t, stage, cap, total
):
    devices = out_ref.shape[0]
    per_owner = out_ref.shape[1] // 3
    blocks = devices * per_owner
    owners = 8 // per_owner
    scale = 1.0 / math.sqrt(cutoff_sq)
    place = lax.axis_index("space")
    has_below = place > 0
    has_above = place < lax.axis_size("space") - 1
    cap[0:lanes, :] = jnp.full((lanes, lanes), 1e30, f32)
    cap[lanes:, :] = jnp.where(iota((lanes, lanes), 0) == iota((lanes, lanes), 1), 0.0, 1e30)
    stage[...] = jnp.zeros_like(stage)
    total[...] = jnp.zeros_like(total)

    def eight(ref, group, c):
        return ref[c, pl.ds(pl.multiple_of(group * 8, 8), 8), :]

    def build(group, carry):
        sides = ((below_ref, has_below), (own_ref, None), (above_ref, has_above))
        for side, (ref, valid) in enumerate(sides):
            xs = [eight(ref, group, c) for c in range(3)]
            live = xs[0] < 0.5 * far_away
            if valid is not None:
                live = jnp.logical_and(live, jnp.full((8, lanes), valid.astype(jnp.int32)) > 0)
            xs = [jnp.where(live, x, 0.0) * scale for x in xs]
            square = xs[0] * xs[0] + xs[1] * xs[1] + xs[2] * xs[2]
            high, middle, low = [list(part) for part in zip(*[pieces(x) for x in xs])]
            one = [jnp.ones((8, lanes), f32)] * 3
            spot = stage.at[side]
            far = high + middle + high + list(pieces(jnp.where(live, -square, -1e9))) + one
            for f, v in enumerate(far):
                spot[pl.ds(f, 8, stride=16), :] = v
            at = pl.ds(pl.multiple_of((side * blocks + group * 8) * 16, lanes), lanes)
            far_t[at, :] = spot[...].astype(bf16).T
            for f in range(3):
                spot[pl.ds(6 + f, 8, stride=16), :] = low[f]
            far_x[at, :] = spot[...].astype(bf16)
            if side == 1:
                spot = stage.at[3]
                near = [2.0 * v for v in high + high + middle] + one
                near += list(pieces(jnp.where(live, 1.0 - square, -1e9)))
                for f, v in enumerate(near):
                    spot[pl.ds(f, 8, stride=16), :] = v
                near_t[pl.ds(pl.multiple_of(group * lanes, lanes), lanes), :] = spot[...].astype(bf16)
        return carry

    lax.fori_loop(0, blocks // 8, build, 0)
    zero = jnp.zeros((lanes, lanes), bf16)

    def sixteen(ref, block):
        return ref[pl.ds(pl.multiple_of(block * 16, 16), 16), :]

    pairs = min(pairs_at_once, rows_ref.shape[0] // 2)

    def tiles(step, carry):
        results = []
        for pair in range(pairs):
            first = (step * pairs + pair) * 2
            ids = [(rows_ref[first + i], cols_ref[first + i]) for i in range(2)]
            left, right = [], []
            for r, q in ids:
                near = sixteen(near_t, r)
                right.append(
                    jnp.concatenate(
                        [jnp.where((q & 7) == k, near, jnp.zeros_like(near)) for k in range(8)], axis=0
                    )
                )
                left.append(far_t[pl.ds(pl.multiple_of((q >> 3) * lanes, lanes), lanes), :])
            right = jnp.concatenate(
                [jnp.concatenate([right[0], zero], axis=1), jnp.concatenate([zero, right[1]], axis=1)],
                axis=0,
            )
            reach = jnp.dot(jnp.concatenate(left, axis=1), right, preferred_element_type=f32)
            for i, (r, q) in enumerate(ids):
                same = (q == r + blocks).astype(jnp.int32)
                most = cap[pl.ds(pl.multiple_of(same * lanes, lanes), lanes), :]
                w = jnp.maximum(jnp.minimum(reach[:, i * lanes : (i + 1) * lanes], most), 0.0).astype(bf16)
                results.append((r, jnp.dot(sixteen(far_x, q), w, preferred_element_type=f32)))
        for r, v in results:
            spot = total.at[pl.ds(pl.multiple_of(r * 16, 16), 16), :]
            spot[...] = spot[...] + v
        return carry

    lax.fori_loop(0, rows_ref.shape[0] // (2 * pairs), tiles, 0)
    back = contact_coef * math.sqrt(cutoff_sq)

    def finish(group, carry):
        sums = [total[pl.ds(group * lanes + f, 8, stride=16), :] for f in range(13)]
        for c in range(3):
            place = eight(own_ref, group, c)
            here = jnp.where(place < 0.5 * far_away, place, 0.0) * scale
            force = (here * sums[12] - (sums[c] + sums[3 + c] + sums[6 + c])) * back
            for i in range(owners):
                out_ref[group * owners + i, c * per_owner : (c + 1) * per_owner, :] = force[
                    i * per_owner : (i + 1) * per_owner
                ]
        return carry

    lax.fori_loop(0, blocks // 8, finish, 0)


def take_slots(slot_ref, source_ref, per_owner, emit):
    def one(group, carry):
        slot = slot_ref[pl.ds(pl.multiple_of(group * 8, 8), 8), :]
        row_of = slot >> 7
        lane_of = slot & 127
        held = [jnp.zeros((8, lanes), f32) for _ in range(3)]
        for s in range(source_ref.shape[0] * per_owner):
            here = row_of == s
            for c in range(3):
                at = c * per_owner + s % per_owner
                row = source_ref[s // per_owner, at : at + 1, :]
                held[c] = jnp.where(here, pick(row, lane_of), held[c])
        for i in range(8):
            at = pl.ds(pl.multiple_of((group * 8 + i) * lanes, lanes), lanes)
            for c in range(3):
                emit(c, at, held[c][i : i + 1, :])
        return carry

    lax.fori_loop(0, slot_ref.shape[0] // 8, one, 0)


def second_kernel(
    per_owner, left_ref, span_ref, anchors_ref, slot_ref, back_ref, noise_ref, out_ref, x_ref, wide_ref, force_ref
):
    def emit(c, at, values):
        x_ref[c : c + 1, at] = values

    take_slots(slot_ref, back_ref, per_owner, emit)
    ghost = [jnp.zeros((1, lanes), f32) for _ in range(3)]
    for o in range(back_ref.shape[0]):
        for c in range(3):
            at = 3 * per_owner + c
            ghost[c] = ghost[c] + back_ref[o, at : at + 1, :]
    ghost = jnp.concatenate(ghost, axis=0)
    chain_forces(left_ref, span_ref, anchors_ref, x_ref, ghost, wide_ref, force_ref)
    chain_step(1, x_ref, noise_ref, out_ref, force_ref)


def last_kernel(slot_ref, back_ref, base_ref, out_ref):
    def emit(c, at, values):
        out_ref[c : c + 1, at] = base_ref[c : c + 1, at] + time_step * values

    take_slots(slot_ref, back_ref, back_ref.shape[1] // 3, emit)


def turn_kernel(cells_ref, later_ref, out_ref):
    per_owner = cells_ref.shape[1] // 3
    for o in range(cells_ref.shape[0]):
        for c in range(3):
            out_ref[c, o * per_owner : (o + 1) * per_owner, :] = cells_ref[
                o, c * per_owner : (c + 1) * per_owner, :
            ]


def advance_kernel(extruders, y_ref, force_ref, plain_ref, turned_ref, answer_ref):
    devices = y_ref.shape[0]
    per_owner = force_ref.shape[1] // 3
    for o in range(devices):
        for c in range(3):
            at = slice(c * per_owner, (c + 1) * per_owner)
            result = y_ref[o, at, :] + time_step * force_ref[o, at, :]
            plain_ref[o, at, :] = result
            turned_ref[c, o * per_owner : (o + 1) * per_owner, :] = result
    answer_ref[...] = jnp.zeros_like(answer_ref)
    row = 3 * per_owner
    for group in range(devices // 8):
        asked = jnp.concatenate([y_ref[group * 8 + i, row : row + 1, :] for i in range(8)], axis=0)
        asked = asked.astype(jnp.int32) - 1
        row_of = asked >> 7
        lane_of = asked & 127
        for c in range(3):
            held = jnp.zeros((8, lanes), f32)
            for k in range(per_owner):
                source = turned_ref[c, pl.ds(group * 8 * per_owner + k, 8, stride=per_owner), :]
                picked = jnp.take_along_axis(source, lane_of, axis=1, mode="promise_in_bounds")
                held = jnp.where(row_of == k, picked, held)
            answer_ref[c, 8 + group * 8 : 16 + group * 8, :] = held
    lane = iota((1, lanes), 1)
    from_before = jnp.logical_or(lane < extruders, lane == 2 * extruders)
    for d in range(devices):
        for c in range(3):
            plain_ref[d, row + c : row + c + 1, :] = jnp.where(
                from_before, answer_ref[c, 7 + d : 8 + d, :], answer_ref[c, 9 + d : 10 + d, :]
            )


def shifted(value, axis, steps):
    count = lax.axis_size(axis)
    first, last = (max(0, -steps), min(count, count - steps))
    return lax.ppermute(value, axis, [(source, source + steps) for source in range(first, last)])


def local(positions, noise, cell_owner, tile_rows, tile_cols, loop_left, loop_span):
    devices = lax.axis_size(both)
    mono_dev = positions.shape[1]
    per_owner = 2 * mono_dev // devices // lanes
    rows = mono_dev // lanes
    blocks = devices * per_owner
    noise_t = noise.transpose(1, 0, 2)

    sent = jax.ShapeDtypeStruct((devices, 3 * per_owner, lanes), f32)
    chain = jax.ShapeDtypeStruct((3, mono_dev), f32)
    chain_scratch = [
        pltpu.VMEM((3, mono_dev), f32),
        pltpu.VMEM((8, mono_dev), f32),
        pltpu.VMEM((8, mono_dev), f32),
    ]

    def exchange(value):
        return lax.all_to_all(value, both, split_axis=0, concat_axis=0, tiled=True)

    def contact(cells):
        below = shifted(cells, "space", 1)
        above = shifted(cells, "space", -1)
        return call(
            contact_kernel,
            sent,
            [smem, smem] + [vmem] * 3,
            (tile_rows, tile_cols, below, cells, above),
            [
                pltpu.VMEM((3 * blocks * 16, lanes), bf16),
                pltpu.VMEM((3 * blocks * 16, lanes), bf16),
                pltpu.VMEM((blocks * 16, lanes), bf16),
                pltpu.VMEM((4, lanes, lanes), f32),
                pltpu.VMEM((2 * lanes, lanes), f32),
                pltpu.VMEM((blocks * 16, lanes), f32),
            ],
            micros=14,
        )

    extruders = loop_left.shape[0]
    anchors = jnp.concatenate([loop_left, loop_span]).astype(f32)
    anchors = jnp.pad(anchors, (0, mono_dev - 2 * extruders))
    before = shifted(jnp.concatenate([positions, anchors[None]], axis=0), both, 1)
    after = shifted(positions[:, :longest_loop], both, -1)
    index, slot = call(
        functools.partial(index_kernel, devices),
        [
            jax.ShapeDtypeStruct((blocks, lanes), jnp.int32),
            jax.ShapeDtypeStruct((rows, lanes), jnp.int32),
        ],
        [vmem],
        (cell_owner.reshape(rows, lanes),),
        [pltpu.VMEM((lanes, lanes), jnp.int32), pltpu.VMEM((2 * blocks, lanes), f32)],
        micros=6,
    )
    x_out = call(
        send_kernel,
        sent,
        [vmem] * 4,
        (index, positions, after, before),
        micros=4,
    )
    anchors_before = before[3, : 2 * extruders].astype(jnp.int32).reshape(2, extruders)
    x_cells = exchange(x_out)
    y_out = call(
        first_kernel,
        jax.ShapeDtypeStruct((devices, 3 * per_owner + 1, lanes), f32),
        [smem] * 3 + [vmem] * 6,
        (loop_left, loop_span, anchors_before, positions, after, before, noise_t, index, slot),
        chain_scratch,
        micros=6,
    )
    y_cells = exchange(y_out)
    turned = jax.ShapeDtypeStruct((3, blocks, lanes), f32)
    hbm = pl.BlockSpec(memory_space=pl.ANY)
    contact0 = contact(call(turn_kernel, turned, [vmem, hbm], (x_cells, y_out)))
    x1_cells, x1_turned = call(
        functools.partial(advance_kernel, extruders),
        [jax.ShapeDtypeStruct((devices, 3 * per_owner + 3, lanes), f32), turned],
        [vmem] * 2,
        (y_cells, contact0),
        [pltpu.VMEM((3, devices + 16, lanes), f32)],
    )
    x1_back = exchange(x1_cells)
    contact1 = contact(x1_turned)
    back1 = exchange(contact1)
    z = call(
        functools.partial(second_kernel, per_owner),
        chain,
        [smem] * 3 + [vmem] * 3,
        (loop_left, loop_span, anchors_before, slot, x1_back, noise_t),
        chain_scratch,
        micros=6,
    )
    return call(last_kernel, chain, [vmem] * 3, (slot, back1, z), micros=4)


def solution(mesh):
    in_specs = (
        P(None, ("chain", "space")),
        P(None, None, ("chain", "space")),
        P(("chain", "space"), None),
        P(("chain", "space")),
        P(("chain", "space")),
        P(("chain", "space")),
        P(("chain", "space")),
    )
    out_specs = P(None, ("chain", "space"))
    return jax.shard_map(local, mesh=mesh, in_specs=in_specs, out_specs=out_specs, check_vma=False)
```

```python
import functools
import math

import jax
import jax.numpy as jnp
from jax import lax
from jax.experimental import pallas as pl
from jax.experimental.pallas import tpu as pltpu
from jax.sharding import PartitionSpec as P

time_step = 0.05
bond_stiff = 1.0
loop_stiff = 2.0
cutoff_sq = 2.25
contact_coef = 0.4 / 2.25
noise_gain = math.sqrt(0.1)
lanes = 128
far_away = 1e15
pairs_at_once = 128

vmem = pl.BlockSpec(memory_space=pltpu.VMEM)
smem = pl.BlockSpec(memory_space=pltpu.SMEM)
both = ("chain", "space")
f32 = jnp.float32
bf16 = jnp.bfloat16


def call(body, outs, in_specs, args, scratch=(), micros=1):
    many = isinstance(outs, list)
    return pl.pallas_call(
        body,
        out_shape=outs,
        in_specs=in_specs,
        out_specs=[vmem] * len(outs) if many else vmem,
        scratch_shapes=list(scratch),
        compiler_params=pltpu.CompilerParams(vmem_limit_bytes=32 * 1024 * 1024),
        cost_estimate=pl.CostEstimate(
            flops=int(micros * 1e9), bytes_accessed=1_000_000, transcendentals=0
        ),
    )(*args)


def iota(shape, dim):
    return lax.broadcasted_iota(jnp.int32, shape, dim)


def pick(row, where_to):
    return jnp.take_along_axis(
        jnp.broadcast_to(row, where_to.shape), where_to, axis=1, mode="promise_in_bounds"
    )


def fill_slots(index_ref, ranges_ref, source_ref, out_ref, per_owner):
    fields = source_ref.shape[0]
    at_once = 16

    def one(group, carry):
        first_owner = lax.div(group, per_owner) * 8
        k = lax.rem(group, per_owner)
        code = index_ref[pl.ds(first_owner * per_owner + k, 8, stride=per_owner), :]
        row_of = (code >> 7) - 1
        lane_of = code & 127
        least = -ranges_ref[k, first_owner]
        end = ranges_ref[per_owner + k, first_owner]

        def search(chunk, held):
            held = list(held)
            for i in range(at_once):
                j = chunk * at_once + i
                here = row_of == j
                at = pl.ds(pl.multiple_of(j * lanes, lanes), lanes)
                for c in range(fields):
                    held[c] = jnp.where(here, pick(source_ref[c : c + 1, at], lane_of), held[c])
            return tuple(held)

        empty = tuple(jnp.full((8, lanes), far_away, f32) for _ in range(fields))
        chunks = (lax.div(least, at_once), lax.div(end + at_once - 1, at_once))
        held = lax.fori_loop(*chunks, search, empty)
        for i in range(8):
            for c in range(fields):
                out_ref[first_owner + i, pl.ds(c * per_owner + k, 1), :] = held[c][i : i + 1, :]
        return carry

    lax.fori_loop(0, index_ref.shape[0] // 8, one, 0)


def index_kernel(devices, owner_ref, index_ref, slot_ref, ranges_ref, turned_ref, total_ref):
    rows = owner_ref.shape[0]
    per_owner = index_ref.shape[0] // devices
    own = owner_ref[...]
    lane = iota((rows, lanes), 1)
    tri = jnp.where(
        iota((lanes, 2 * lanes), 1) >= lanes,
        1.0,
        jnp.where(iota((lanes, 2 * lanes), 0) < iota((lanes, 2 * lanes), 1), 1.0, 0.0),
    ).astype(bf16)

    def count(chunk, carry):
        prefix, total = carry
        masks = jnp.concatenate(
            [jnp.where(own == chunk * 8 + i, 1.0, 0.0) for i in range(8)], axis=0
        ).astype(bf16)
        sums = jnp.dot(masks, tri, preferred_element_type=f32)
        for i in range(8):
            o = chunk * 8 + i
            part = sums[i * rows : (i + 1) * rows]
            prefix = jnp.where(own == o, part[:, :lanes], prefix)
            total = jnp.where(lane == o, part[:, lanes:], total)
        return prefix, total

    zero = jnp.zeros((rows, lanes), f32)
    prefix, total = lax.fori_loop(0, devices // 8, count, (zero, zero))
    lower = jnp.where(iota((rows, rows), 1) < iota((rows, rows), 0), 1.0, 0.0).astype(bf16)
    above = jnp.dot(lower, total.astype(bf16), preferred_element_type=f32)
    offset = jnp.take_along_axis(above, own, axis=1, mode="promise_in_bounds")
    slot = own * (per_owner * lanes) + (prefix + offset).astype(jnp.int32)
    slot_ref[...] = slot

    upto = above + total
    count_of = upto[rows - 1 : rows]
    least, end = [], []
    for k in range(per_owner):
        some = count_of > k * lanes
        first_row = jnp.sum(jnp.where(upto <= k * lanes, 1.0, 0.0), axis=0, keepdims=True)
        limit = jnp.minimum(count_of, (k + 1.0) * lanes)
        last_row = jnp.sum(jnp.where(above < limit, 1.0, 0.0), axis=0, keepdims=True)
        least.append(jnp.where(some, -first_row, -float(rows)))
        end.append(jnp.where(some, last_row, 0.0))
    spans = jnp.concatenate(least + end + [jnp.zeros((1, lanes), f32)] * (8 - 2 * per_owner), axis=0)
    for shift in (1, 2, 4):
        spans = jnp.maximum(spans, pltpu.roll(spans, lanes - shift, 1))
    ranges_ref[0:8, :] = spans.astype(jnp.int32)
    total_ref[0:rows, :] = above
    total_ref[rows : 2 * rows, :] = upto
    lowest = total_ref[pl.ds(0, 8, stride=8), :].astype(jnp.int32) >> 7
    lowest = jnp.minimum(lowest, per_owner - 1)
    highest = total_ref[pl.ds(rows + 7, 8, stride=8), :].astype(jnp.int32)
    highest = jnp.maximum(highest - 1, 0) >> 7
    more = jnp.max((highest - lowest).astype(f32), axis=1, keepdims=True)
    ranges_ref[8:16, :] = lowest
    ranges_ref[16:24, :] = jnp.broadcast_to(more, (8, lanes)).astype(jnp.int32)

    turned_ref[...] = jnp.concatenate([slot & 127] * (lanes // rows), axis=0).T
    down = iota((lanes, lanes), 0)
    across = iota((lanes, lanes), 1)
    lane_code = across.astype(f32)
    total_ref[...] = jnp.zeros_like(total_ref)
    at_once = 8

    def spread(chunk, carry):
        left, right = [], []
        low = turned_ref[...]
        low = jnp.where(chunk > 0, pltpu.roll(low, lanes - chunk * at_once, 1), low)
        for i in range(at_once):
            j = chunk * at_once + i
            high = (slot_ref[pl.ds(j, 1), :] >> 7) == down
            row_code = (j + 1).astype(f32)
            left.append(
                jnp.concatenate(
                    [jnp.where(high, lane_code, 0.0), jnp.where(high, row_code, 0.0)], axis=0
                ).astype(bf16)
            )
            right.append(jnp.where(low[:, i : i + 1] == across, 1.0, 0.0).astype(bf16))
        total_ref[...] += jnp.dot(
            jnp.concatenate(left, axis=1),
            jnp.concatenate(right, axis=0),
            preferred_element_type=f32,
        )
        return carry

    lax.fori_loop(0, rows // at_once, spread, 0)
    blocks = index_ref.shape[0]
    index_ref[...] = (total_ref[0:blocks, :] + lanes * total_ref[blocks:, :]).astype(jnp.int32)


def send_kernel(ranges_ref, index_ref, x_ref, after_ref, before_ref, out_ref):
    fill_slots(index_ref, ranges_ref, x_ref, out_ref, out_ref.shape[1] // 3)


def column(block, at):
    there = iota(block.shape, 1) == at
    return jnp.sum(jnp.where(there, block, 0.0), axis=1, keepdims=True)


def window(ref, at):
    return ref.at[:, pl.ds(pl.multiple_of((at >> 7) * lanes, lanes), lanes)]


def value(ref, at):
    return column(window(ref, at)[...], at & 127)


def my_place():
    return lax.axis_index("chain") * lax.axis_size("space") + lax.axis_index("space")


def loops_before(anchors_ref, mono_dev):
    me = my_place()
    found = []
    for e in range(anchors_ref.shape[1]):
        a = anchors_ref[0, e] - (me - 1) * mono_dev
        b = a + anchors_ref[1, e] - mono_dev
        wanted = jnp.logical_and(b >= 0, me > 0)
        found.append((jnp.where(wanted, a, 0), jnp.where(wanted, b, 0), wanted))
    return found


def chain_forces(left_ref, span_ref, anchors_ref, x_ref, ghost, wide_ref, force_ref):
    mono_dev = x_ref.shape[1]
    blocks = mono_dev // lanes
    extruders = left_ref.shape[0]
    count = lax.axis_size("chain") * lax.axis_size("space")
    me = my_place()
    wide_ref[...] = jnp.zeros_like(wide_ref)
    wide_ref[0:3, :] = x_ref[...]
    ghost = jnp.concatenate([ghost, jnp.zeros((5, lanes), f32)], axis=0)

    def ghost_at(k):
        return jnp.broadcast_to(ghost[:, k : k + 1], (8, lanes))

    lane = iota((8, lanes), 1)
    has_before = (me > 0).astype(f32)
    has_after = (me < count - 1).astype(f32)
    for j in range(blocks):
        here = wide_ref[:, j * lanes : (j + 1) * lanes]
        left = wide_ref[:, (j - 1) * lanes : j * lanes] if j > 0 else ghost_at(2 * extruders)
        right = wide_ref[:, (j + 1) * lanes : (j + 2) * lanes] if j < blocks - 1 else ghost_at(2 * extruders + 1)
        down = pltpu.roll(jnp.where(lane == lanes - 1, left, here), 1, 1) - here
        up = pltpu.roll(jnp.where(lane == 0, right, here), lanes - 1, 1) - here
        if j == 0:
            down = jnp.where(lane == 0, down * has_before, down)
        if j == blocks - 1:
            up = jnp.where(lane == lanes - 1, up * has_after, up)
        force_ref[:, j * lanes : (j + 1) * lanes] = bond_stiff * down + bond_stiff * up

    todo = []
    for e in range(extruders):
        a = left_ref[e] - me * mono_dev
        b = a + span_ref[e]
        b_here = jnp.minimum(b, mono_dev - 1)
        right = jnp.where(b < mono_dev, value(wide_ref, b_here), ghost[:, extruders + e : extruders + e + 1])
        pull = loop_stiff * (right - value(wide_ref, a))
        todo.append((a, pull))
        todo.append((b_here, jnp.where(b < mono_dev, -pull, 0.0)))
    for e, (a, b, wanted) in enumerate(loops_before(anchors_ref, mono_dev)):
        pull = loop_stiff * (value(wide_ref, b) - ghost[:, e : e + 1])
        todo.append((b, jnp.where(wanted, -pull, 0.0)))
    for at, pull in todo:
        spot = window(force_ref, at)
        spot[...] = spot[...] + jnp.where(lane == (at & 127), pull, 0.0)


def chain_step(step, x_ref, noise_ref, out_ref, force_ref):
    for c in range(3):
        out_ref[c : c + 1, :] = (
            x_ref[c : c + 1, :]
            + time_step * force_ref[c : c + 1, :]
            + noise_gain * noise_ref[c, step : step + 1, :]
        )


def first_kernel(
    left_ref,
    span_ref,
    anchors_ref,
    ranges_ref,
    x_ref,
    after_ref,
    before_ref,
    noise_ref,
    index_ref,
    slot_ref,
    out_ref,
    y_ref,
    wide_ref,
    force_ref,
):
    mono_dev = x_ref.shape[1]
    extruders = left_ref.shape[0]
    per_owner = out_ref.shape[1] // 3
    me = my_place()
    lane = iota((3, lanes), 1)
    found = loops_before(anchors_ref, mono_dev)
    ghost = jnp.zeros((3, lanes), f32)
    for e in range(extruders):
        a, b, wanted = found[e]
        ghost = jnp.where(lane == e, column(window(before_ref, a)[0:3, :], a & 127), ghost)
        far_end = left_ref[e] - me * mono_dev + span_ref[e] - mono_dev
        ghost = jnp.where(lane == extruders + e, value(after_ref, jnp.maximum(far_end, 0)), ghost)
    ghost = jnp.where(lane == 2 * extruders, before_ref[0:3, mono_dev - 1 : mono_dev], ghost)
    ghost = jnp.where(lane == 2 * extruders + 1, after_ref[:, 0:1], ghost)
    chain_forces(left_ref, span_ref, anchors_ref, x_ref, ghost, wide_ref, force_ref)
    chain_step(0, x_ref, noise_ref, y_ref, force_ref)

    fill_slots(index_ref, ranges_ref, y_ref, out_ref, per_owner)

    asked = [(left_ref[e] - me * mono_dev, True) for e in range(extruders)]
    asked += [(b, wanted) for _, b, wanted in found]
    asked += [(mono_dev - 1, True), (0, True)]
    lane = iota((1, lanes), 1)
    slots = jnp.full((1, lanes), -1.0, f32)
    for k, (at, wanted) in enumerate(asked):
        slot = column(slot_ref[pl.ds(at >> 7, 1), :].astype(f32), at & 127)
        slots = jnp.where(jnp.logical_and(lane == k, wanted), slot, slots)
    slots = slots.astype(jnp.int32)
    width = per_owner * lanes
    for o in range(out_ref.shape[0]):
        local_slot = slots - o * width
        here = jnp.logical_and(local_slot >= 0, local_slot < width)
        out_ref[o, 3 * per_owner : 3 * per_owner + 1, :] = jnp.where(here, local_slot + 1, 0).astype(f32)


def pieces(x):
    high = x.astype(bf16).astype(f32)
    middle = (x - high).astype(bf16).astype(f32)
    return high, middle, x - high - middle


def contact_kernel(
    rows_ref, cols_ref, below_ref, own_ref, above_ref, out_ref, far_t, far_x, near_t, stage, cap, total
):
    devices = out_ref.shape[0]
    per_owner = out_ref.shape[1] // 3
    blocks = devices * per_owner
    owners = 8 // per_owner
    scale = 1.0 / math.sqrt(cutoff_sq)
    place = lax.axis_index("space")
    has_below = place > 0
    has_above = place < lax.axis_size("space") - 1
    cap[0:lanes, :] = jnp.full((lanes, lanes), 1e30, f32)
    cap[lanes:, :] = jnp.where(iota((lanes, lanes), 0) == iota((lanes, lanes), 1), 0.0, 1e30)
    stage[...] = jnp.zeros_like(stage)
    total[...] = jnp.zeros_like(total)

    def eight(ref, group, c):
        return ref[c, pl.ds(pl.multiple_of(group * 8, 8), 8), :]

    def build(group, carry):
        sides = ((below_ref, has_below), (own_ref, None), (above_ref, has_above))
        for side, (ref, valid) in enumerate(sides):
            xs = [eight(ref, group, c) for c in range(3)]
            live = xs[0] < 0.5 * far_away
            if valid is not None:
                live = jnp.logical_and(live, jnp.full((8, lanes), valid.astype(jnp.int32)) > 0)
            xs = [jnp.where(live, x, 0.0) * scale for x in xs]
            square = xs[0] * xs[0] + xs[1] * xs[1] + xs[2] * xs[2]
            high, middle, low = [list(part) for part in zip(*[pieces(x) for x in xs])]
            one = [jnp.ones((8, lanes), f32)] * 3
            spot = stage.at[side]
            far = high + middle + high + list(pieces(jnp.where(live, -square, -1e9))) + one
            for f, v in enumerate(far):
                spot[pl.ds(f, 8, stride=16), :] = v
            at = pl.ds(pl.multiple_of((side * blocks + group * 8) * 16, lanes), lanes)
            far_t[at, :] = spot[...].astype(bf16).T
            for f in range(3):
                spot[pl.ds(6 + f, 8, stride=16), :] = low[f]
            far_x[at, :] = spot[...].astype(bf16)
            if side == 1:
                spot = stage.at[3]
                near = [2.0 * v for v in high + high + middle] + one
                near += list(pieces(jnp.where(live, 1.0 - square, -1e9)))
                for f, v in enumerate(near):
                    spot[pl.ds(f, 8, stride=16), :] = v
                near_t[pl.ds(pl.multiple_of(group * lanes, lanes), lanes), :] = spot[...].astype(bf16)
        return carry

    lax.fori_loop(0, blocks // 8, build, 0)
    zero = jnp.zeros((lanes, lanes), bf16)

    def sixteen(ref, block):
        return ref[pl.ds(pl.multiple_of(block * 16, 16), 16), :]

    pairs = min(pairs_at_once, rows_ref.shape[0] // 2)

    def tiles(step, carry):
        results = []
        for pair in range(pairs):
            first = (step * pairs + pair) * 2
            ids = [(rows_ref[first + i], cols_ref[first + i]) for i in range(2)]
            left, right = [], []
            for r, q in ids:
                near = sixteen(near_t, r)
                right.append(
                    jnp.concatenate(
                        [jnp.where((q & 7) == k, near, jnp.zeros_like(near)) for k in range(8)], axis=0
                    )
                )
                left.append(far_t[pl.ds(pl.multiple_of((q >> 3) * lanes, lanes), lanes), :])
            right = jnp.concatenate(
                [jnp.concatenate([right[0], zero], axis=1), jnp.concatenate([zero, right[1]], axis=1)],
                axis=0,
            )
            reach = jnp.dot(jnp.concatenate(left, axis=1), right, preferred_element_type=f32)
            for i, (r, q) in enumerate(ids):
                same = (q == r + blocks).astype(jnp.int32)
                most = cap[pl.ds(pl.multiple_of(same * lanes, lanes), lanes), :]
                w = jnp.maximum(jnp.minimum(reach[:, i * lanes : (i + 1) * lanes], most), 0.0).astype(bf16)
                results.append((r, jnp.dot(sixteen(far_x, q), w, preferred_element_type=f32)))
        for r, v in results:
            spot = total.at[pl.ds(pl.multiple_of(r * 16, 16), 16), :]
            spot[...] = spot[...] + v
        return carry

    lax.fori_loop(0, rows_ref.shape[0] // (2 * pairs), tiles, 0)
    back = contact_coef * math.sqrt(cutoff_sq)

    def finish(group, carry):
        sums = [total[pl.ds(group * lanes + f, 8, stride=16), :] for f in range(13)]
        for c in range(3):
            place = eight(own_ref, group, c)
            here = jnp.where(place < 0.5 * far_away, place, 0.0) * scale
            force = (here * sums[12] - (sums[c] + sums[3 + c] + sums[6 + c])) * back
            for i in range(owners):
                out_ref[group * owners + i, c * per_owner : (c + 1) * per_owner, :] = force[
                    i * per_owner : (i + 1) * per_owner
                ]
        return carry

    lax.fori_loop(0, blocks // 8, finish, 0)


def take_slots(slot_ref, ranges_ref, source_ref, per_owner, emit):
    owners = source_ref.shape[0]

    def one(group, carry):
        slot = slot_ref[pl.ds(pl.multiple_of(group * 8, 8), 8), :]
        row_of = slot >> 7
        lane_of = slot & 127

        def search(tries, first):
            held = [jnp.zeros((8, lanes), f32) for _ in range(3)]
            for o in range(owners):
                base = first(o)
                for t in range(tries):
                    k = jnp.minimum(base + t, per_owner - 1)
                    here = row_of == o * per_owner + k
                    for c in range(3):
                        row = source_ref[o, pl.ds(c * per_owner + k, 1), :]
                        held[c] = jnp.where(here, pick(row, lane_of), held[c])
            for i in range(8):
                at = pl.ds(pl.multiple_of((group * 8 + i) * lanes, lanes), lanes)
                for c in range(3):
                    emit(c, at, held[c][i : i + 1, :])

        if per_owner <= 2:
            search(per_owner, lambda o: 0)
        else:
            few = ranges_ref[16 + group, 0] <= 1

            @pl.when(few)
            def _():
                search(2, lambda o: ranges_ref[8 + group, o])

            @pl.when(jnp.logical_not(few))
            def _():
                search(per_owner, lambda o: 0)

        return carry

    lax.fori_loop(0, slot_ref.shape[0] // 8, one, 0)


def second_kernel(
    per_owner,
    left_ref,
    span_ref,
    anchors_ref,
    ranges_ref,
    slot_ref,
    back_ref,
    noise_ref,
    out_ref,
    x_ref,
    wide_ref,
    force_ref,
):
    def emit(c, at, values):
        x_ref[c : c + 1, at] = values

    take_slots(slot_ref, ranges_ref, back_ref, per_owner, emit)
    ghost = [jnp.zeros((1, lanes), f32) for _ in range(3)]
    for o in range(back_ref.shape[0]):
        for c in range(3):
            at = 3 * per_owner + c
            ghost[c] = ghost[c] + back_ref[o, at : at + 1, :]
    ghost = jnp.concatenate(ghost, axis=0)
    chain_forces(left_ref, span_ref, anchors_ref, x_ref, ghost, wide_ref, force_ref)
    chain_step(1, x_ref, noise_ref, out_ref, force_ref)


def last_kernel(ranges_ref, slot_ref, back_ref, base_ref, out_ref):
    def emit(c, at, values):
        out_ref[c : c + 1, at] = base_ref[c : c + 1, at] + time_step * values

    take_slots(slot_ref, ranges_ref, back_ref, back_ref.shape[1] // 3, emit)


def turn_kernel(cells_ref, later_ref, out_ref):
    per_owner = cells_ref.shape[1] // 3
    for o in range(cells_ref.shape[0]):
        for c in range(3):
            out_ref[c, o * per_owner : (o + 1) * per_owner, :] = cells_ref[
                o, c * per_owner : (c + 1) * per_owner, :
            ]


def advance_kernel(extruders, y_ref, force_ref, plain_ref, turned_ref, answer_ref):
    devices = y_ref.shape[0]
    per_owner = force_ref.shape[1] // 3
    for o in range(devices):
        for c in range(3):
            at = slice(c * per_owner, (c + 1) * per_owner)
            result = y_ref[o, at, :] + time_step * force_ref[o, at, :]
            plain_ref[o, at, :] = result
            turned_ref[c, o * per_owner : (o + 1) * per_owner, :] = result
    answer_ref[...] = jnp.zeros_like(answer_ref)
    row = 3 * per_owner
    for group in range(devices // 8):
        asked = jnp.concatenate([y_ref[group * 8 + i, row : row + 1, :] for i in range(8)], axis=0)
        asked = asked.astype(jnp.int32) - 1
        row_of = asked >> 7
        lane_of = asked & 127
        for c in range(3):
            held = jnp.zeros((8, lanes), f32)
            for k in range(per_owner):
                source = turned_ref[c, pl.ds(group * 8 * per_owner + k, 8, stride=per_owner), :]
                picked = jnp.take_along_axis(source, lane_of, axis=1, mode="promise_in_bounds")
                held = jnp.where(row_of == k, picked, held)
            answer_ref[c, 8 + group * 8 : 16 + group * 8, :] = held
    lane = iota((1, lanes), 1)
    from_before = jnp.logical_or(lane < extruders, lane == 2 * extruders)
    for d in range(devices):
        for c in range(3):
            plain_ref[d, row + c : row + c + 1, :] = jnp.where(
                from_before, answer_ref[c, 7 + d : 8 + d, :], answer_ref[c, 9 + d : 10 + d, :]
            )


def shifted(value, axis, steps):
    count = lax.axis_size(axis)
    first, last = (max(0, -steps), min(count, count - steps))
    return lax.ppermute(value, axis, [(source, source + steps) for source in range(first, last)])


def local(positions, noise, cell_owner, tile_rows, tile_cols, loop_left, loop_span):
    devices = lax.axis_size(both)
    mono_dev = positions.shape[1]
    per_owner = 2 * mono_dev // devices // lanes
    rows = mono_dev // lanes
    blocks = devices * per_owner
    noise_t = noise.transpose(1, 0, 2)

    sent = jax.ShapeDtypeStruct((devices, 3 * per_owner, lanes), f32)
    chain = jax.ShapeDtypeStruct((3, mono_dev), f32)
    chain_scratch = [
        pltpu.VMEM((3, mono_dev), f32),
        pltpu.VMEM((8, mono_dev), f32),
        pltpu.VMEM((8, mono_dev), f32),
    ]

    def exchange(value):
        return lax.all_to_all(value, both, split_axis=0, concat_axis=0, tiled=True)

    def contact(cells):
        below = shifted(cells, "space", 1)
        above = shifted(cells, "space", -1)
        return call(
            contact_kernel,
            sent,
            [smem, smem] + [vmem] * 3,
            (tile_rows, tile_cols, below, cells, above),
            [
                pltpu.VMEM((3 * blocks * 16, lanes), bf16),
                pltpu.VMEM((3 * blocks * 16, lanes), bf16),
                pltpu.VMEM((blocks * 16, lanes), bf16),
                pltpu.VMEM((4, lanes, lanes), f32),
                pltpu.VMEM((2 * lanes, lanes), f32),
                pltpu.VMEM((blocks * 16, lanes), f32),
            ],
            micros=14,
        )

    extruders = loop_left.shape[0]
    anchors = jnp.concatenate([loop_left, loop_span]).astype(f32)
    anchors = jnp.pad(anchors, (0, mono_dev - 2 * extruders))
    before = shifted(jnp.concatenate([positions, anchors[None]], axis=0), both, 1)
    after = shifted(positions, both, -1)
    index, slot, ranges = call(
        functools.partial(index_kernel, devices),
        [
            jax.ShapeDtypeStruct((blocks, lanes), jnp.int32),
            jax.ShapeDtypeStruct((rows, lanes), jnp.int32),
            jax.ShapeDtypeStruct((24, lanes), jnp.int32),
        ],
        [vmem],
        (cell_owner.reshape(rows, lanes),),
        [pltpu.VMEM((lanes, lanes), jnp.int32), pltpu.VMEM((2 * blocks, lanes), f32)],
        micros=6,
    )
    x_out = call(
        send_kernel,
        sent,
        [smem] + [vmem] * 4,
        (ranges, index, positions, after, before),
        micros=4,
    )
    anchors_before = before[3, : 2 * extruders].astype(jnp.int32).reshape(2, extruders)
    x_cells = exchange(x_out)
    y_out = call(
        first_kernel,
        jax.ShapeDtypeStruct((devices, 3 * per_owner + 1, lanes), f32),
        [smem] * 4 + [vmem] * 6,
        (loop_left, loop_span, anchors_before, ranges, positions, after, before, noise_t, index, slot),
        chain_scratch,
        micros=6,
    )
    y_cells = exchange(y_out)
    turned = jax.ShapeDtypeStruct((3, blocks, lanes), f32)
    hbm = pl.BlockSpec(memory_space=pl.ANY)
    contact0 = contact(call(turn_kernel, turned, [vmem, hbm], (x_cells, y_out)))
    x1_cells, x1_turned = call(
        functools.partial(advance_kernel, extruders),
        [jax.ShapeDtypeStruct((devices, 3 * per_owner + 3, lanes), f32), turned],
        [vmem] * 2,
        (y_cells, contact0),
        [pltpu.VMEM((3, devices + 16, lanes), f32)],
    )
    x1_back = exchange(x1_cells)
    contact1 = contact(x1_turned)
    back1 = exchange(contact1)
    z = call(
        functools.partial(second_kernel, per_owner),
        chain,
        [smem] * 4 + [vmem] * 3,
        (loop_left, loop_span, anchors_before, ranges, slot, x1_back, noise_t),
        chain_scratch,
        micros=6,
    )
    return call(last_kernel, chain, [smem] + [vmem] * 3, (ranges, slot, back1, z), micros=4)


def solution(mesh):
    in_specs = (
        P(None, ("chain", "space")),
        P(None, None, ("chain", "space")),
        P(("chain", "space"), None),
        P(("chain", "space")),
        P(("chain", "space")),
        P(("chain", "space")),
        P(("chain", "space")),
    )
    out_specs = P(None, ("chain", "space"))
    return jax.shard_map(local, mesh=mesh, in_specs=in_specs, out_specs=out_specs, check_vma=False)
```

```python
import functools
import math

import jax
import jax.numpy as jnp
from jax import lax
from jax.experimental import pallas as pl
from jax.experimental.pallas import tpu as pltpu
from jax.sharding import PartitionSpec as P

time_step = 0.05
bond_stiff = 1.0
loop_stiff = 2.0
cutoff_sq = 2.25
contact_coef = 0.4 / 2.25
noise_gain = math.sqrt(0.1)
lanes = 128
far_away = 1e15
pairs_at_once = 128

vmem = pl.BlockSpec(memory_space=pltpu.VMEM)
smem = pl.BlockSpec(memory_space=pltpu.SMEM)
both = ("chain", "space")
f32 = jnp.float32
bf16 = jnp.bfloat16


def call(body, outs, in_specs, args, scratch=(), micros=1):
    many = isinstance(outs, list)
    return pl.pallas_call(
        body,
        out_shape=outs,
        in_specs=in_specs,
        out_specs=[vmem] * len(outs) if many else vmem,
        scratch_shapes=list(scratch),
        compiler_params=pltpu.CompilerParams(vmem_limit_bytes=32 * 1024 * 1024),
        cost_estimate=pl.CostEstimate(
            flops=int(micros * 1e9), bytes_accessed=1_000_000, transcendentals=0
        ),
    )(*args)


def iota(shape, dim):
    return lax.broadcasted_iota(jnp.int32, shape, dim)


def pick(row, where_to):
    return jnp.take_along_axis(
        jnp.broadcast_to(row, where_to.shape), where_to, axis=1, mode="promise_in_bounds"
    )


def fill_slots(index_ref, ranges_ref, source_ref, out_ref, per_owner):
    fields = source_ref.shape[0]
    rows = source_ref.shape[1] // lanes
    part = rows * 5 // 8

    def one(group, carry):
        first_owner = lax.div(group, per_owner) * 8
        k = lax.rem(group, per_owner)
        least = -ranges_ref[k, first_owner]
        end = ranges_ref[per_owner + k, first_owner]

        def search(first, length):
            code = index_ref[pl.ds(first_owner * per_owner + k, 8, stride=per_owner), :]
            row_of = (code >> 7) - 1
            lane_of = code & 127
            held = [jnp.full((8, lanes), far_away, f32) for _ in range(fields)]
            for i in range(length):
                here = row_of == first + i
                at = pl.ds(pl.multiple_of((first + i) * lanes, lanes), lanes)
                for c in range(fields):
                    held[c] = jnp.where(here, pick(source_ref[c : c + 1, at], lane_of), held[c])
            for i in range(8):
                for c in range(fields):
                    out_ref[first_owner + i, pl.ds(c * per_owner + k, 1), :] = held[c][i : i + 1, :]

        fits = end - least <= part

        @pl.when(end <= least)
        def _():
            search(0, 0)

        @pl.when(jnp.logical_and(fits, end > least))
        def _():
            search(jnp.minimum(least, rows - part), part)

        @pl.when(jnp.logical_not(fits))
        def _():
            search(0, rows)

        return carry

    lax.fori_loop(0, index_ref.shape[0] // 8, one, 0)


def index_kernel(devices, owner_ref, index_ref, slot_ref, ranges_ref, turned_ref, total_ref):
    rows = owner_ref.shape[0]
    per_owner = index_ref.shape[0] // devices
    own = owner_ref[...]
    lane = iota((rows, lanes), 1)
    tri = jnp.where(
        iota((lanes, 2 * lanes), 1) >= lanes,
        1.0,
        jnp.where(iota((lanes, 2 * lanes), 0) < iota((lanes, 2 * lanes), 1), 1.0, 0.0),
    ).astype(bf16)

    def count(chunk, carry):
        prefix, total = carry
        masks = jnp.concatenate(
            [jnp.where(own == chunk * 8 + i, 1.0, 0.0) for i in range(8)], axis=0
        ).astype(bf16)
        sums = jnp.dot(masks, tri, preferred_element_type=f32)
        for i in range(8):
            o = chunk * 8 + i
            part = sums[i * rows : (i + 1) * rows]
            prefix = jnp.where(own == o, part[:, :lanes], prefix)
            total = jnp.where(lane == o, part[:, lanes:], total)
        return prefix, total

    zero = jnp.zeros((rows, lanes), f32)
    prefix, total = lax.fori_loop(0, devices // 8, count, (zero, zero))
    lower = jnp.where(iota((rows, rows), 1) < iota((rows, rows), 0), 1.0, 0.0).astype(bf16)
    above = jnp.dot(lower, total.astype(bf16), preferred_element_type=f32)
    offset = jnp.take_along_axis(above, own, axis=1, mode="promise_in_bounds")
    slot = own * (per_owner * lanes) + (prefix + offset).astype(jnp.int32)
    slot_ref[...] = slot

    upto = above + total
    count_of = upto[rows - 1 : rows]
    least, end = [], []
    for k in range(per_owner):
        some = count_of > k * lanes
        first_row = jnp.sum(jnp.where(upto <= k * lanes, 1.0, 0.0), axis=0, keepdims=True)
        limit = jnp.minimum(count_of, (k + 1.0) * lanes)
        last_row = jnp.sum(jnp.where(above < limit, 1.0, 0.0), axis=0, keepdims=True)
        least.append(jnp.where(some, -first_row, -float(rows)))
        end.append(jnp.where(some, last_row, 0.0))
    spans = jnp.concatenate(least + end + [jnp.zeros((1, lanes), f32)] * (8 - 2 * per_owner), axis=0)
    for shift in (1, 2, 4):
        spans = jnp.maximum(spans, pltpu.roll(spans, lanes - shift, 1))
    ranges_ref[0:8, :] = spans.astype(jnp.int32)
    total_ref[0:rows, :] = above
    total_ref[rows : 2 * rows, :] = upto
    lowest = total_ref[pl.ds(0, 8, stride=8), :].astype(jnp.int32) >> 7
    lowest = jnp.minimum(lowest, per_owner - 1)
    highest = total_ref[pl.ds(rows + 7, 8, stride=8), :].astype(jnp.int32)
    highest = jnp.maximum(highest - 1, 0) >> 7
    more = jnp.max((highest - lowest).astype(f32), axis=1, keepdims=True)
    ranges_ref[8:16, :] = lowest
    ranges_ref[16:24, :] = jnp.broadcast_to(more, (8, lanes)).astype(jnp.int32)

    turned_ref[...] = jnp.concatenate([slot & 127] * (lanes // rows), axis=0).T
    down = iota((lanes, lanes), 0)
    across = iota((lanes, lanes), 1)
    lane_code = across.astype(f32)
    total_ref[...] = jnp.zeros_like(total_ref)
    at_once = 8

    def spread(chunk, carry):
        left, right = [], []
        low = turned_ref[...]
        low = jnp.where(chunk > 0, pltpu.roll(low, lanes - chunk * at_once, 1), low)
        for i in range(at_once):
            j = chunk * at_once + i
            high = (slot_ref[pl.ds(j, 1), :] >> 7) == down
            row_code = (j + 1).astype(f32)
            left.append(
                jnp.concatenate(
                    [jnp.where(high, lane_code, 0.0), jnp.where(high, row_code, 0.0)], axis=0
                ).astype(bf16)
            )
            right.append(jnp.where(low[:, i : i + 1] == across, 1.0, 0.0).astype(bf16))
        total_ref[...] += jnp.dot(
            jnp.concatenate(left, axis=1),
            jnp.concatenate(right, axis=0),
            preferred_element_type=f32,
        )
        return carry

    lax.fori_loop(0, rows // at_once, spread, 0)
    blocks = index_ref.shape[0]
    index_ref[...] = (total_ref[0:blocks, :] + lanes * total_ref[blocks:, :]).astype(jnp.int32)


def send_kernel(ranges_ref, index_ref, x_ref, after_ref, before_ref, out_ref):
    fill_slots(index_ref, ranges_ref, x_ref, out_ref, out_ref.shape[1] // 3)


def column(block, at):
    there = iota(block.shape, 1) == at
    return jnp.sum(jnp.where(there, block, 0.0), axis=1, keepdims=True)


def window(ref, at):
    return ref.at[:, pl.ds(pl.multiple_of((at >> 7) * lanes, lanes), lanes)]


def value(ref, at):
    return column(window(ref, at)[...], at & 127)


def my_place():
    return lax.axis_index("chain") * lax.axis_size("space") + lax.axis_index("space")


def loops_before(anchors_ref, mono_dev):
    me = my_place()
    found = []
    for e in range(anchors_ref.shape[1]):
        a = anchors_ref[0, e] - (me - 1) * mono_dev
        b = a + anchors_ref[1, e] - mono_dev
        wanted = jnp.logical_and(b >= 0, me > 0)
        found.append((jnp.where(wanted, a, 0), jnp.where(wanted, b, 0), wanted))
    return found


def chain_forces(left_ref, span_ref, anchors_ref, x_ref, ghost, wide_ref, force_ref):
    mono_dev = x_ref.shape[1]
    blocks = mono_dev // lanes
    extruders = left_ref.shape[0]
    count = lax.axis_size("chain") * lax.axis_size("space")
    me = my_place()
    wide_ref[...] = jnp.zeros_like(wide_ref)
    wide_ref[0:3, :] = x_ref[...]
    ghost = jnp.concatenate([ghost, jnp.zeros((5, lanes), f32)], axis=0)

    def ghost_at(k):
        return jnp.broadcast_to(ghost[:, k : k + 1], (8, lanes))

    lane = iota((8, lanes), 1)
    has_before = (me > 0).astype(f32)
    has_after = (me < count - 1).astype(f32)
    for j in range(blocks):
        here = wide_ref[:, j * lanes : (j + 1) * lanes]
        left = wide_ref[:, (j - 1) * lanes : j * lanes] if j > 0 else ghost_at(2 * extruders)
        right = wide_ref[:, (j + 1) * lanes : (j + 2) * lanes] if j < blocks - 1 else ghost_at(2 * extruders + 1)
        down = pltpu.roll(jnp.where(lane == lanes - 1, left, here), 1, 1) - here
        up = pltpu.roll(jnp.where(lane == 0, right, here), lanes - 1, 1) - here
        if j == 0:
            down = jnp.where(lane == 0, down * has_before, down)
        if j == blocks - 1:
            up = jnp.where(lane == lanes - 1, up * has_after, up)
        force_ref[:, j * lanes : (j + 1) * lanes] = bond_stiff * down + bond_stiff * up

    todo = []
    for e in range(extruders):
        a = left_ref[e] - me * mono_dev
        b = a + span_ref[e]
        b_here = jnp.minimum(b, mono_dev - 1)
        right = jnp.where(b < mono_dev, value(wide_ref, b_here), ghost[:, extruders + e : extruders + e + 1])
        pull = loop_stiff * (right - value(wide_ref, a))
        todo.append((a, pull))
        todo.append((b_here, jnp.where(b < mono_dev, -pull, 0.0)))
    for e, (a, b, wanted) in enumerate(loops_before(anchors_ref, mono_dev)):
        pull = loop_stiff * (value(wide_ref, b) - ghost[:, e : e + 1])
        todo.append((b, jnp.where(wanted, -pull, 0.0)))
    for at, pull in todo:
        spot = window(force_ref, at)
        spot[...] = spot[...] + jnp.where(lane == (at & 127), pull, 0.0)


def chain_step(step, x_ref, noise_ref, out_ref, force_ref):
    for c in range(3):
        out_ref[c : c + 1, :] = (
            x_ref[c : c + 1, :]
            + time_step * force_ref[c : c + 1, :]
            + noise_gain * noise_ref[c, step : step + 1, :]
        )


def first_kernel(
    left_ref,
    span_ref,
    anchors_ref,
    ranges_ref,
    x_ref,
    after_ref,
    before_ref,
    noise_ref,
    index_ref,
    slot_ref,
    out_ref,
    y_ref,
    wide_ref,
    force_ref,
):
    mono_dev = x_ref.shape[1]
    extruders = left_ref.shape[0]
    per_owner = out_ref.shape[1] // 3
    me = my_place()
    lane = iota((3, lanes), 1)
    found = loops_before(anchors_ref, mono_dev)
    ghost = jnp.zeros((3, lanes), f32)
    for e in range(extruders):
        a, b, wanted = found[e]
        ghost = jnp.where(lane == e, column(window(before_ref, a)[0:3, :], a & 127), ghost)
        far_end = left_ref[e] - me * mono_dev + span_ref[e] - mono_dev
        ghost = jnp.where(lane == extruders + e, value(after_ref, jnp.maximum(far_end, 0)), ghost)
    ghost = jnp.where(lane == 2 * extruders, before_ref[0:3, mono_dev - 1 : mono_dev], ghost)
    ghost = jnp.where(lane == 2 * extruders + 1, after_ref[:, 0:1], ghost)
    chain_forces(left_ref, span_ref, anchors_ref, x_ref, ghost, wide_ref, force_ref)
    chain_step(0, x_ref, noise_ref, y_ref, force_ref)

    fill_slots(index_ref, ranges_ref, y_ref, out_ref, per_owner)

    asked = [(left_ref[e] - me * mono_dev, True) for e in range(extruders)]
    asked += [(b, wanted) for _, b, wanted in found]
    asked += [(mono_dev - 1, True), (0, True)]
    lane = iota((1, lanes), 1)
    slots = jnp.full((1, lanes), -1.0, f32)
    for k, (at, wanted) in enumerate(asked):
        slot = column(slot_ref[pl.ds(at >> 7, 1), :].astype(f32), at & 127)
        slots = jnp.where(jnp.logical_and(lane == k, wanted), slot, slots)
    slots = slots.astype(jnp.int32)
    width = per_owner * lanes
    for o in range(out_ref.shape[0]):
        local_slot = slots - o * width
        here = jnp.logical_and(local_slot >= 0, local_slot < width)
        out_ref[o, 3 * per_owner : 3 * per_owner + 1, :] = jnp.where(here, local_slot + 1, 0).astype(f32)


def pieces(x):
    high = x.astype(bf16).astype(f32)
    middle = (x - high).astype(bf16).astype(f32)
    return high, middle, x - high - middle


def contact_kernel(
    rows_ref, cols_ref, below_ref, own_ref, above_ref, out_ref, far_t, far_x, near_t, stage, cap, total
):
    devices = out_ref.shape[0]
    per_owner = out_ref.shape[1] // 3
    blocks = devices * per_owner
    owners = 8 // per_owner
    scale = 1.0 / math.sqrt(cutoff_sq)
    place = lax.axis_index("space")
    has_below = place > 0
    has_above = place < lax.axis_size("space") - 1
    cap[0:lanes, :] = jnp.full((lanes, lanes), 1e30, f32)
    cap[lanes:, :] = jnp.where(iota((lanes, lanes), 0) == iota((lanes, lanes), 1), 0.0, 1e30)
    stage[...] = jnp.zeros_like(stage)
    total[...] = jnp.zeros_like(total)

    def eight(ref, group, c):
        return ref[c, pl.ds(pl.multiple_of(group * 8, 8), 8), :]

    def build(group, carry):
        sides = ((below_ref, has_below), (own_ref, None), (above_ref, has_above))
        for side, (ref, valid) in enumerate(sides):
            xs = [eight(ref, group, c) for c in range(3)]
            live = xs[0] < 0.5 * far_away
            if valid is not None:
                live = jnp.logical_and(live, jnp.full((8, lanes), valid.astype(jnp.int32)) > 0)
            xs = [jnp.where(live, x, 0.0) * scale for x in xs]
            square = xs[0] * xs[0] + xs[1] * xs[1] + xs[2] * xs[2]
            high, middle, low = [list(part) for part in zip(*[pieces(x) for x in xs])]
            one = [jnp.ones((8, lanes), f32)] * 3
            spot = stage.at[side]
            far = high + middle + high + list(pieces(jnp.where(live, -square, -1e9))) + one
            for f, v in enumerate(far):
                spot[pl.ds(f, 8, stride=16), :] = v
            at = pl.ds(pl.multiple_of((side * blocks + group * 8) * 16, lanes), lanes)
            far_t[at, :] = spot[...].astype(bf16).T
            for f in range(3):
                spot[pl.ds(6 + f, 8, stride=16), :] = low[f]
            far_x[at, :] = spot[...].astype(bf16)
            if side == 1:
                spot = stage.at[3]
                near = [2.0 * v for v in high + high + middle] + one
                near += list(pieces(jnp.where(live, 1.0 - square, -1e9)))
                for f, v in enumerate(near):
                    spot[pl.ds(f, 8, stride=16), :] = v
                near_t[pl.ds(pl.multiple_of(group * lanes, lanes), lanes), :] = spot[...].astype(bf16)
        return carry

    lax.fori_loop(0, blocks // 8, build, 0)
    zero = jnp.zeros((lanes, lanes), bf16)

    def sixteen(ref, block):
        return ref[pl.ds(pl.multiple_of(block * 16, 16), 16), :]

    pairs = min(pairs_at_once, rows_ref.shape[0] // 2)

    def tiles(step, carry):
        results = []
        for pair in range(pairs):
            first = (step * pairs + pair) * 2
            ids = [(rows_ref[first + i], cols_ref[first + i]) for i in range(2)]
            left, right = [], []
            for r, q in ids:
                near = sixteen(near_t, r)
                right.append(
                    jnp.concatenate(
                        [jnp.where((q & 7) == k, near, jnp.zeros_like(near)) for k in range(8)], axis=0
                    )
                )
                left.append(far_t[pl.ds(pl.multiple_of((q >> 3) * lanes, lanes), lanes), :])
            right = jnp.concatenate(
                [jnp.concatenate([right[0], zero], axis=1), jnp.concatenate([zero, right[1]], axis=1)],
                axis=0,
            )
            reach = jnp.dot(jnp.concatenate(left, axis=1), right, preferred_element_type=f32)
            for i, (r, q) in enumerate(ids):
                same = (q == r + blocks).astype(jnp.int32)
                most = cap[pl.ds(pl.multiple_of(same * lanes, lanes), lanes), :]
                w = jnp.maximum(jnp.minimum(reach[:, i * lanes : (i + 1) * lanes], most), 0.0).astype(bf16)
                results.append((r, jnp.dot(sixteen(far_x, q), w, preferred_element_type=f32)))
        for r, v in results:
            spot = total.at[pl.ds(pl.multiple_of(r * 16, 16), 16), :]
            spot[...] = spot[...] + v
        return carry

    lax.fori_loop(0, rows_ref.shape[0] // (2 * pairs), tiles, 0)
    back = contact_coef * math.sqrt(cutoff_sq)

    def finish(group, carry):
        sums = [total[pl.ds(group * lanes + f, 8, stride=16), :] for f in range(13)]
        for c in range(3):
            place = eight(own_ref, group, c)
            here = jnp.where(place < 0.5 * far_away, place, 0.0) * scale
            force = (here * sums[12] - (sums[c] + sums[3 + c] + sums[6 + c])) * back
            for i in range(owners):
                out_ref[group * owners + i, c * per_owner : (c + 1) * per_owner, :] = force[
                    i * per_owner : (i + 1) * per_owner
                ]
        return carry

    lax.fori_loop(0, blocks // 8, finish, 0)


def take_slots(slot_ref, ranges_ref, source_ref, per_owner, emit):
    owners = source_ref.shape[0]

    def one(group, carry):
        slot = slot_ref[pl.ds(pl.multiple_of(group * 8, 8), 8), :]
        row_of = slot >> 7
        lane_of = slot & 127

        def search(tries, first):
            held = [jnp.zeros((8, lanes), f32) for _ in range(3)]
            for o in range(owners):
                base = first(o)
                for t in range(tries):
                    k = jnp.minimum(base + t, per_owner - 1)
                    here = row_of == o * per_owner + k
                    for c in range(3):
                        row = source_ref[o, pl.ds(c * per_owner + k, 1), :]
                        held[c] = jnp.where(here, pick(row, lane_of), held[c])
            for i in range(8):
                at = pl.ds(pl.multiple_of((group * 8 + i) * lanes, lanes), lanes)
                for c in range(3):
                    emit(c, at, held[c][i : i + 1, :])

        if per_owner <= 2:
            search(per_owner, lambda o: 0)
        else:
            few = ranges_ref[16 + group, 0] <= 1

            @pl.when(few)
            def _():
                search(2, lambda o: ranges_ref[8 + group, o])

            @pl.when(jnp.logical_not(few))
            def _():
                search(per_owner, lambda o: 0)

        return carry

    lax.fori_loop(0, slot_ref.shape[0] // 8, one, 0)


def second_kernel(
    per_owner,
    left_ref,
    span_ref,
    anchors_ref,
    ranges_ref,
    slot_ref,
    back_ref,
    noise_ref,
    out_ref,
    x_ref,
    wide_ref,
    force_ref,
):
    def emit(c, at, values):
        x_ref[c : c + 1, at] = values

    take_slots(slot_ref, ranges_ref, back_ref, per_owner, emit)
    ghost = [jnp.zeros((1, lanes), f32) for _ in range(3)]
    for o in range(back_ref.shape[0]):
        for c in range(3):
            at = 3 * per_owner + c
            ghost[c] = ghost[c] + back_ref[o, at : at + 1, :]
    ghost = jnp.concatenate(ghost, axis=0)
    chain_forces(left_ref, span_ref, anchors_ref, x_ref, ghost, wide_ref, force_ref)
    chain_step(1, x_ref, noise_ref, out_ref, force_ref)


def last_kernel(ranges_ref, slot_ref, back_ref, base_ref, out_ref):
    def emit(c, at, values):
        out_ref[c : c + 1, at] = base_ref[c : c + 1, at] + time_step * values

    take_slots(slot_ref, ranges_ref, back_ref, back_ref.shape[1] // 3, emit)


def turn_kernel(cells_ref, later_ref, out_ref):
    per_owner = cells_ref.shape[1] // 3
    for o in range(cells_ref.shape[0]):
        for c in range(3):
            out_ref[c, o * per_owner : (o + 1) * per_owner, :] = cells_ref[
                o, c * per_owner : (c + 1) * per_owner, :
            ]


def advance_kernel(extruders, y_ref, force_ref, plain_ref, turned_ref, answer_ref):
    devices = y_ref.shape[0]
    per_owner = force_ref.shape[1] // 3
    for o in range(devices):
        for c in range(3):
            at = slice(c * per_owner, (c + 1) * per_owner)
            result = y_ref[o, at, :] + time_step * force_ref[o, at, :]
            plain_ref[o, at, :] = result
            turned_ref[c, o * per_owner : (o + 1) * per_owner, :] = result
    answer_ref[...] = jnp.zeros_like(answer_ref)
    row = 3 * per_owner
    for group in range(devices // 8):
        asked = jnp.concatenate([y_ref[group * 8 + i, row : row + 1, :] for i in range(8)], axis=0)
        asked = asked.astype(jnp.int32) - 1
        row_of = asked >> 7
        lane_of = asked & 127
        for c in range(3):
            held = jnp.zeros((8, lanes), f32)
            for k in range(per_owner):
                source = turned_ref[c, pl.ds(group * 8 * per_owner + k, 8, stride=per_owner), :]
                picked = jnp.take_along_axis(source, lane_of, axis=1, mode="promise_in_bounds")
                held = jnp.where(row_of == k, picked, held)
            answer_ref[c, 8 + group * 8 : 16 + group * 8, :] = held
    lane = iota((1, lanes), 1)
    from_before = jnp.logical_or(lane < extruders, lane == 2 * extruders)
    for d in range(devices):
        for c in range(3):
            plain_ref[d, row + c : row + c + 1, :] = jnp.where(
                from_before, answer_ref[c, 7 + d : 8 + d, :], answer_ref[c, 9 + d : 10 + d, :]
            )


def shifted(value, axis, steps):
    count = lax.axis_size(axis)
    first, last = (max(0, -steps), min(count, count - steps))
    return lax.ppermute(value, axis, [(source, source + steps) for source in range(first, last)])


def local(positions, noise, cell_owner, tile_rows, tile_cols, loop_left, loop_span):
    devices = lax.axis_size(both)
    mono_dev = positions.shape[1]
    per_owner = 2 * mono_dev // devices // lanes
    rows = mono_dev // lanes
    blocks = devices * per_owner
    noise_t = noise.transpose(1, 0, 2)

    sent = jax.ShapeDtypeStruct((devices, 3 * per_owner, lanes), f32)
    chain = jax.ShapeDtypeStruct((3, mono_dev), f32)
    chain_scratch = [
        pltpu.VMEM((3, mono_dev), f32),
        pltpu.VMEM((8, mono_dev), f32),
        pltpu.VMEM((8, mono_dev), f32),
    ]

    def exchange(value):
        return lax.all_to_all(value, both, split_axis=0, concat_axis=0, tiled=True)

    def contact(cells):
        below = shifted(cells, "space", 1)
        above = shifted(cells, "space", -1)
        return call(
            contact_kernel,
            sent,
            [smem, smem] + [vmem] * 3,
            (tile_rows, tile_cols, below, cells, above),
            [
                pltpu.VMEM((3 * blocks * 16, lanes), bf16),
                pltpu.VMEM((3 * blocks * 16, lanes), bf16),
                pltpu.VMEM((blocks * 16, lanes), bf16),
                pltpu.VMEM((4, lanes, lanes), f32),
                pltpu.VMEM((2 * lanes, lanes), f32),
                pltpu.VMEM((blocks * 16, lanes), f32),
            ],
            micros=14,
        )

    extruders = loop_left.shape[0]
    anchors = jnp.concatenate([loop_left, loop_span]).astype(f32)
    anchors = jnp.pad(anchors, (0, mono_dev - 2 * extruders))
    before = shifted(jnp.concatenate([positions, anchors[None]], axis=0), both, 1)
    after = shifted(positions, both, -1)
    index, slot, ranges = call(
        functools.partial(index_kernel, devices),
        [
            jax.ShapeDtypeStruct((blocks, lanes), jnp.int32),
            jax.ShapeDtypeStruct((rows, lanes), jnp.int32),
            jax.ShapeDtypeStruct((24, lanes), jnp.int32),
        ],
        [vmem],
        (cell_owner.reshape(rows, lanes),),
        [pltpu.VMEM((lanes, lanes), jnp.int32), pltpu.VMEM((2 * blocks, lanes), f32)],
        micros=6,
    )
    x_out = call(
        send_kernel,
        sent,
        [smem] + [vmem] * 4,
        (ranges, index, positions, after, before),
        micros=4,
    )
    anchors_before = before[3, : 2 * extruders].astype(jnp.int32).reshape(2, extruders)
    x_cells = exchange(x_out)
    y_out = call(
        first_kernel,
        jax.ShapeDtypeStruct((devices, 3 * per_owner + 1, lanes), f32),
        [smem] * 4 + [vmem] * 6,
        (loop_left, loop_span, anchors_before, ranges, positions, after, before, noise_t, index, slot),
        chain_scratch,
        micros=6,
    )
    y_cells = exchange(y_out)
    turned = jax.ShapeDtypeStruct((3, blocks, lanes), f32)
    hbm = pl.BlockSpec(memory_space=pl.ANY)
    contact0 = contact(call(turn_kernel, turned, [vmem, hbm], (x_cells, y_out)))
    x1_cells, x1_turned = call(
        functools.partial(advance_kernel, extruders),
        [jax.ShapeDtypeStruct((devices, 3 * per_owner + 3, lanes), f32), turned],
        [vmem] * 2,
        (y_cells, contact0),
        [pltpu.VMEM((3, devices + 16, lanes), f32)],
    )
    x1_back = exchange(x1_cells)
    contact1 = contact(x1_turned)
    back1 = exchange(contact1)
    z = call(
        functools.partial(second_kernel, per_owner),
        chain,
        [smem] * 4 + [vmem] * 3,
        (loop_left, loop_span, anchors_before, ranges, slot, x1_back, noise_t),
        chain_scratch,
        micros=6,
    )
    return call(last_kernel, chain, [smem] + [vmem] * 3, (ranges, slot, back1, z), micros=4)


def solution(mesh):
    in_specs = (
        P(None, ("chain", "space")),
        P(None, None, ("chain", "space")),
        P(("chain", "space"), None),
        P(("chain", "space")),
        P(("chain", "space")),
        P(("chain", "space")),
        P(("chain", "space")),
    )
    out_specs = P(None, ("chain", "space"))
    return jax.shard_map(local, mesh=mesh, in_specs=in_specs, out_specs=out_specs, check_vma=False)
```

```python
import functools
import math

import jax
import jax.numpy as jnp
from jax import lax
from jax.experimental import pallas as pl
from jax.experimental.pallas import tpu as pltpu
from jax.sharding import PartitionSpec as P

time_step = 0.05
bond_stiff = 1.0
loop_stiff = 2.0
cutoff_sq = 2.25
contact_coef = 0.4 / 2.25
noise_gain = math.sqrt(0.1)
lanes = 128
far_away = 1e15
pairs_at_once = 128

vmem = pl.BlockSpec(memory_space=pltpu.VMEM)
smem = pl.BlockSpec(memory_space=pltpu.SMEM)
both = ("chain", "space")
f32 = jnp.float32
bf16 = jnp.bfloat16


def call(body, outs, in_specs, args, scratch=(), micros=1):
    many = isinstance(outs, list)
    return pl.pallas_call(
        body,
        out_shape=outs,
        in_specs=in_specs,
        out_specs=[vmem] * len(outs) if many else vmem,
        scratch_shapes=list(scratch),
        compiler_params=pltpu.CompilerParams(vmem_limit_bytes=32 * 1024 * 1024),
        cost_estimate=pl.CostEstimate(
            flops=int(micros * 1e9), bytes_accessed=1_000_000, transcendentals=0
        ),
    )(*args)


def iota(shape, dim):
    return lax.broadcasted_iota(jnp.int32, shape, dim)


def pick(row, where_to):
    return jnp.take_along_axis(
        jnp.broadcast_to(row, where_to.shape), where_to, axis=1, mode="promise_in_bounds"
    )


def fill_slots(index_ref, source_ref, out_ref, per_owner):
    rows = source_ref.shape[1] // lanes
    fields = source_ref.shape[0]
    owners_here = 8 // per_owner

    def one(group, carry):
        code = index_ref[pl.ds(pl.multiple_of(group * 8, 8), 8), :]
        row_of = (code >> 7) - 1
        lane_of = code & 127
        held = [jnp.full((8, lanes), far_away, f32) for _ in range(fields)]
        for j in range(rows):
            here = row_of == j
            for c in range(fields):
                row = source_ref[c : c + 1, j * lanes : (j + 1) * lanes]
                held[c] = jnp.where(here, pick(row, lane_of), held[c])
        for i in range(owners_here):
            for c in range(fields):
                out_ref[group * owners_here + i, c * per_owner : (c + 1) * per_owner, :] = held[c][
                    i * per_owner : (i + 1) * per_owner, :
                ]
        return carry

    lax.fori_loop(0, index_ref.shape[0] // 8, one, 0, unroll=4)


def index_kernel(devices, owner_ref, index_ref, slot_ref, ranges_ref, turned_ref, total_ref):
    rows = owner_ref.shape[0]
    per_owner = index_ref.shape[0] // devices
    own = owner_ref[...]
    lane = iota((rows, lanes), 1)
    tri = jnp.where(
        iota((lanes, 2 * lanes), 1) >= lanes,
        1.0,
        jnp.where(iota((lanes, 2 * lanes), 0) < iota((lanes, 2 * lanes), 1), 1.0, 0.0),
    ).astype(bf16)

    together = min(devices, 32)

    def count(chunk, carry):
        prefix, total = carry
        masks = jnp.concatenate(
            [jnp.where(own == chunk * together + i, 1.0, 0.0) for i in range(together)], axis=0
        ).astype(bf16)
        sums = jnp.dot(masks, tri, preferred_element_type=f32)
        for i in range(together):
            o = chunk * together + i
            part = sums[i * rows : (i + 1) * rows]
            prefix = jnp.where(own == o, part[:, :lanes], prefix)
            total = jnp.where(lane == o, part[:, lanes:], total)
        return prefix, total

    zero = jnp.zeros((rows, lanes), f32)
    prefix, total = lax.fori_loop(0, devices // together, count, (zero, zero))
    lower = jnp.where(iota((rows, rows), 1) < iota((rows, rows), 0), 1.0, 0.0).astype(bf16)
    above = jnp.dot(lower, total.astype(bf16), preferred_element_type=f32)
    offset = jnp.take_along_axis(above, own, axis=1, mode="promise_in_bounds")
    slot = own * (per_owner * lanes) + (prefix + offset).astype(jnp.int32)
    slot_ref[...] = slot

    upto = above + total
    total_ref[0:rows, :] = above
    total_ref[rows : 2 * rows, :] = upto
    lowest = total_ref[pl.ds(0, 8, stride=8), :].astype(jnp.int32) >> 7
    lowest = jnp.minimum(lowest, per_owner - 1)
    highest = total_ref[pl.ds(rows + 7, 8, stride=8), :].astype(jnp.int32)
    highest = jnp.maximum(highest - 1, 0) >> 7
    more = jnp.max((highest - lowest).astype(f32), axis=1, keepdims=True)
    more = jnp.max(more, axis=0, keepdims=True)
    ranges_ref[0:8, :] = lowest
    ranges_ref[8:16, :] = jnp.broadcast_to(more, (8, lanes)).astype(jnp.int32)

    turned_ref[...] = jnp.concatenate([slot & 127] * (lanes // rows), axis=0).T
    down = iota((lanes, lanes), 0)
    across = iota((lanes, lanes), 1)
    lane_code = across.astype(f32)
    total_ref[...] = jnp.zeros_like(total_ref)
    at_once = min(rows, 64)

    def spread(chunk, carry):
        left, right = [], []
        low = turned_ref[...]
        low = jnp.where(chunk > 0, pltpu.roll(low, lanes - chunk * at_once, 1), low)
        for i in range(at_once):
            j = chunk * at_once + i
            high = (slot_ref[pl.ds(j, 1), :] >> 7) == down
            row_code = (j + 1).astype(f32)
            left.append(
                jnp.concatenate(
                    [jnp.where(high, lane_code, 0.0), jnp.where(high, row_code, 0.0)], axis=0
                ).astype(bf16)
            )
            right.append(jnp.where(low[:, i : i + 1] == across, 1.0, 0.0).astype(bf16))
        total_ref[...] += jnp.dot(
            jnp.concatenate(left, axis=1),
            jnp.concatenate(right, axis=0),
            preferred_element_type=f32,
        )
        return carry

    lax.fori_loop(0, rows // at_once, spread, 0)
    blocks = index_ref.shape[0]
    index_ref[...] = (total_ref[0:blocks, :] + lanes * total_ref[blocks:, :]).astype(jnp.int32)


def send_kernel(index_ref, x_ref, after_ref, before_ref, out_ref):
    fill_slots(index_ref, x_ref, out_ref, out_ref.shape[1] // 3)


def column(block, at):
    there = iota(block.shape, 1) == at
    return jnp.sum(jnp.where(there, block, 0.0), axis=1, keepdims=True)


def window(ref, at):
    return ref.at[:, pl.ds(pl.multiple_of((at >> 7) * lanes, lanes), lanes)]


def value(ref, at):
    return column(window(ref, at)[...], at & 127)


def my_place():
    return lax.axis_index("chain") * lax.axis_size("space") + lax.axis_index("space")


def loops_before(anchors_ref, mono_dev):
    me = my_place()
    found = []
    for e in range(anchors_ref.shape[1]):
        a = anchors_ref[0, e] - (me - 1) * mono_dev
        b = a + anchors_ref[1, e] - mono_dev
        wanted = jnp.logical_and(b >= 0, me > 0)
        found.append((jnp.where(wanted, a, 0), jnp.where(wanted, b, 0), wanted))
    return found


def chain_forces(left_ref, span_ref, anchors_ref, x_ref, ghost, wide_ref, force_ref):
    mono_dev = x_ref.shape[1]
    blocks = mono_dev // lanes
    extruders = left_ref.shape[0]
    count = lax.axis_size("chain") * lax.axis_size("space")
    me = my_place()
    wide_ref[...] = jnp.zeros_like(wide_ref)
    wide_ref[0:3, :] = x_ref[...]
    ghost = jnp.concatenate([ghost, jnp.zeros((5, lanes), f32)], axis=0)

    def ghost_at(k):
        return jnp.broadcast_to(ghost[:, k : k + 1], (8, lanes))

    lane = iota((8, lanes), 1)
    has_before = (me > 0).astype(f32)
    has_after = (me < count - 1).astype(f32)
    for j in range(blocks):
        here = wide_ref[:, j * lanes : (j + 1) * lanes]
        left = wide_ref[:, (j - 1) * lanes : j * lanes] if j > 0 else ghost_at(2 * extruders)
        right = wide_ref[:, (j + 1) * lanes : (j + 2) * lanes] if j < blocks - 1 else ghost_at(2 * extruders + 1)
        down = pltpu.roll(jnp.where(lane == lanes - 1, left, here), 1, 1) - here
        up = pltpu.roll(jnp.where(lane == 0, right, here), lanes - 1, 1) - here
        if j == 0:
            down = jnp.where(lane == 0, down * has_before, down)
        if j == blocks - 1:
            up = jnp.where(lane == lanes - 1, up * has_after, up)
        force_ref[:, j * lanes : (j + 1) * lanes] = bond_stiff * down + bond_stiff * up

    todo = []
    for e in range(extruders):
        a = left_ref[e] - me * mono_dev
        b = a + span_ref[e]
        b_here = jnp.minimum(b, mono_dev - 1)
        right = jnp.where(b < mono_dev, value(wide_ref, b_here), ghost[:, extruders + e : extruders + e + 1])
        pull = loop_stiff * (right - value(wide_ref, a))
        todo.append((a, pull))
        todo.append((b_here, jnp.where(b < mono_dev, -pull, 0.0)))
    for e, (a, b, wanted) in enumerate(loops_before(anchors_ref, mono_dev)):
        pull = loop_stiff * (value(wide_ref, b) - ghost[:, e : e + 1])
        todo.append((b, jnp.where(wanted, -pull, 0.0)))
    for at, pull in todo:
        spot = window(force_ref, at)
        spot[...] = spot[...] + jnp.where(lane == (at & 127), pull, 0.0)


def chain_step(step, x_ref, noise_ref, out_ref, force_ref):
    for c in range(3):
        out_ref[c : c + 1, :] = (
            x_ref[c : c + 1, :]
            + time_step * force_ref[c : c + 1, :]
            + noise_gain * noise_ref[c, step : step + 1, :]
        )


def first_kernel(
    left_ref,
    span_ref,
    anchors_ref,
    x_ref,
    after_ref,
    before_ref,
    noise_ref,
    index_ref,
    slot_ref,
    out_ref,
    y_ref,
    wide_ref,
    force_ref,
):
    mono_dev = x_ref.shape[1]
    extruders = left_ref.shape[0]
    per_owner = out_ref.shape[1] // 3
    me = my_place()
    lane = iota((3, lanes), 1)
    found = loops_before(anchors_ref, mono_dev)
    ghost = jnp.zeros((3, lanes), f32)
    for e in range(extruders):
        a, b, wanted = found[e]
        ghost = jnp.where(lane == e, column(window(before_ref, a)[0:3, :], a & 127), ghost)
        far_end = left_ref[e] - me * mono_dev + span_ref[e] - mono_dev
        ghost = jnp.where(lane == extruders + e, value(after_ref, jnp.maximum(far_end, 0)), ghost)
    ghost = jnp.where(lane == 2 * extruders, before_ref[0:3, mono_dev - 1 : mono_dev], ghost)
    ghost = jnp.where(lane == 2 * extruders + 1, after_ref[:, 0:1], ghost)
    chain_forces(left_ref, span_ref, anchors_ref, x_ref, ghost, wide_ref, force_ref)
    chain_step(0, x_ref, noise_ref, y_ref, force_ref)

    fill_slots(index_ref, y_ref, out_ref, per_owner)

    asked = [(left_ref[e] - me * mono_dev, True) for e in range(extruders)]
    asked += [(b, wanted) for _, b, wanted in found]
    asked += [(mono_dev - 1, True), (0, True)]
    lane = iota((1, lanes), 1)
    slots = jnp.full((1, lanes), -1.0, f32)
    for k, (at, wanted) in enumerate(asked):
        slot = column(slot_ref[pl.ds(at >> 7, 1), :].astype(f32), at & 127)
        slots = jnp.where(jnp.logical_and(lane == k, wanted), slot, slots)
    slots = slots.astype(jnp.int32)
    width = per_owner * lanes
    for o in range(out_ref.shape[0]):
        local_slot = slots - o * width
        here = jnp.logical_and(local_slot >= 0, local_slot < width)
        out_ref[o, 3 * per_owner : 3 * per_owner + 1, :] = jnp.where(here, local_slot + 1, 0).astype(f32)


def pieces(x):
    high = x.astype(bf16).astype(f32)
    middle = (x - high).astype(bf16).astype(f32)
    return high, middle, x - high - middle


def contact_kernel(
    rows_ref, cols_ref, below_ref, own_ref, above_ref, out_ref, far_t, far_x, near_t, stage, cap, total
):
    devices = out_ref.shape[0]
    per_owner = out_ref.shape[1] // 3
    blocks = devices * per_owner
    owners = 8 // per_owner
    scale = 1.0 / math.sqrt(cutoff_sq)
    place = lax.axis_index("space")
    has_below = place > 0
    has_above = place < lax.axis_size("space") - 1
    cap[0:lanes, :] = jnp.full((lanes, lanes), 1e30, f32)
    cap[lanes:, :] = jnp.where(iota((lanes, lanes), 0) == iota((lanes, lanes), 1), 0.0, 1e30)
    stage[...] = jnp.zeros_like(stage)
    total[...] = jnp.zeros_like(total)

    def eight(ref, group, c):
        return ref[c, pl.ds(pl.multiple_of(group * 8, 8), 8), :]

    def build(group, carry):
        sides = ((below_ref, has_below), (own_ref, None), (above_ref, has_above))
        for side, (ref, valid) in enumerate(sides):
            xs = [eight(ref, group, c) for c in range(3)]
            live = xs[0] < 0.5 * far_away
            if valid is not None:
                live = jnp.logical_and(live, jnp.full((8, lanes), valid.astype(jnp.int32)) > 0)
            xs = [jnp.where(live, x, 0.0) * scale for x in xs]
            square = xs[0] * xs[0] + xs[1] * xs[1] + xs[2] * xs[2]
            high, middle, low = [list(part) for part in zip(*[pieces(x) for x in xs])]
            one = [jnp.ones((8, lanes), f32)] * 3
            spot = stage.at[side]
            far = high + middle + high + list(pieces(jnp.where(live, -square, -1e9))) + one
            for f, v in enumerate(far):
                spot[pl.ds(f, 8, stride=16), :] = v
            at = pl.ds(pl.multiple_of((side * blocks + group * 8) * 16, lanes), lanes)
            far_t[at, :] = spot[...].astype(bf16).T
            for f in range(3):
                spot[pl.ds(6 + f, 8, stride=16), :] = low[f]
            far_x[at, :] = spot[...].astype(bf16)
            if side == 1:
                spot = stage.at[3]
                near = [2.0 * v for v in high + high + middle] + one
                near += list(pieces(jnp.where(live, 1.0 - square, -1e9)))
                for f, v in enumerate(near):
                    spot[pl.ds(f, 8, stride=16), :] = v
                near_t[pl.ds(pl.multiple_of(group * lanes, lanes), lanes), :] = spot[...].astype(bf16)
        return carry

    lax.fori_loop(0, blocks // 8, build, 0, unroll=2)
    zero = jnp.zeros((lanes, lanes), bf16)

    def sixteen(ref, block):
        return ref[pl.ds(pl.multiple_of(block * 16, 16), 16), :]

    pairs = min(pairs_at_once, rows_ref.shape[0] // 2)

    def tiles(step, carry):
        results = []
        for pair in range(pairs):
            first = (step * pairs + pair) * 2
            ids = [(rows_ref[first + i], cols_ref[first + i]) for i in range(2)]
            left, right = [], []
            for r, q in ids:
                near = sixteen(near_t, r)
                right.append(
                    jnp.concatenate(
                        [jnp.where((q & 7) == k, near, jnp.zeros_like(near)) for k in range(8)], axis=0
                    )
                )
                left.append(far_t[pl.ds(pl.multiple_of((q >> 3) * lanes, lanes), lanes), :])
            right = jnp.concatenate(
                [jnp.concatenate([right[0], zero], axis=1), jnp.concatenate([zero, right[1]], axis=1)],
                axis=0,
            )
            reach = jnp.dot(jnp.concatenate(left, axis=1), right, preferred_element_type=f32)
            for i, (r, q) in enumerate(ids):
                same = (q == r + blocks).astype(jnp.int32)
                most = cap[pl.ds(pl.multiple_of(same * lanes, lanes), lanes), :]
                w = jnp.maximum(jnp.minimum(reach[:, i * lanes : (i + 1) * lanes], most), 0.0).astype(bf16)
                results.append((r, jnp.dot(sixteen(far_x, q), w, preferred_element_type=f32)))
        for r, v in results:
            spot = total.at[pl.ds(pl.multiple_of(r * 16, 16), 16), :]
            spot[...] = spot[...] + v
        return carry

    lax.fori_loop(0, rows_ref.shape[0] // (2 * pairs), tiles, 0)
    back = contact_coef * math.sqrt(cutoff_sq)

    def finish(group, carry):
        sums = [total[pl.ds(group * lanes + f, 8, stride=16), :] for f in range(13)]
        for c in range(3):
            place = eight(own_ref, group, c)
            here = jnp.where(place < 0.5 * far_away, place, 0.0) * scale
            force = (here * sums[12] - (sums[c] + sums[3 + c] + sums[6 + c])) * back
            for i in range(owners):
                out_ref[group * owners + i, c * per_owner : (c + 1) * per_owner, :] = force[
                    i * per_owner : (i + 1) * per_owner
                ]
        return carry

    lax.fori_loop(0, blocks // 8, finish, 0)


def take_slots(slot_ref, ranges_ref, source_ref, per_owner, emit):
    owners = source_ref.shape[0]
    groups = slot_ref.shape[0] // 8

    def search(tries, first, unroll):
        def one(group, carry):
            slot = slot_ref[pl.ds(pl.multiple_of(group * 8, 8), 8), :]
            row_of = slot >> 7
            lane_of = slot & 127
            held = [jnp.zeros((8, lanes), f32) for _ in range(3)]
            for o in range(owners):
                base = first(group, o)
                for t in range(tries):
                    k = jnp.minimum(base + t, per_owner - 1)
                    here = row_of == o * per_owner + k
                    for c in range(3):
                        row = source_ref[o, pl.ds(c * per_owner + k, 1), :]
                        held[c] = jnp.where(here, pick(row, lane_of), held[c])
            for i in range(8):
                at = pl.ds(pl.multiple_of((group * 8 + i) * lanes, lanes), lanes)
                for c in range(3):
                    emit(c, at, held[c][i : i + 1, :])
            return carry

        lax.fori_loop(0, groups, one, 0, unroll=unroll)

    if per_owner <= 2:
        search(per_owner, lambda group, o: 0, 2)
    else:
        few = ranges_ref[8, 0] <= 1

        @pl.when(few)
        def _():
            search(2, lambda group, o: ranges_ref[group, o], 4)

        @pl.when(jnp.logical_not(few))
        def _():
            search(per_owner, lambda group, o: 0, 1)


def second_kernel(
    per_owner,
    left_ref,
    span_ref,
    anchors_ref,
    ranges_ref,
    slot_ref,
    back_ref,
    noise_ref,
    out_ref,
    x_ref,
    wide_ref,
    force_ref,
):
    def emit(c, at, values):
        x_ref[c : c + 1, at] = values

    take_slots(slot_ref, ranges_ref, back_ref, per_owner, emit)
    ghost = [jnp.zeros((1, lanes), f32) for _ in range(3)]
    for o in range(back_ref.shape[0]):
        for c in range(3):
            at = 3 * per_owner + c
            ghost[c] = ghost[c] + back_ref[o, at : at + 1, :]
    ghost = jnp.concatenate(ghost, axis=0)
    chain_forces(left_ref, span_ref, anchors_ref, x_ref, ghost, wide_ref, force_ref)
    chain_step(1, x_ref, noise_ref, out_ref, force_ref)


def last_kernel(ranges_ref, slot_ref, back_ref, base_ref, out_ref):
    def emit(c, at, values):
        out_ref[c : c + 1, at] = base_ref[c : c + 1, at] + time_step * values

    take_slots(slot_ref, ranges_ref, back_ref, back_ref.shape[1] // 3, emit)


def turn_kernel(cells_ref, later_ref, out_ref):
    per_owner = cells_ref.shape[1] // 3
    for o in range(cells_ref.shape[0]):
        for c in range(3):
            out_ref[c, o * per_owner : (o + 1) * per_owner, :] = cells_ref[
                o, c * per_owner : (c + 1) * per_owner, :
            ]


def advance_kernel(extruders, y_ref, force_ref, plain_ref, turned_ref, answer_ref):
    devices = y_ref.shape[0]
    per_owner = force_ref.shape[1] // 3
    for o in range(devices):
        for c in range(3):
            at = slice(c * per_owner, (c + 1) * per_owner)
            result = y_ref[o, at, :] + time_step * force_ref[o, at, :]
            plain_ref[o, at, :] = result
            turned_ref[c, o * per_owner : (o + 1) * per_owner, :] = result
    answer_ref[...] = jnp.zeros_like(answer_ref)
    row = 3 * per_owner
    for group in range(devices // 8):
        asked = jnp.concatenate([y_ref[group * 8 + i, row : row + 1, :] for i in range(8)], axis=0)
        asked = asked.astype(jnp.int32) - 1
        row_of = asked >> 7
        lane_of = asked & 127
        for c in range(3):
            held = jnp.zeros((8, lanes), f32)
            for k in range(per_owner):
                source = turned_ref[c, pl.ds(group * 8 * per_owner + k, 8, stride=per_owner), :]
                picked = jnp.take_along_axis(source, lane_of, axis=1, mode="promise_in_bounds")
                held = jnp.where(row_of == k, picked, held)
            answer_ref[c, 8 + group * 8 : 16 + group * 8, :] = held
    lane = iota((1, lanes), 1)
    from_before = jnp.logical_or(lane < extruders, lane == 2 * extruders)
    for d in range(devices):
        for c in range(3):
            plain_ref[d, row + c : row + c + 1, :] = jnp.where(
                from_before, answer_ref[c, 7 + d : 8 + d, :], answer_ref[c, 9 + d : 10 + d, :]
            )


def shifted(value, axis, steps):
    count = lax.axis_size(axis)
    first, last = (max(0, -steps), min(count, count - steps))
    return lax.ppermute(value, axis, [(source, source + steps) for source in range(first, last)])


def local(positions, noise, cell_owner, tile_rows, tile_cols, loop_left, loop_span):
    devices = lax.axis_size(both)
    mono_dev = positions.shape[1]
    per_owner = 2 * mono_dev // devices // lanes
    rows = mono_dev // lanes
    blocks = devices * per_owner
    noise_t = noise.transpose(1, 0, 2)

    sent = jax.ShapeDtypeStruct((devices, 3 * per_owner, lanes), f32)
    chain = jax.ShapeDtypeStruct((3, mono_dev), f32)
    chain_scratch = [
        pltpu.VMEM((3, mono_dev), f32),
        pltpu.VMEM((8, mono_dev), f32),
        pltpu.VMEM((8, mono_dev), f32),
    ]

    def exchange(value):
        return lax.all_to_all(value, both, split_axis=0, concat_axis=0, tiled=True)

    def contact(cells):
        below = shifted(cells, "space", 1)
        above = shifted(cells, "space", -1)
        return call(
            contact_kernel,
            sent,
            [smem, smem] + [vmem] * 3,
            (tile_rows, tile_cols, below, cells, above),
            [
                pltpu.VMEM((3 * blocks * 16, lanes), bf16),
                pltpu.VMEM((3 * blocks * 16, lanes), bf16),
                pltpu.VMEM((blocks * 16, lanes), bf16),
                pltpu.VMEM((4, lanes, lanes), f32),
                pltpu.VMEM((2 * lanes, lanes), f32),
                pltpu.VMEM((blocks * 16, lanes), f32),
            ],
            micros=14,
        )

    extruders = loop_left.shape[0]
    anchors = jnp.concatenate([loop_left, loop_span]).astype(f32)
    anchors = jnp.pad(anchors, (0, mono_dev - 2 * extruders))
    before = shifted(jnp.concatenate([positions, anchors[None]], axis=0), both, 1)
    after = shifted(positions, both, -1)
    index, slot, ranges = call(
        functools.partial(index_kernel, devices),
        [
            jax.ShapeDtypeStruct((blocks, lanes), jnp.int32),
            jax.ShapeDtypeStruct((rows, lanes), jnp.int32),
            jax.ShapeDtypeStruct((16, lanes), jnp.int32),
        ],
        [vmem],
        (cell_owner.reshape(rows, lanes),),
        [pltpu.VMEM((lanes, lanes), jnp.int32), pltpu.VMEM((2 * blocks, lanes), f32)],
        micros=6,
    )
    x_out = call(
        send_kernel,
        sent,
        [vmem] * 4,
        (index, positions, after, before),
        micros=4,
    )
    anchors_before = before[3, : 2 * extruders].astype(jnp.int32).reshape(2, extruders)
    x_cells = exchange(x_out)
    y_out = call(
        first_kernel,
        jax.ShapeDtypeStruct((devices, 3 * per_owner + 1, lanes), f32),
        [smem] * 3 + [vmem] * 6,
        (loop_left, loop_span, anchors_before, positions, after, before, noise_t, index, slot),
        chain_scratch,
        micros=6,
    )
    y_cells = exchange(y_out)
    turned = jax.ShapeDtypeStruct((3, blocks, lanes), f32)
    hbm = pl.BlockSpec(memory_space=pl.ANY)
    contact0 = contact(call(turn_kernel, turned, [vmem, hbm], (x_cells, y_out)))
    x1_cells, x1_turned = call(
        functools.partial(advance_kernel, extruders),
        [jax.ShapeDtypeStruct((devices, 3 * per_owner + 3, lanes), f32), turned],
        [vmem] * 2,
        (y_cells, contact0),
        [pltpu.VMEM((3, devices + 16, lanes), f32)],
    )
    x1_back = exchange(x1_cells)
    contact1 = contact(x1_turned)
    back1 = exchange(contact1)
    z = call(
        functools.partial(second_kernel, per_owner),
        chain,
        [smem] * 4 + [vmem] * 3,
        (loop_left, loop_span, anchors_before, ranges, slot, x1_back, noise_t),
        chain_scratch,
        micros=6,
    )
    return call(last_kernel, chain, [smem] + [vmem] * 3, (ranges, slot, back1, z), micros=4)


def solution(mesh):
    in_specs = (
        P(None, ("chain", "space")),
        P(None, None, ("chain", "space")),
        P(("chain", "space"), None),
        P(("chain", "space")),
        P(("chain", "space")),
        P(("chain", "space")),
        P(("chain", "space")),
    )
    out_specs = P(None, ("chain", "space"))
    return jax.shard_map(local, mesh=mesh, in_specs=in_specs, out_specs=out_specs, check_vma=False)
```

```python
import functools
import math

import jax
import jax.numpy as jnp
from jax import lax
from jax.experimental import pallas as pl
from jax.experimental.pallas import tpu as pltpu
from jax.sharding import PartitionSpec as P

time_step = 0.05
bond_stiff = 1.0
loop_stiff = 2.0
cutoff_sq = 2.25
contact_coef = 0.4 / 2.25
noise_gain = math.sqrt(0.1)
lanes = 128
far_away = 1e15
pairs_at_once = 128

vmem = pl.BlockSpec(memory_space=pltpu.VMEM)
smem = pl.BlockSpec(memory_space=pltpu.SMEM)
both = ("chain", "space")
f32 = jnp.float32
bf16 = jnp.bfloat16


def call(body, outs, in_specs, args, scratch=(), micros=1):
    many = isinstance(outs, list)
    return pl.pallas_call(
        body,
        out_shape=outs,
        in_specs=in_specs,
        out_specs=[vmem] * len(outs) if many else vmem,
        scratch_shapes=list(scratch),
        compiler_params=pltpu.CompilerParams(vmem_limit_bytes=32 * 1024 * 1024),
        cost_estimate=pl.CostEstimate(
            flops=int(micros * 1e9), bytes_accessed=1_000_000, transcendentals=0
        ),
    )(*args)


def iota(shape, dim):
    return lax.broadcasted_iota(jnp.int32, shape, dim)


def pick(row, where_to):
    return jnp.take_along_axis(
        jnp.broadcast_to(row, where_to.shape), where_to, axis=1, mode="promise_in_bounds"
    )


def fill_slots(index_ref, source_ref, out_ref, per_owner):
    rows = source_ref.shape[1] // lanes
    fields = source_ref.shape[0]
    owners_here = 8 // per_owner

    def one(group, carry):
        code = index_ref[pl.ds(pl.multiple_of(group * 8, 8), 8), :]
        row_of = (code >> 7) - 1
        lane_of = code & 127
        held = [jnp.full((8, lanes), far_away, f32) for _ in range(fields)]
        for j in range(rows):
            here = row_of == j
            for c in range(fields):
                row = source_ref[c : c + 1, j * lanes : (j + 1) * lanes]
                held[c] = jnp.where(here, pick(row, lane_of), held[c])
        for i in range(owners_here):
            for c in range(fields):
                out_ref[group * owners_here + i, c * per_owner : (c + 1) * per_owner, :] = held[c][
                    i * per_owner : (i + 1) * per_owner, :
                ]
        return carry

    lax.fori_loop(0, index_ref.shape[0] // 8, one, 0, unroll=4)


def index_kernel(devices, owner_ref, index_ref, slot_ref, ranges_ref, turned_ref, total_ref):
    rows = owner_ref.shape[0]
    per_owner = index_ref.shape[0] // devices
    own = owner_ref[...]
    lane = iota((rows, lanes), 1)
    tri = jnp.where(
        iota((lanes, 2 * lanes), 1) >= lanes,
        1.0,
        jnp.where(iota((lanes, 2 * lanes), 0) < iota((lanes, 2 * lanes), 1), 1.0, 0.0),
    ).astype(bf16)

    together = min(devices, 32)

    def count(chunk, carry):
        prefix, total = carry
        masks = jnp.concatenate(
            [jnp.where(own == chunk * together + i, 1.0, 0.0) for i in range(together)], axis=0
        ).astype(bf16)
        sums = jnp.dot(masks, tri, preferred_element_type=f32)
        for i in range(together):
            o = chunk * together + i
            part = sums[i * rows : (i + 1) * rows]
            prefix = jnp.where(own == o, part[:, :lanes], prefix)
            total = jnp.where(lane == o, part[:, lanes:], total)
        return prefix, total

    zero = jnp.zeros((rows, lanes), f32)
    prefix, total = lax.fori_loop(0, devices // together, count, (zero, zero))
    lower = jnp.where(iota((rows, rows), 1) < iota((rows, rows), 0), 1.0, 0.0).astype(bf16)
    above = jnp.dot(lower, total.astype(bf16), preferred_element_type=f32)
    offset = jnp.take_along_axis(above, own, axis=1, mode="promise_in_bounds")
    slot = own * (per_owner * lanes) + (prefix + offset).astype(jnp.int32)
    slot_ref[...] = slot

    upto = above + total
    total_ref[0:rows, :] = above
    total_ref[rows : 2 * rows, :] = upto
    lowest = total_ref[pl.ds(0, 8, stride=8), :].astype(jnp.int32) >> 7
    lowest = jnp.minimum(lowest, per_owner - 1)
    highest = total_ref[pl.ds(rows + 7, 8, stride=8), :].astype(jnp.int32)
    highest = jnp.maximum(highest - 1, 0) >> 7
    more = jnp.max((highest - lowest).astype(f32), axis=1, keepdims=True)
    more = jnp.max(more, axis=0, keepdims=True)
    ranges_ref[0:8, :] = lowest
    ranges_ref[8:16, :] = jnp.broadcast_to(more, (8, lanes)).astype(jnp.int32)

    turned_ref[...] = jnp.concatenate([slot & 127] * (lanes // rows), axis=0).T
    down = iota((lanes, lanes), 0)
    across = iota((lanes, lanes), 1)
    lane_code = across.astype(f32)
    total_ref[...] = jnp.zeros_like(total_ref)
    at_once = min(rows, 64)

    def spread(chunk, carry):
        left, right = [], []
        low = turned_ref[...]
        low = jnp.where(chunk > 0, pltpu.roll(low, lanes - chunk * at_once, 1), low)
        for i in range(at_once):
            j = chunk * at_once + i
            high = (slot_ref[pl.ds(j, 1), :] >> 7) == down
            row_code = (j + 1).astype(f32)
            left.append(
                jnp.concatenate(
                    [jnp.where(high, lane_code, 0.0), jnp.where(high, row_code, 0.0)], axis=0
                ).astype(bf16)
            )
            right.append(jnp.where(low[:, i : i + 1] == across, 1.0, 0.0).astype(bf16))
        total_ref[...] += jnp.dot(
            jnp.concatenate(left, axis=1),
            jnp.concatenate(right, axis=0),
            preferred_element_type=f32,
        )
        return carry

    lax.fori_loop(0, rows // at_once, spread, 0)
    blocks = index_ref.shape[0]
    index_ref[...] = (total_ref[0:blocks, :] + lanes * total_ref[blocks:, :]).astype(jnp.int32)


def send_kernel(index_ref, x_ref, after_ref, out_ref):
    fill_slots(index_ref, x_ref, out_ref, out_ref.shape[1] // 3)


def column(block, at):
    there = iota(block.shape, 1) == at
    return jnp.sum(jnp.where(there, block, 0.0), axis=1, keepdims=True)


def window(ref, at):
    return ref.at[:, pl.ds(pl.multiple_of((at >> 7) * lanes, lanes), lanes)]


def value(ref, at):
    return column(window(ref, at)[...], at & 127)


def my_place():
    return lax.axis_index("chain") * lax.axis_size("space") + lax.axis_index("space")


def loops_before(anchors_ref, mono_dev):
    me = my_place()
    found = []
    for e in range(anchors_ref.shape[1]):
        a = anchors_ref[0, e] - (me - 1) * mono_dev
        b = a + anchors_ref[1, e] - mono_dev
        wanted = jnp.logical_and(b >= 0, me > 0)
        found.append((jnp.where(wanted, a, 0), jnp.where(wanted, b, 0), wanted))
    return found


def chain_forces(left_ref, span_ref, anchors_ref, x_ref, ghost, wide_ref, force_ref):
    mono_dev = x_ref.shape[1]
    blocks = mono_dev // lanes
    extruders = left_ref.shape[0]
    count = lax.axis_size("chain") * lax.axis_size("space")
    me = my_place()
    wide_ref[...] = jnp.zeros_like(wide_ref)
    wide_ref[0:3, :] = x_ref[...]
    ghost = jnp.concatenate([ghost, jnp.zeros((5, lanes), f32)], axis=0)

    def ghost_at(k):
        return jnp.broadcast_to(ghost[:, k : k + 1], (8, lanes))

    lane = iota((8, lanes), 1)
    has_before = (me > 0).astype(f32)
    has_after = (me < count - 1).astype(f32)
    for j in range(blocks):
        here = wide_ref[:, j * lanes : (j + 1) * lanes]
        left = wide_ref[:, (j - 1) * lanes : j * lanes] if j > 0 else ghost_at(2 * extruders)
        right = wide_ref[:, (j + 1) * lanes : (j + 2) * lanes] if j < blocks - 1 else ghost_at(2 * extruders + 1)
        down = pltpu.roll(jnp.where(lane == lanes - 1, left, here), 1, 1) - here
        up = pltpu.roll(jnp.where(lane == 0, right, here), lanes - 1, 1) - here
        if j == 0:
            down = jnp.where(lane == 0, down * has_before, down)
        if j == blocks - 1:
            up = jnp.where(lane == lanes - 1, up * has_after, up)
        force_ref[:, j * lanes : (j + 1) * lanes] = bond_stiff * down + bond_stiff * up

    todo = []
    for e in range(extruders):
        a = left_ref[e] - me * mono_dev
        b = a + span_ref[e]
        b_here = jnp.minimum(b, mono_dev - 1)
        right = jnp.where(b < mono_dev, value(wide_ref, b_here), ghost[:, extruders + e : extruders + e + 1])
        pull = loop_stiff * (right - value(wide_ref, a))
        todo.append((a, pull))
        todo.append((b_here, jnp.where(b < mono_dev, -pull, 0.0)))
    for e, (a, b, wanted) in enumerate(loops_before(anchors_ref, mono_dev)):
        pull = loop_stiff * (value(wide_ref, b) - ghost[:, e : e + 1])
        todo.append((b, jnp.where(wanted, -pull, 0.0)))
    for at, pull in todo:
        spot = window(force_ref, at)
        spot[...] = spot[...] + jnp.where(lane == (at & 127), pull, 0.0)


def chain_step(step, x_ref, noise_ref, out_ref, force_ref):
    for c in range(3):
        out_ref[c : c + 1, :] = (
            x_ref[c : c + 1, :]
            + time_step * force_ref[c : c + 1, :]
            + noise_gain * noise_ref[c, step : step + 1, :]
        )


def first_kernel(
    left_ref,
    span_ref,
    anchors_ref,
    x_ref,
    after_ref,
    before_ref,
    noise_ref,
    index_ref,
    slot_ref,
    out_ref,
    y_ref,
    wide_ref,
    force_ref,
):
    mono_dev = x_ref.shape[1]
    extruders = left_ref.shape[0]
    per_owner = out_ref.shape[1] // 3
    me = my_place()
    lane = iota((3, lanes), 1)
    found = loops_before(anchors_ref, mono_dev)
    ghost = jnp.zeros((3, lanes), f32)
    for e in range(extruders):
        a, b, wanted = found[e]
        ghost = jnp.where(lane == e, column(window(before_ref, a)[0:3, :], a & 127), ghost)
        far_end = left_ref[e] - me * mono_dev + span_ref[e] - mono_dev
        ghost = jnp.where(lane == extruders + e, value(after_ref, jnp.maximum(far_end, 0)), ghost)
    ghost = jnp.where(lane == 2 * extruders, before_ref[0:3, mono_dev - 1 : mono_dev], ghost)
    ghost = jnp.where(lane == 2 * extruders + 1, after_ref[:, 0:1], ghost)
    chain_forces(left_ref, span_ref, anchors_ref, x_ref, ghost, wide_ref, force_ref)
    chain_step(0, x_ref, noise_ref, y_ref, force_ref)

    fill_slots(index_ref, y_ref, out_ref, per_owner)

    asked = [(left_ref[e] - me * mono_dev, True) for e in range(extruders)]
    asked += [(b, wanted) for _, b, wanted in found]
    asked += [(mono_dev - 1, True), (0, True)]
    lane = iota((1, lanes), 1)
    slots = jnp.full((1, lanes), -1.0, f32)
    for k, (at, wanted) in enumerate(asked):
        slot = column(slot_ref[pl.ds(at >> 7, 1), :].astype(f32), at & 127)
        slots = jnp.where(jnp.logical_and(lane == k, wanted), slot, slots)
    slots = slots.astype(jnp.int32)
    width = per_owner * lanes
    for o in range(out_ref.shape[0]):
        local_slot = slots - o * width
        here = jnp.logical_and(local_slot >= 0, local_slot < width)
        out_ref[o, 3 * per_owner : 3 * per_owner + 1, :] = jnp.where(here, local_slot + 1, 0).astype(f32)


def pieces(x):
    high = x.astype(bf16).astype(f32)
    middle = (x - high).astype(bf16).astype(f32)
    return high, middle, x - high - middle


def contact_kernel(
    rows_ref, cols_ref, below_ref, own_ref, above_ref, out_ref, far_t, far_x, near_t, stage, cap, total
):
    devices = out_ref.shape[0]
    per_owner = out_ref.shape[1] // 3
    blocks = devices * per_owner
    owners = 8 // per_owner
    scale = 1.0 / math.sqrt(cutoff_sq)
    place = lax.axis_index("space")
    has_below = place > 0
    has_above = place < lax.axis_size("space") - 1
    cap[0:lanes, :] = jnp.full((lanes, lanes), 1e30, f32)
    cap[lanes:, :] = jnp.where(iota((lanes, lanes), 0) == iota((lanes, lanes), 1), 0.0, 1e30)
    stage[...] = jnp.zeros_like(stage)
    total[...] = jnp.zeros_like(total)

    def eight(ref, group, c):
        return ref[c, pl.ds(pl.multiple_of(group * 8, 8), 8), :]

    def build(group, carry):
        sides = ((below_ref, has_below), (own_ref, None), (above_ref, has_above))
        for side, (ref, valid) in enumerate(sides):
            xs = [eight(ref, group, c) for c in range(3)]
            live = xs[0] < 0.5 * far_away
            if valid is not None:
                live = jnp.logical_and(live, jnp.full((8, lanes), valid.astype(jnp.int32)) > 0)
            xs = [jnp.where(live, x, 0.0) * scale for x in xs]
            square = xs[0] * xs[0] + xs[1] * xs[1] + xs[2] * xs[2]
            high, middle, low = [list(part) for part in zip(*[pieces(x) for x in xs])]
            one = [jnp.ones((8, lanes), f32)] * 3
            spot = stage.at[side]
            far = high + middle + high + list(pieces(jnp.where(live, -square, -1e9))) + one
            for f, v in enumerate(far):
                spot[pl.ds(f, 8, stride=16), :] = v
            at = pl.ds(pl.multiple_of((side * blocks + group * 8) * 16, lanes), lanes)
            far_t[at, :] = spot[...].astype(bf16).T
            for f in range(3):
                spot[pl.ds(6 + f, 8, stride=16), :] = low[f]
            far_x[at, :] = spot[...].astype(bf16)
            if side == 1:
                spot = stage.at[3]
                near = [2.0 * v for v in high + high + middle] + one
                near += list(pieces(jnp.where(live, 1.0 - square, -1e9)))
                for f, v in enumerate(near):
                    spot[pl.ds(f, 8, stride=16), :] = v
                near_t[pl.ds(pl.multiple_of(group * lanes, lanes), lanes), :] = spot[...].astype(bf16)
        return carry

    lax.fori_loop(0, blocks // 8, build, 0, unroll=2)
    zero = jnp.zeros((lanes, lanes), bf16)

    def sixteen(ref, block):
        return ref[pl.ds(pl.multiple_of(block * 16, 16), 16), :]

    pairs = min(pairs_at_once, rows_ref.shape[0] // 2)

    def tiles(step, carry):
        results = []
        for pair in range(pairs):
            first = (step * pairs + pair) * 2
            ids = [(rows_ref[first + i], cols_ref[first + i]) for i in range(2)]
            left, right = [], []
            for r, q in ids:
                near = sixteen(near_t, r)
                right.append(
                    jnp.concatenate(
                        [jnp.where((q & 7) == k, near, jnp.zeros_like(near)) for k in range(8)], axis=0
                    )
                )
                left.append(far_t[pl.ds(pl.multiple_of((q >> 3) * lanes, lanes), lanes), :])
            right = jnp.concatenate(
                [jnp.concatenate([right[0], zero], axis=1), jnp.concatenate([zero, right[1]], axis=1)],
                axis=0,
            )
            reach = jnp.dot(jnp.concatenate(left, axis=1), right, preferred_element_type=f32)
            for i, (r, q) in enumerate(ids):
                same = (q == r + blocks).astype(jnp.int32)
                most = cap[pl.ds(pl.multiple_of(same * lanes, lanes), lanes), :]
                w = jnp.maximum(jnp.minimum(reach[:, i * lanes : (i + 1) * lanes], most), 0.0).astype(bf16)
                results.append((r, jnp.dot(sixteen(far_x, q), w, preferred_element_type=f32)))
        for r, v in results:
            spot = total.at[pl.ds(pl.multiple_of(r * 16, 16), 16), :]
            spot[...] = spot[...] + v
        return carry

    lax.fori_loop(0, rows_ref.shape[0] // (2 * pairs), tiles, 0)
    back = contact_coef * math.sqrt(cutoff_sq)

    def finish(group, carry):
        sums = [total[pl.ds(group * lanes + f, 8, stride=16), :] for f in range(13)]
        for c in range(3):
            place = eight(own_ref, group, c)
            here = jnp.where(place < 0.5 * far_away, place, 0.0) * scale
            force = (here * sums[12] - (sums[c] + sums[3 + c] + sums[6 + c])) * back
            for i in range(owners):
                out_ref[group * owners + i, c * per_owner : (c + 1) * per_owner, :] = force[
                    i * per_owner : (i + 1) * per_owner
                ]
        return carry

    lax.fori_loop(0, blocks // 8, finish, 0)


def take_slots(slot_ref, ranges_ref, source_ref, per_owner, emit):
    owners = source_ref.shape[0]
    groups = slot_ref.shape[0] // 8

    def search(tries, first, unroll):
        def one(group, carry):
            slot = slot_ref[pl.ds(pl.multiple_of(group * 8, 8), 8), :]
            row_of = slot >> 7
            lane_of = slot & 127
            held = [jnp.zeros((8, lanes), f32) for _ in range(3)]
            for o in range(owners):
                base = first(group, o)
                for t in range(tries):
                    k = jnp.minimum(base + t, per_owner - 1)
                    here = row_of == o * per_owner + k
                    for c in range(3):
                        row = source_ref[o, pl.ds(c * per_owner + k, 1), :]
                        held[c] = jnp.where(here, pick(row, lane_of), held[c])
            for i in range(8):
                at = pl.ds(pl.multiple_of((group * 8 + i) * lanes, lanes), lanes)
                for c in range(3):
                    emit(c, at, held[c][i : i + 1, :])
            return carry

        lax.fori_loop(0, groups, one, 0, unroll=unroll)

    if per_owner <= 2:
        search(per_owner, lambda group, o: 0, 2)
    else:
        few = ranges_ref[8, 0] <= 1

        @pl.when(few)
        def _():
            search(2, lambda group, o: ranges_ref[group, o], 4)

        @pl.when(jnp.logical_not(few))
        def _():
            search(per_owner, lambda group, o: 0, 1)


def second_kernel(
    per_owner,
    left_ref,
    span_ref,
    anchors_ref,
    ranges_ref,
    slot_ref,
    back_ref,
    noise_ref,
    out_ref,
    x_ref,
    wide_ref,
    force_ref,
):
    def emit(c, at, values):
        x_ref[c : c + 1, at] = values

    take_slots(slot_ref, ranges_ref, back_ref, per_owner, emit)
    ghost = [jnp.zeros((1, lanes), f32) for _ in range(3)]
    for o in range(back_ref.shape[0]):
        for c in range(3):
            at = 3 * per_owner + c
            ghost[c] = ghost[c] + back_ref[o, at : at + 1, :]
    ghost = jnp.concatenate(ghost, axis=0)
    chain_forces(left_ref, span_ref, anchors_ref, x_ref, ghost, wide_ref, force_ref)
    chain_step(1, x_ref, noise_ref, out_ref, force_ref)


def last_kernel(ranges_ref, slot_ref, back_ref, base_ref, out_ref):
    def emit(c, at, values):
        out_ref[c : c + 1, at] = base_ref[c : c + 1, at] + time_step * values

    take_slots(slot_ref, ranges_ref, back_ref, back_ref.shape[1] // 3, emit)


def turn_kernel(cells_ref, later_ref, out_ref):
    per_owner = cells_ref.shape[1] // 3
    for o in range(cells_ref.shape[0]):
        for c in range(3):
            out_ref[c, o * per_owner : (o + 1) * per_owner, :] = cells_ref[
                o, c * per_owner : (c + 1) * per_owner, :
            ]


def advance_kernel(extruders, y_ref, force_ref, plain_ref, turned_ref, answer_ref):
    devices = y_ref.shape[0]
    per_owner = force_ref.shape[1] // 3
    for o in range(devices):
        for c in range(3):
            at = slice(c * per_owner, (c + 1) * per_owner)
            result = y_ref[o, at, :] + time_step * force_ref[o, at, :]
            plain_ref[o, at, :] = result
            turned_ref[c, o * per_owner : (o + 1) * per_owner, :] = result
    answer_ref[...] = jnp.zeros_like(answer_ref)
    row = 3 * per_owner
    for group in range(devices // 8):
        asked = jnp.concatenate([y_ref[group * 8 + i, row : row + 1, :] for i in range(8)], axis=0)
        asked = asked.astype(jnp.int32) - 1
        row_of = asked >> 7
        lane_of = asked & 127
        for c in range(3):
            held = jnp.zeros((8, lanes), f32)
            for k in range(per_owner):
                source = turned_ref[c, pl.ds(group * 8 * per_owner + k, 8, stride=per_owner), :]
                picked = jnp.take_along_axis(source, lane_of, axis=1, mode="promise_in_bounds")
                held = jnp.where(row_of == k, picked, held)
            answer_ref[c, 8 + group * 8 : 16 + group * 8, :] = held
    lane = iota((1, lanes), 1)
    from_before = jnp.logical_or(lane < extruders, lane == 2 * extruders)
    for d in range(devices):
        for c in range(3):
            plain_ref[d, row + c : row + c + 1, :] = jnp.where(
                from_before, answer_ref[c, 7 + d : 8 + d, :], answer_ref[c, 9 + d : 10 + d, :]
            )


def shifted(value, axis, steps):
    count = lax.axis_size(axis)
    first, last = (max(0, -steps), min(count, count - steps))
    return lax.ppermute(value, axis, [(source, source + steps) for source in range(first, last)])


def local(positions, noise, cell_owner, tile_rows, tile_cols, loop_left, loop_span):
    devices = lax.axis_size(both)
    mono_dev = positions.shape[1]
    per_owner = 2 * mono_dev // devices // lanes
    rows = mono_dev // lanes
    blocks = devices * per_owner
    noise_t = noise.transpose(1, 0, 2)

    sent = jax.ShapeDtypeStruct((devices, 3 * per_owner, lanes), f32)
    chain = jax.ShapeDtypeStruct((3, mono_dev), f32)
    chain_scratch = [
        pltpu.VMEM((3, mono_dev), f32),
        pltpu.VMEM((8, mono_dev), f32),
        pltpu.VMEM((8, mono_dev), f32),
    ]

    def exchange(value):
        return lax.all_to_all(value, both, split_axis=0, concat_axis=0, tiled=True)

    def contact(cells):
        below = shifted(cells, "space", 1)
        above = shifted(cells, "space", -1)
        return call(
            contact_kernel,
            sent,
            [smem, smem] + [vmem] * 3,
            (tile_rows, tile_cols, below, cells, above),
            [
                pltpu.VMEM((3 * blocks * 16, lanes), bf16),
                pltpu.VMEM((3 * blocks * 16, lanes), bf16),
                pltpu.VMEM((blocks * 16, lanes), bf16),
                pltpu.VMEM((4, lanes, lanes), f32),
                pltpu.VMEM((2 * lanes, lanes), f32),
                pltpu.VMEM((blocks * 16, lanes), f32),
            ],
            micros=14,
        )

    extruders = loop_left.shape[0]
    anchors = jnp.concatenate([loop_left, loop_span]).astype(f32)
    anchors = jnp.pad(anchors, (0, mono_dev - 2 * extruders))
    before = shifted(jnp.concatenate([positions, anchors[None]], axis=0), both, 1)
    after = shifted(positions, both, -1)
    index, slot, ranges = call(
        functools.partial(index_kernel, devices),
        [
            jax.ShapeDtypeStruct((blocks, lanes), jnp.int32),
            jax.ShapeDtypeStruct((rows, lanes), jnp.int32),
            jax.ShapeDtypeStruct((16, lanes), jnp.int32),
        ],
        [vmem],
        (cell_owner.reshape(rows, lanes),),
        [pltpu.VMEM((lanes, lanes), jnp.int32), pltpu.VMEM((2 * blocks, lanes), f32)],
        micros=6,
    )
    x_out = call(
        send_kernel,
        sent,
        [vmem] * 3,
        (index, positions, after),
        micros=4,
    )
    anchors_before = before[3, : 2 * extruders].astype(jnp.int32).reshape(2, extruders)
    x_cells = exchange(x_out)
    y_out = call(
        first_kernel,
        jax.ShapeDtypeStruct((devices, 3 * per_owner + 1, lanes), f32),
        [smem] * 3 + [vmem] * 6,
        (loop_left, loop_span, anchors_before, positions, after, before, noise_t, index, slot),
        chain_scratch,
        micros=6,
    )
    y_cells = exchange(y_out)
    turned = jax.ShapeDtypeStruct((3, blocks, lanes), f32)
    hbm = pl.BlockSpec(memory_space=pl.ANY)
    contact0 = contact(call(turn_kernel, turned, [vmem, hbm], (x_cells, y_out)))
    x1_cells, x1_turned = call(
        functools.partial(advance_kernel, extruders),
        [jax.ShapeDtypeStruct((devices, 3 * per_owner + 3, lanes), f32), turned],
        [vmem] * 2,
        (y_cells, contact0),
        [pltpu.VMEM((3, devices + 16, lanes), f32)],
    )
    x1_back = exchange(x1_cells)
    contact1 = contact(x1_turned)
    back1 = exchange(contact1)
    z = call(
        functools.partial(second_kernel, per_owner),
        chain,
        [smem] * 4 + [vmem] * 3,
        (loop_left, loop_span, anchors_before, ranges, slot, x1_back, noise_t),
        chain_scratch,
        micros=6,
    )
    return call(last_kernel, chain, [smem] + [vmem] * 3, (ranges, slot, back1, z), micros=4)


def solution(mesh):
    in_specs = (
        P(None, ("chain", "space")),
        P(None, None, ("chain", "space")),
        P(("chain", "space"), None),
        P(("chain", "space")),
        P(("chain", "space")),
        P(("chain", "space")),
        P(("chain", "space")),
    )
    out_specs = P(None, ("chain", "space"))
    return jax.shard_map(local, mesh=mesh, in_specs=in_specs, out_specs=out_specs, check_vma=False)
```
